256 devices in a mesh: seq: 128 (over x, y, z), head: 2 (over core).
Axes of the slice: x: 4, y: 4, z: 8, core: 2. Of those that a mesh axis runs over, the one named last changes fastest.
Arguments:
- queries: bfloat16 [16384, 4096], P('seq', 'head'), may hold values from -45 to 45
- key_states: bfloat16 [16384, 4096], P('seq', 'head'), may hold values from -6 to 6
- values: bfloat16 [16384, 4096], P('seq', 'head'), may hold values from -6 to 6
- out_grad: bfloat16 [16384, 4096], P('seq', 'head'), may hold values from -6 to 6
- rand_blocks: int32 [256, 32, 3], P(None, 'head'), may hold values from 0 to 255, as said below
Outputs:
- attended: bfloat16 [16384, 4096], P('seq', 'head')
- query_grad: bfloat16 [16384, 4096], P('seq', 'head')
- key_grad: bfloat16 [16384, 4096], P('seq', 'head')
- value_grad: bfloat16 [16384, 4096], P('seq', 'head')
The draws below stay inside these ranges and needn't reach their ends.
Inputs may be any that keep to these rules, and one draw needn't show every extreme that they name: `rand_blocks`: for every query block i and head the three entries are different blocks; none lies on the seq shard (of 2 blocks) of block 0 or of block 255, nor on the shard of block i. Over the query blocks of one seq shard and the heads of one head shard, the blocks of any one seq shard are named at most 1 times, and some shard's blocks exactly 1 times.
All inputs are finite; a program needn't handle non-finite values.
Results may differ from the reference program's by a relative error of at most 0.028.
Values may be sent and summed in bfloat16 or wider, within the bound.
No kernel may reach another device: no remote copies, remote signals or barrier semaphores. Data moves between devices by JAX's collectives and lax.ppermute only.
A program may use at most 128 MiB of HBM per device.

```python
import math
import jax
import jax.numpy as jnp
from jax import lax

HEADS = 32
DH = 128
BLOCK = 64
BLK_DEV = 2
TOKENS = 16384
NB = 256
HEADS_DEV = 16
N_SEQ = 128
N_HEAD = 2


def shared_fields(key):
    shape = (TOKENS, HEADS * DH)
    keys_field = jnp.clip(jax.random.normal(jax.random.fold_in(key, 11), shape, jnp.float32), -6.0, 6.0)
    query_field = jnp.clip(jax.random.normal(jax.random.fold_in(key, 12), shape, jnp.float32), -6.0, 6.0)
    return (query_field, keys_field)


def draw_queries(key, part):
    return shared_fields(key)[0].astype(jnp.bfloat16)


def draw_key_states(key, part):
    return shared_fields(key)[1].astype(jnp.bfloat16)


def owner_plan(key, shard):
    peer_ids = jnp.arange(N_SEQ, dtype=jnp.int32)
    banned = (peer_ids == 0) | (peer_ids == N_SEQ - 1) | (peer_ids == shard)
    favoured = (peer_ids == (shard + N_SEQ - 1) % N_SEQ) | (peer_ids == (shard + 1) % N_SEQ) | (peer_ids == (shard + N_SEQ // 2) % N_SEQ)
    order_rank = jax.random.permutation(jax.random.fold_in(key, 1), N_SEQ).astype(jnp.int32)
    order_key = banned.astype(jnp.int32) * (4 * N_SEQ) + (1 - favoured.astype(jnp.int32)) * (2 * N_SEQ) + order_rank
    order = jnp.argsort(order_key).astype(jnp.int32)
    avail = N_SEQ - jnp.sum(banned.astype(jnp.int32))
    request_count = 3 * BLK_DEV * HEADS_DEV
    slot_ids = jnp.arange(request_count, dtype=jnp.int32)
    owner = order[slot_ids % avail]
    local_block = jax.random.randint(jax.random.fold_in(key, 2), (request_count,), 0, BLK_DEV).astype(jnp.int32)
    return (owner * BLK_DEV + local_block).reshape(BLK_DEV, HEADS_DEV, 3)


def plan_for_shard(key, shard):
    group_ids = jnp.arange(N_HEAD, dtype=jnp.int32)

    def for_group(group):
        return owner_plan(jax.random.fold_in(jax.random.fold_in(key, shard), group + 1000), shard)
    return jax.vmap(for_group)(group_ids)


def draw_rand_blocks(key, part):
    shard_ids = jnp.arange(N_SEQ, dtype=jnp.int32)
    table = jax.vmap(lambda shard: plan_for_shard(key, shard))(shard_ids)
    return jnp.transpose(table, (0, 2, 1, 3, 4)).reshape(NB, HEADS, 3).astype(jnp.int32)


def block_scale(rng, extent, cuts, least, largest):
    def one(dim, parts):
        steps = jax.random.uniform(jax.random.fold_in(jax.random.fold_in(rng, 6), dim), (parts,), jnp.float32, least / len(cuts), largest / len(cuts))
        return jnp.repeat(jnp.exp(steps), extent[dim] // parts).reshape((-1,) + (1,) * (len(extent) - dim - 1))

    gain = one(*cuts[0])
    for cut in cuts[1:]:
        gain = gain * one(*cut)
    return gain


def normal_values(rng, shape, width, reach, split=(), kind=jnp.bfloat16):
    factor_of = block_scale(rng, shape, split, -0.22, 0.18) if split else 1.0
    array = jax.random.normal(rng, shape, jnp.float32) * width * factor_of
    return jnp.minimum(jnp.maximum(array, -reach), reach).astype(kind)


def setup_inputs(seed: int = 0) -> dict:
    splits = jax.random.split(jax.random.key(seed), 6)
    return {
        "queries": draw_queries(jax.random.fold_in(splits[5], 71), 0),
        "key_states": draw_key_states(jax.random.fold_in(splits[5], 71), 0),
        "values": normal_values(splits[2], (TOKENS, HEADS * DH), 1.0, 6.0, ((0, 128), (1, 2))),
        "out_grad": normal_values(splits[3], (TOKENS, HEADS * DH), 1.0, 6.0, ((0, 128), (1, 2))),
        "rand_blocks": draw_rand_blocks(jax.random.fold_in(splits[5], 71), 0),
    }


def head_major(flat_rows):
    block_total = flat_rows.shape[0] // BLOCK
    return flat_rows.reshape(block_total, BLOCK, HEADS, DH).transpose(2, 0, 1, 3)

def token_major(arranged):
    return arranged.transpose(1, 2, 0, 3).reshape(TOKENS, HEADS * DH)

def reference(queries, key_states, values, out_grad, rand_blocks):
    block_total = TOKENS // BLOCK
    score_scale = 1.0 / math.sqrt(DH)
    highest = lax.Precision.HIGHEST
    block_ids = jnp.arange(block_total, dtype=jnp.int32)
    window_ids = jnp.stack([block_ids - 1, block_ids, block_ids + 1], axis=1)
    window_ok = (window_ids >= 0) & (window_ids < block_total)
    window_ids = jnp.clip(window_ids, 0, block_total - 1).astype(jnp.int32)
    global_ids = jnp.stack([jnp.zeros_like(block_ids), jnp.full_like(block_ids, block_total - 1)], axis=1)
    global_ok = jnp.stack([block_ids >= 2, block_ids <= block_total - 3], axis=1)
    random_ok = jnp.ones((block_total, 3), dtype=jnp.bool_)
    allowed = jnp.repeat(jnp.concatenate([window_ok, global_ok, random_ok], axis=1), BLOCK, axis=1)

    def one_head(inputs):
        query_h, key_h, value_h, grad_h, random_h = inputs
        chosen = jnp.concatenate([window_ids, global_ids, random_h.astype(jnp.int32)], axis=1).astype(jnp.int32)
        key_sel = key_h[chosen].reshape(block_total, 8 * BLOCK, DH).astype(jnp.float32)
        value_sel = value_h[chosen].reshape(block_total, 8 * BLOCK, DH).astype(jnp.float32)
        query_f = query_h.astype(jnp.float32)
        grad_f = grad_h.astype(jnp.float32)
        scores = jnp.einsum('nqd,nkd->nqk', query_f, key_sel, precision=highest) * score_scale
        scores = jnp.where(allowed[:, None, :], scores, -jnp.inf)
        row_max = lax.optimization_barrier(jnp.max(scores, axis=-1, keepdims=True))
        log_total = row_max + jnp.log(lax.optimization_barrier(jnp.sum(jnp.exp(scores - row_max), axis=-1, keepdims=True)))
        weights = jnp.exp(scores - log_total)
        weights_low = lax.optimization_barrier(weights.astype(jnp.bfloat16)).astype(jnp.float32)
        attended = jnp.einsum('nqk,nkd->nqd', weights_low, value_sel, precision=highest).astype(jnp.bfloat16)
        attended_f = lax.optimization_barrier(attended).astype(jnp.float32)
        row_dot = lax.optimization_barrier(jnp.sum(grad_f * attended_f, axis=-1, keepdims=True))
        weight_grads = jnp.einsum('nqd,nkd->nqk', grad_f, value_sel, precision=highest)
        score_grads = (weights * (weight_grads - row_dot) * score_scale).astype(jnp.bfloat16)
        score_grads = lax.optimization_barrier(score_grads).astype(jnp.float32)
        query_grad = jnp.einsum('nqk,nkd->nqd', score_grads, key_sel, precision=highest).astype(jnp.bfloat16)
        key_terms = jnp.einsum('nqk,nqd->nkd', score_grads, query_f, precision=highest).reshape(block_total, 8, BLOCK, DH)
        value_terms = jnp.einsum('nqk,nqd->nkd', weights_low, grad_f, precision=highest).reshape(block_total, 8, BLOCK, DH)
        key_random = lax.optimization_barrier(key_terms[:, 5:].astype(jnp.bfloat16)).astype(jnp.float32)
        value_random = lax.optimization_barrier(value_terms[:, 5:].astype(jnp.bfloat16)).astype(jnp.float32)
        key_terms = jnp.concatenate([key_terms[:, :5], key_random], axis=1)
        value_terms = jnp.concatenate([value_terms[:, :5], value_random], axis=1)
        key_grad = jnp.zeros((block_total, BLOCK, DH), jnp.float32).at[chosen].add(key_terms)
        value_grad = jnp.zeros((block_total, BLOCK, DH), jnp.float32).at[chosen].add(value_terms)
        return (attended, query_grad, key_grad.astype(jnp.bfloat16), value_grad.astype(jnp.bfloat16))
    stacked = (head_major(queries), head_major(key_states), head_major(values), head_major(out_grad), jnp.transpose(rand_blocks, (1, 0, 2)))
    results = lax.map(one_head, stacked)
    return (token_major(results[0]), token_major(results[1]), token_major(results[2]), token_major(results[3]))
```

```python
import math

import jax
import jax.numpy as jnp
from jax import lax
from jax.experimental import pallas as pl
from jax.experimental.pallas import tpu as pltpu
from jax.sharding import PartitionSpec as P

DH = 128
BLOCK = 64
HEADS = 16
SHARDS = 128
LAST = SHARDS - 1
PICKS = 3 * HEADS
NX, NY, NZ = 4, 4, 8
VMEM_BYTES = 48 * 2**20
MASKED = -1e30
SCALE = 1.0 / math.sqrt(DH)
EXP2_SCALE = SCALE * math.log2(math.e)
BF16 = jnp.bfloat16
F32 = jnp.float32

IN_VMEM = pl.BlockSpec(memory_space=pltpu.VMEM)
IN_SMEM = pl.BlockSpec(memory_space=pltpu.SMEM)


def params():
    return pltpu.CompilerParams(vmem_limit_bytes=VMEM_BYTES)


def cost(flops, moved, exps=0):
    return pl.CostEstimate(flops=flops, bytes_accessed=moved, transcendentals=exps)


def lanes(head):
    return pl.ds(pl.multiple_of(head * DH, DH), DH)


def rows(block):
    return pl.ds(pl.multiple_of(block * BLOCK, BLOCK), BLOCK)


def nt(a, b):
    return lax.dot_general(a, b, (((1,), (1,)), ((), ())), preferred_element_type=F32)


def nn(a, b):
    return lax.dot_general(a, b, (((1,), (0,)), ((), ())), preferred_element_type=F32)


def tn(a, b):
    return lax.dot_general(a, b, (((0,), (0,)), ((), ())), preferred_element_type=F32)


def pack_kernel(item_ref, key_ref, value_ref, slots_ref, low_ref, high_ref):
    per_step = slots_ref.shape[0]
    step = pl.program_id(0)

    def one(slot, carry):
        item = item_ref[step * per_step + slot]
        block, head = item >> 4, item & 15
        slots_ref[slot, 0] = key_ref[rows(block), lanes(head)]
        slots_ref[slot, 1] = value_ref[rows(block), lanes(head)]
        return carry

    lax.fori_loop(0, per_step, one, 0, unroll=4)

    @pl.when(step == 0)
    def _():
        low_ref[0] = key_ref[:BLOCK]
        low_ref[1] = value_ref[:BLOCK]
        high_ref[0] = key_ref[BLOCK:]
        high_ref[1] = value_ref[BLOCK:]


def pack(items, key_states, values):
    steps = 8
    edge = jax.ShapeDtypeStruct((2, BLOCK, HEADS * DH), BF16)
    whole = pl.BlockSpec((2 * BLOCK, HEADS * DH), lambda i, items: (0, 0))
    edge_spec = pl.BlockSpec(edge.shape, lambda i, items: (0, 0, 0))
    return pl.pallas_call(
        pack_kernel,
        grid_spec=pltpu.PrefetchScalarGridSpec(
            num_scalar_prefetch=1,
            grid=(steps,),
            in_specs=[whole, whole],
            out_specs=[
                pl.BlockSpec((SHARDS // steps, 2, BLOCK, DH), lambda i, items: (i, 0, 0, 0)),
                edge_spec,
                edge_spec,
            ],
        ),
        out_shape=[jax.ShapeDtypeStruct((SHARDS, 2, BLOCK, DH), BF16), edge, edge],
        compiler_params=params(),
        cost_estimate=cost(0, 6 * 2**20),
        name="pack",
    )(items, key_states, values)


def attend_kernel(
    pick_ref,
    where_ref,
    query_ref,
    grad_ref,
    key_ref,
    value_ref,
    far_ref,
    prev_ref,
    next_ref,
    ends_ref,
    attended_ref,
    query_grad_ref,
    terms_ref,
    own_ref,
    prev_terms_ref,
    next_terms_ref,
    end_terms_ref,
):
    shard, my_x, my_y = where_ref[0], where_ref[1], where_ref[2]
    column = lax.broadcasted_iota(jnp.int32, (1, 4 * BLOCK), 1)
    at_first, at_last = shard == 0, shard == LAST
    no_end = (at_first & (column >= 2 * BLOCK) & (column < 3 * BLOCK)) | (
        at_last & (column >= 3 * BLOCK)
    )
    shared_bias = jnp.where(no_end, MASKED, 0.0)
    bias = [
        jnp.where(at_first & (column < BLOCK), MASKED, 0.0),
        jnp.where(at_last & (column < BLOCK), MASKED, 0.0),
    ]
    halves = [slice(0, BLOCK), slice(BLOCK, 2 * BLOCK)]

    def one(head, carry):
        at = lanes(head)
        head_x, head_y = head >> 2, head & 3
        end = ((my_x - head_x) & 3) * 4 + ((my_y - head_y) & 3)
        end_to = ((head_x - my_x) & 3) * 4 + ((head_y - my_y) & 3)
        query, grad = query_ref[:, at], grad_ref[:, at]
        shared_key = jnp.concatenate([key_ref[:, at], ends_ref[end, 0, 0], ends_ref[end, 1, 0]])
        shared_value = jnp.concatenate(
            [value_ref[:, at], ends_ref[end, 0, 1], ends_ref[end, 1, 1]]
        )
        owners = [
            [pick_ref[b * PICKS + head * 3 + r] >> 1 for r in range(3)] for b in range(2)
        ]
        edges = [prev_ref, next_ref]
        own_key = [
            jnp.concatenate([edges[b][0, :, at]] + [far_ref[o, 0] for o in owners[b]])
            for b in range(2)
        ]
        own_value = [
            jnp.concatenate([edges[b][1, :, at]] + [far_ref[o, 1] for o in owners[b]])
            for b in range(2)
        ]

        def both(of):
            return jnp.concatenate([of(0), of(1)])

        score_a = nt(query, shared_key) + shared_bias
        score_b = both(lambda b: nt(query[halves[b]], own_key[b]) + bias[b])
        top = jnp.max(jnp.maximum(score_a, score_b), axis=1, keepdims=True)
        exp_a = jnp.exp2((score_a - top) * EXP2_SCALE)
        exp_b = jnp.exp2((score_b - top) * EXP2_SCALE)
        inverse = 1.0 / jnp.sum(exp_a + exp_b, axis=1, keepdims=True)
        weight_a, weight_b = exp_a * inverse, exp_b * inverse
        low_a, low_b = weight_a.astype(BF16), weight_b.astype(BF16)
        attended = nn(low_a, shared_value) + both(lambda b: nn(low_b[halves[b]], own_value[b]))
        attended = attended.astype(BF16)
        attended_ref[:, at] = attended
        row_dot = jnp.sum(grad.astype(F32) * attended.astype(F32), axis=1, keepdims=True)
        wgrad_a = nt(grad, shared_value)
        wgrad_b = both(lambda b: nt(grad[halves[b]], own_value[b]))
        sgrad_a = (weight_a * (wgrad_a - row_dot) * SCALE).astype(BF16)
        sgrad_b = (weight_b * (wgrad_b - row_dot) * SCALE).astype(BF16)
        query_grad = nn(sgrad_a, shared_key) + both(lambda b: nn(sgrad_b[halves[b]], own_key[b]))
        query_grad_ref[:, at] = query_grad.astype(BF16)

        for side, left_a, left_b, right in ((0, sgrad_a, sgrad_b, query), (1, low_a, low_b, grad)):
            shared = tn(left_a, right)
            own_ref[side, :, at] = shared[: 2 * BLOCK]
            end_terms_ref[end_to, 0, side] = shared[2 * BLOCK : 3 * BLOCK].astype(BF16)
            end_terms_ref[end_to, 1, side] = shared[3 * BLOCK :].astype(BF16)
            for b, edge_ref in enumerate((prev_terms_ref, next_terms_ref)):
                part = tn(left_b[halves[b]], right[halves[b]]).astype(BF16)
                edge_ref[side, :, at] = part[:BLOCK]
                for r in range(3):
                    terms_ref[owners[b][r], side] = part[(r + 1) * BLOCK : (r + 2) * BLOCK]
        return carry

    lax.fori_loop(0, HEADS, one, 0)


def attend(picks, where, query, grad, key, value, far, prev, following, ends):
    flat = jax.ShapeDtypeStruct((2 * BLOCK, HEADS * DH), BF16)
    edge = jax.ShapeDtypeStruct((2, BLOCK, HEADS * DH), BF16)
    return pl.pallas_call(
        attend_kernel,
        in_specs=[IN_SMEM, IN_SMEM] + [IN_VMEM] * 8,
        out_specs=[IN_VMEM] * 7,
        out_shape=[
            flat,
            flat,
            jax.ShapeDtypeStruct((SHARDS, 2, BLOCK, DH), BF16),
            jax.ShapeDtypeStruct((2, 2 * BLOCK, HEADS * DH), F32),
            edge,
            edge,
            jax.ShapeDtypeStruct((HEADS, 2, 2, BLOCK, DH), BF16),
        ],
        compiler_params=params(),
        cost_estimate=cost(2 * 10**9, 17 * 2**20, 10**6),
        name="attend",
    )(picks, where, query, grad, key, value, far, prev, following, ends)


def gather_kernel(
    item_ref, where_ref, terms_ref, own_ref, low_ref, high_ref, ends_ref, key_ref, value_ref, total_ref
):
    shard, my_x, my_y = where_ref[0], where_ref[1], where_ref[2]
    steps, per_step = pl.num_programs(0), terms_ref.shape[0]
    step = pl.program_id(0)

    @pl.when(step == 0)
    def _():
        total_ref[...] = jnp.zeros_like(total_ref)

    def one(slot, carry):
        item = item_ref[step * per_step + slot]
        for side in range(2):
            total_ref[item, side] += terms_ref[slot, side].astype(F32)
        return carry

    lax.fori_loop(0, per_step, one, 0, unroll=4)

    @pl.when(step == steps - 1)
    def _():
        @pl.when((shard == 0) | (shard == LAST))
        def _():
            block = jnp.where(shard == 0, 0, 1)
            for rel in range(HEADS):
                head = ((my_x + rel // 4) & 3) * 4 + ((my_y + rel % 4) & 3)
                total_ref[block * HEADS + head] += ends_ref[rel]

        for side, out_ref in enumerate((key_ref, value_ref)):
            for block, edge_ref in enumerate((low_ref, high_ref)):
                span = slice(block * BLOCK, (block + 1) * BLOCK)
                for head in range(HEADS):
                    at = slice(head * DH, (head + 1) * DH)
                    total = total_ref[block * HEADS + head, side] + own_ref[side, span, at]
                    total = total + edge_ref[side, :, at].astype(F32)
                    out_ref[span, at] = total.astype(BF16)


def gather(items, where, terms, own, low, high, ends):
    steps = 8
    flat = jax.ShapeDtypeStruct((2 * BLOCK, HEADS * DH), BF16)

    def whole(shape):
        return pl.BlockSpec(shape, lambda i, items, where: (0,) * len(shape))

    return pl.pallas_call(
        gather_kernel,
        grid_spec=pltpu.PrefetchScalarGridSpec(
            num_scalar_prefetch=2,
            grid=(steps,),
            in_specs=[
                pl.BlockSpec((SHARDS // steps, 2, BLOCK, DH), lambda i, items, where: (i, 0, 0, 0)),
                whole(own.shape),
                whole(low.shape),
                whole(high.shape),
                whole(ends.shape),
            ],
            out_specs=[whole(flat.shape), whole(flat.shape)],
            scratch_shapes=[pltpu.VMEM((2 * HEADS + 1, 2, BLOCK, DH), F32)],
        ),
        out_shape=[flat, flat],
        compiler_params=params(),
        cost_estimate=cost(10**6, 9 * 2**20),
        name="gather",
    )(items, where, terms, own, low, high, ends)


def shard_of(x, y, z):
    return (x % NX * NY + y % NY) * NZ + z


def send(value, route):
    return lax.ppermute(value, "seq", route)


def x_shift(by):
    cells = [(x, y, z) for x in range(NX) for y in range(NY) for z in range(NZ)]
    return [(shard_of(x, y, z), shard_of(x + by, y, z)) for x, y, z in cells]


def y_shift(by):
    cells = [(x, y, z) for x in range(NX) for y in range(NY) for z in range(NZ)]
    return [(shard_of(x, y, z), shard_of(x, y + by, z)) for x, y, z in cells]


def z_moves(pairs):
    cells = [(x, y) for x in range(NX) for y in range(NY)]
    return [(shard_of(x, y, a), shard_of(x, y, b)) for x, y in cells for a, b in pairs]


Z_SPREAD = (((0, 4), (7, 3)), ((0, 2), (4, 6), (7, 5), (3, 1)))
Z_SWAP = tuple((z, z ^ 1) for z in range(NZ))
FIRST = (0, 0, 0)
FINAL = (NX - 1, NY - 1, NZ - 1)


def spread_ends(low, high, my_x, my_y, my_z):
    shard = lax.axis_index("seq")
    mine = jnp.where(shard == 0, low, high).reshape(2, BLOCK, NX, NY * DH)
    roots = (FIRST, FINAL)

    def x_piece(by):
        return lax.dynamic_slice_in_dim(mine, (my_x + by) % NX, 1, 2)[:, :, 0]

    held = jnp.where((shard == 0) | (shard == LAST), x_piece(0), jnp.zeros((), BF16))
    arrived = [
        send(x_piece(by), [(shard_of(x, y, z), shard_of(x + by, y, z)) for x, y, z in roots])
        for by in range(1, NX)
    ]
    held = (held + arrived[0] + arrived[1] + arrived[2]).reshape(2, BLOCK, NY, DH)

    def y_piece(by):
        return lax.dynamic_slice_in_dim(held, (my_y + by) % NY, 1, 2)[:, :, 0]

    in_line = ((my_y == 0) & (my_z == 0)) | ((my_y == NY - 1) & (my_z == NZ - 1))
    arrived = [
        send(
            y_piece(by),
            [(shard_of(x, y, z), shard_of(x, y + by, z)) for x in range(NX) for _, y, z in roots],
        )
        for by in range(1, NY)
    ]
    kept = jnp.where(in_line, y_piece(0), jnp.zeros((), BF16))
    held = kept + arrived[0] + arrived[1] + arrived[2]
    for pairs in Z_SPREAD:
        held = held + send(held, z_moves(pairs))
    other = send(held, z_moves(Z_SWAP))
    even = my_z % 2 == 0
    pair = jnp.stack([jnp.where(even, held, other), jnp.where(even, other, held)])
    line = jnp.stack([pair] + [send(pair, y_shift(by)) for by in range(1, NY)])
    plane = jnp.stack([line] + [send(line, x_shift(by)) for by in range(1, NX)])
    return plane.reshape(HEADS, 2, 2, BLOCK, DH)


def collect_ends(terms, my_x, my_y, my_z):
    terms = terms.reshape(NX, NY, 2, 2, BLOCK, DH)
    line = terms[0].astype(F32)
    for by in range(1, NX):
        line = line + send(terms[by], x_shift(by)).astype(F32)
    low_line = line.astype(BF16)
    pair = line[0]
    for by in range(1, NY):
        pair = pair + send(low_line[by], y_shift(by)).astype(F32)
    even = my_z % 2 == 0
    held = jnp.where(even, pair[0], pair[1])
    held = held + send(jnp.where(even, pair[1], pair[0]), z_moves(Z_SWAP))
    for pairs in reversed(Z_SPREAD):
        held = held + send(held, z_moves([(b, a) for a, b in pairs]))
    roots = (FIRST, FINAL)
    line = jnp.stack(
        [held]
        + [
            send(
                held,
                [(shard_of(x, y + by, z), shard_of(x, y, z)) for x in range(NX) for _, y, z in roots],
            )
            for by in range(1, NY)
        ]
    )
    plane = jnp.stack(
        [line]
        + [
            send(line, [(shard_of(x + by, y, z), shard_of(x, y, z)) for x, y, z in roots])
            for by in range(1, NX)
        ]
    )
    return plane.reshape(HEADS, 2, BLOCK, DH)


def on_device(queries, key_states, values, out_grad, rand_blocks):
    shard = lax.axis_index("seq")
    my_x, my_y, my_z = shard // (NY * NZ), shard // NZ % NY, shard % NZ
    where = jnp.stack([shard, my_x, my_y]).astype(jnp.int32)
    wanted = rand_blocks // 2 == shard
    item = rand_blocks % 2 * HEADS + lax.broadcasted_iota(jnp.int32, rand_blocks.shape, 1)
    items = jnp.max(jnp.where(wanted, item, -1), axis=(1, 2))
    items = jnp.max(items.reshape(SHARDS, 2), axis=1)
    picks = lax.dynamic_slice_in_dim(rand_blocks, 2 * shard, 2, 0).reshape(2 * PICKS)

    slots, low, high = pack(jnp.maximum(items, 0), key_states, values)
    far = lax.all_to_all(slots, "seq", split_axis=0, concat_axis=0, tiled=True)
    prev = send(high, [(i, i + 1) for i in range(LAST)])
    following = send(low, [(i + 1, i) for i in range(LAST)])
    ends = spread_ends(low, high, my_x, my_y, my_z)
    attended, query_grad, terms, own, prev_terms, next_terms, end_terms = attend(
        picks, where, queries, out_grad, key_states, values, far, prev, following, ends
    )
    back = lax.all_to_all(terms, "seq", split_axis=0, concat_axis=0, tiled=True)
    from_next = send(prev_terms, [(i + 1, i) for i in range(LAST)])
    from_prev = send(next_terms, [(i, i + 1) for i in range(LAST)])
    end_sums = collect_ends(end_terms, my_x, my_y, my_z)
    key_grad, value_grad = gather(
        jnp.where(items < 0, 2 * HEADS, items), where, back, own, from_prev, from_next, end_sums
    )
    return (attended, query_grad, key_grad, value_grad)


def solution(mesh):
    placed = P("seq", "head")
    return jax.shard_map(
        on_device,
        mesh=mesh,
        in_specs=(placed, placed, placed, placed, P(None, "head", None)),
        out_specs=(placed, placed, placed, placed),
        check_vma=False,
    )
```

```python
import math

import jax
import jax.numpy as jnp
from jax import lax
from jax.experimental import pallas as pl
from jax.experimental.pallas import tpu as pltpu
from jax.sharding import PartitionSpec as P

DH = 128
BLOCK = 64
HEADS = 16
SHARDS = 128
LAST = SHARDS - 1
PICKS = 3 * HEADS
NX, NY, NZ = 4, 4, 8
VMEM_BYTES = 48 * 2**20
MASKED = -1e30
SCALE = 1.0 / math.sqrt(DH)
EXP2_SCALE = SCALE * math.log2(math.e)
BF16 = jnp.bfloat16
F32 = jnp.float32

IN_VMEM = pl.BlockSpec(memory_space=pltpu.VMEM)
IN_SMEM = pl.BlockSpec(memory_space=pltpu.SMEM)


def params():
    return pltpu.CompilerParams(vmem_limit_bytes=VMEM_BYTES)


def cost(flops, moved, exps=0):
    return pl.CostEstimate(flops=flops, bytes_accessed=moved, transcendentals=exps)


def lanes(head):
    return pl.ds(pl.multiple_of(head * DH, DH), DH)


def rows(block):
    return pl.ds(pl.multiple_of(block * BLOCK, BLOCK), BLOCK)


def nt(a, b):
    return lax.dot_general(a, b, (((1,), (1,)), ((), ())), preferred_element_type=F32)


def nn(a, b):
    return lax.dot_general(a, b, (((1,), (0,)), ((), ())), preferred_element_type=F32)


def tn(a, b):
    return lax.dot_general(a, b, (((0,), (0,)), ((), ())), preferred_element_type=F32)


def pack_kernel(item_ref, key_ref, value_ref, slots_ref, low_ref, high_ref):
    per_step = slots_ref.shape[0]
    step = pl.program_id(0)

    def one(slot, carry):
        item = item_ref[step * per_step + slot]
        block, head = item >> 4, item & 15
        slots_ref[slot, 0] = key_ref[rows(block), lanes(head)]
        slots_ref[slot, 1] = value_ref[rows(block), lanes(head)]
        return carry

    lax.fori_loop(0, per_step, one, 0, unroll=4)

    @pl.when(step == 0)
    def _():
        low_ref[0] = key_ref[:BLOCK]
        low_ref[1] = value_ref[:BLOCK]
        high_ref[0] = key_ref[BLOCK:]
        high_ref[1] = value_ref[BLOCK:]


def pack(items, key_states, values):
    steps = 8
    edge = jax.ShapeDtypeStruct((2, BLOCK, HEADS * DH), BF16)
    whole = pl.BlockSpec((2 * BLOCK, HEADS * DH), lambda i, items: (0, 0))
    edge_spec = pl.BlockSpec(edge.shape, lambda i, items: (0, 0, 0))
    return pl.pallas_call(
        pack_kernel,
        grid_spec=pltpu.PrefetchScalarGridSpec(
            num_scalar_prefetch=1,
            grid=(steps,),
            in_specs=[whole, whole],
            out_specs=[
                pl.BlockSpec((SHARDS // steps, 2, BLOCK, DH), lambda i, items: (i, 0, 0, 0)),
                edge_spec,
                edge_spec,
            ],
        ),
        out_shape=[jax.ShapeDtypeStruct((SHARDS, 2, BLOCK, DH), BF16), edge, edge],
        compiler_params=params(),
        cost_estimate=cost(0, 6 * 2**20),
        name="pack",
    )(items, key_states, values)


def attend_kernel(
    pick_ref,
    where_ref,
    query_ref,
    grad_ref,
    key_ref,
    value_ref,
    far_ref,
    prev_ref,
    next_ref,
    ends_ref,
    attended_ref,
    query_grad_ref,
    terms_ref,
    own_ref,
    prev_terms_ref,
    next_terms_ref,
    end_terms_ref,
):
    shard, my_x, my_y = where_ref[0], where_ref[1], where_ref[2]
    column = lax.broadcasted_iota(jnp.int32, (1, 4 * BLOCK), 1)
    at_first, at_last = shard == 0, shard == LAST
    no_end = (at_first & (column >= 2 * BLOCK) & (column < 3 * BLOCK)) | (
        at_last & (column >= 3 * BLOCK)
    )
    shared_bias = jnp.where(no_end, MASKED, 0.0)
    bias = [
        jnp.where(at_first & (column < BLOCK), MASKED, 0.0),
        jnp.where(at_last & (column < BLOCK), MASKED, 0.0),
    ]
    halves = [slice(0, BLOCK), slice(BLOCK, 2 * BLOCK)]

    def one(head, carry):
        at = lanes(head)
        head_x, head_y = head >> 2, head & 3
        end = ((my_x - head_x) & 3) * 4 + ((my_y - head_y) & 3)
        end_to = ((head_x - my_x) & 3) * 4 + ((head_y - my_y) & 3)
        query, grad = query_ref[:, at], grad_ref[:, at]
        shared_key = jnp.concatenate([key_ref[:, at], ends_ref[end, 0, 0], ends_ref[end, 1, 0]])
        shared_value = jnp.concatenate(
            [value_ref[:, at], ends_ref[end, 0, 1], ends_ref[end, 1, 1]]
        )
        owners = [
            [pick_ref[b * PICKS + head * 3 + r] >> 1 for r in range(3)] for b in range(2)
        ]
        edges = [prev_ref, next_ref]
        own_key = [
            jnp.concatenate([edges[b][0, :, at]] + [far_ref[o, 0] for o in owners[b]])
            for b in range(2)
        ]
        own_value = [
            jnp.concatenate([edges[b][1, :, at]] + [far_ref[o, 1] for o in owners[b]])
            for b in range(2)
        ]

        def both(of):
            return jnp.concatenate([of(0), of(1)])

        score_a = nt(query, shared_key) + shared_bias
        score_b = both(lambda b: nt(query[halves[b]], own_key[b]) + bias[b])
        top = jnp.max(jnp.maximum(score_a, score_b), axis=1, keepdims=True)
        exp_a = jnp.exp2((score_a - top) * EXP2_SCALE)
        exp_b = jnp.exp2((score_b - top) * EXP2_SCALE)
        inverse = 1.0 / jnp.sum(exp_a + exp_b, axis=1, keepdims=True)
        weight_a, weight_b = exp_a * inverse, exp_b * inverse
        low_a, low_b = weight_a.astype(BF16), weight_b.astype(BF16)
        attended = nn(low_a, shared_value) + both(lambda b: nn(low_b[halves[b]], own_value[b]))
        attended = attended.astype(BF16)
        attended_ref[:, at] = attended
        row_dot = jnp.sum(grad.astype(F32) * attended.astype(F32), axis=1, keepdims=True)
        wgrad_a = nt(grad, shared_value)
        wgrad_b = both(lambda b: nt(grad[halves[b]], own_value[b]))
        sgrad_a = (weight_a * (wgrad_a - row_dot) * SCALE).astype(BF16)
        sgrad_b = (weight_b * (wgrad_b - row_dot) * SCALE).astype(BF16)
        query_grad = nn(sgrad_a, shared_key) + both(lambda b: nn(sgrad_b[halves[b]], own_key[b]))
        query_grad_ref[:, at] = query_grad.astype(BF16)

        for side, left_a, left_b, right in ((0, sgrad_a, sgrad_b, query), (1, low_a, low_b, grad)):
            shared = tn(left_a, right)
            own_ref[side, :, at] = shared[: 2 * BLOCK]
            end_terms_ref[end_to, 0, side] = shared[2 * BLOCK : 3 * BLOCK].astype(BF16)
            end_terms_ref[end_to, 1, side] = shared[3 * BLOCK :].astype(BF16)
            for b, edge_ref in enumerate((prev_terms_ref, next_terms_ref)):
                part = tn(left_b[halves[b]], right[halves[b]]).astype(BF16)
                edge_ref[side, :, at] = part[:BLOCK]
                for r in range(3):
                    terms_ref[owners[b][r], side] = part[(r + 1) * BLOCK : (r + 2) * BLOCK]
        return carry

    lax.fori_loop(0, HEADS, one, 0, unroll=4)


def attend(picks, where, query, grad, key, value, far, prev, following, ends):
    flat = jax.ShapeDtypeStruct((2 * BLOCK, HEADS * DH), BF16)
    edge = jax.ShapeDtypeStruct((2, BLOCK, HEADS * DH), BF16)
    return pl.pallas_call(
        attend_kernel,
        in_specs=[IN_SMEM, IN_SMEM] + [IN_VMEM] * 8,
        out_specs=[IN_VMEM] * 7,
        out_shape=[
            flat,
            flat,
            jax.ShapeDtypeStruct((SHARDS, 2, BLOCK, DH), BF16),
            jax.ShapeDtypeStruct((2, 2 * BLOCK, HEADS * DH), F32),
            edge,
            edge,
            jax.ShapeDtypeStruct((HEADS, 2, 2, BLOCK, DH), BF16),
        ],
        compiler_params=params(),
        cost_estimate=cost(2 * 10**9, 17 * 2**20, 10**6),
        name="attend",
    )(picks, where, query, grad, key, value, far, prev, following, ends)


def gather_kernel(
    item_ref, terms_ref, own_ref, low_ref, high_ref, key_ref, value_ref, total_ref
):
    steps, per_step = pl.num_programs(0), terms_ref.shape[0]
    step = pl.program_id(0)

    @pl.when(step == 0)
    def _():
        total_ref[...] = jnp.zeros_like(total_ref)

    def one(slot, carry):
        item = item_ref[step * per_step + slot]
        for side in range(2):
            total_ref[item, side] += terms_ref[slot, side].astype(F32)
        return carry

    lax.fori_loop(0, per_step, one, 0, unroll=4)

    @pl.when(step == steps - 1)
    def _():
        for side, out_ref in enumerate((key_ref, value_ref)):
            for block, edge_ref in enumerate((low_ref, high_ref)):
                span = slice(block * BLOCK, (block + 1) * BLOCK)
                for head in range(HEADS):
                    at = slice(head * DH, (head + 1) * DH)
                    total = total_ref[block * HEADS + head, side] + own_ref[side, span, at]
                    total = total + edge_ref[side, :, at].astype(F32)
                    out_ref[span, at] = total.astype(BF16)


def gather(items, terms, own, low, high):
    steps = 8
    flat = jax.ShapeDtypeStruct((2 * BLOCK, HEADS * DH), BF16)

    def whole(shape):
        return pl.BlockSpec(shape, lambda i, items: (0,) * len(shape))

    return pl.pallas_call(
        gather_kernel,
        grid_spec=pltpu.PrefetchScalarGridSpec(
            num_scalar_prefetch=1,
            grid=(steps,),
            in_specs=[
                pl.BlockSpec((SHARDS // steps, 2, BLOCK, DH), lambda i, items: (i, 0, 0, 0)),
                whole(own.shape),
                whole(low.shape),
                whole(high.shape),
            ],
            out_specs=[whole(flat.shape), whole(flat.shape)],
            scratch_shapes=[pltpu.VMEM((2 * HEADS + 1, 2, BLOCK, DH), F32)],
        ),
        out_shape=[flat, flat],
        compiler_params=params(),
        cost_estimate=cost(10**6, 9 * 2**20),
        name="gather",
    )(items, terms, own, low, high)


def shard_of(x, y, z):
    return (x % NX * NY + y % NY) * NZ + z


def send(value, route):
    return lax.ppermute(value, "seq", route)


def x_shift(by):
    cells = [(x, y, z) for x in range(NX) for y in range(NY) for z in range(NZ)]
    return [(shard_of(x, y, z), shard_of(x + by, y, z)) for x, y, z in cells]


def y_shift(by):
    cells = [(x, y, z) for x in range(NX) for y in range(NY) for z in range(NZ)]
    return [(shard_of(x, y, z), shard_of(x, y + by, z)) for x, y, z in cells]


def spread_ends(pair):
    line = jnp.stack([pair] + [send(pair, y_shift(by)) for by in range(1, NY)])
    plane = jnp.stack([line] + [send(line, x_shift(by)) for by in range(1, NX)])
    return plane.reshape(HEADS, 2, 2, BLOCK, DH)


def sum_ends(terms):
    terms = terms.reshape(NX, NY, 2, 2, BLOCK, DH)
    line = terms[0].astype(F32)
    for by in range(1, NX):
        line = line + send(terms[by], x_shift(by)).astype(F32)
    low_line = line.astype(BF16)
    pair = line[0]
    for by in range(1, NY):
        pair = pair + send(low_line[by], y_shift(by)).astype(F32)
    return pair.astype(BF16)


def on_device(queries, key_states, values, out_grad, rand_blocks):
    shard = lax.axis_index("seq")
    where = jnp.stack([shard, shard // (NY * NZ), shard // NZ % NY]).astype(jnp.int32)
    wanted = rand_blocks // 2 == shard
    item = rand_blocks % 2 * HEADS + lax.broadcasted_iota(jnp.int32, rand_blocks.shape, 1)
    items = jnp.max(jnp.where(wanted, item, -1), axis=(1, 2))
    items = jnp.max(items.reshape(SHARDS, 2), axis=1)
    cell = jnp.arange(SHARDS, dtype=jnp.int32) // NZ
    items = jnp.where(shard == 0, cell, jnp.where(shard == LAST, HEADS + cell, items))
    picks = lax.dynamic_slice_in_dim(rand_blocks, 2 * shard, 2, 0).reshape(2 * PICKS)

    slots, low, high = pack(jnp.maximum(items, 0), key_states, values)
    far = lax.all_to_all(slots, "seq", split_axis=0, concat_axis=0, tiled=True)
    prev = send(high, [(i, i + 1) for i in range(LAST)])
    following = send(low, [(i + 1, i) for i in range(LAST)])
    far, prev, following = lax.optimization_barrier((far, prev, following))
    ends = spread_ends(jnp.stack([far[0], far[LAST]]))
    attended, query_grad, terms, own, prev_terms, next_terms, end_terms = attend(
        picks, where, queries, out_grad, key_states, values, far, prev, following, ends
    )
    end_pair = sum_ends(end_terms)
    terms = terms.at[0].set(end_pair[0]).at[LAST].set(end_pair[1])
    back = lax.all_to_all(terms, "seq", split_axis=0, concat_axis=0, tiled=True)
    from_next = send(prev_terms, [(i + 1, i) for i in range(LAST)])
    from_prev = send(next_terms, [(i, i + 1) for i in range(LAST)])
    key_grad, value_grad = gather(
        jnp.where(items < 0, 2 * HEADS, items), back, own, from_prev, from_next
    )
    return (attended, query_grad, key_grad, value_grad)


def solution(mesh):
    placed = P("seq", "head")
    return jax.shard_map(
        on_device,
        mesh=mesh,
        in_specs=(placed, placed, placed, placed, P(None, "head", None)),
        out_specs=(placed, placed, placed, placed),
        check_vma=False,
    )
```

```python
import math

import jax
import jax.numpy as jnp
from jax import lax
from jax.experimental import pallas as pl
from jax.experimental.pallas import tpu as pltpu
from jax.sharding import PartitionSpec as P

DH = 128
BLOCK = 64
HEADS = 16
SHARDS = 128
LAST = SHARDS - 1
PICKS = 3 * HEADS
NX, NY, NZ = 4, 4, 8
VMEM_BYTES = 32 * 2**20
MASKED = -1e30
SCALE = 1.0 / math.sqrt(DH)
EXP2_SCALE = SCALE * math.log2(math.e)
BF16 = jnp.bfloat16
F32 = jnp.float32

IN_VMEM = pl.BlockSpec(memory_space=pltpu.VMEM)
IN_SMEM = pl.BlockSpec(memory_space=pltpu.SMEM)


def params():
    return pltpu.CompilerParams(vmem_limit_bytes=VMEM_BYTES)


def cost(flops, moved, exps=0):
    return pl.CostEstimate(flops=flops, bytes_accessed=moved, transcendentals=exps)


def lanes(head):
    return pl.ds(pl.multiple_of(head * DH, DH), DH)


def rows(block):
    return pl.ds(pl.multiple_of(block * BLOCK, BLOCK), BLOCK)


def nt(a, b):
    return lax.dot_general(a, b, (((1,), (1,)), ((), ())), preferred_element_type=F32)


def nn(a, b):
    return lax.dot_general(a, b, (((1,), (0,)), ((), ())), preferred_element_type=F32)


def tn(a, b):
    return lax.dot_general(a, b, (((0,), (0,)), ((), ())), preferred_element_type=F32)


def pack_kernel(item_ref, key_ref, value_ref, slots_ref, sem):
    def moves(slot):
        item = item_ref[slot]
        block, head = item >> 4, item & 15
        return [
            pltpu.make_async_copy(
                ref.at[rows(block), lanes(head)], slots_ref.at[slot, side], sem.at[side]
            )
            for side, ref in enumerate((key_ref, value_ref))
        ]

    def start(slot, carry):
        for move in moves(slot):
            move.start()
        return carry

    lax.fori_loop(0, SHARDS, start, 0, unroll=8)
    for side in range(2):
        whole = slots_ref.at[:, side]
        pltpu.make_async_copy(whole, whole, sem.at[side]).wait()


def pack(items, key_states, values):
    return pl.pallas_call(
        pack_kernel,
        in_specs=[IN_SMEM, IN_VMEM, IN_VMEM],
        out_specs=pl.BlockSpec(memory_space=pl.ANY),
        out_shape=jax.ShapeDtypeStruct((SHARDS, 2, BLOCK, DH), BF16),
        scratch_shapes=[pltpu.SemaphoreType.DMA((2,))],
        compiler_params=params(),
        cost_estimate=cost(0, 6 * 2**20),
        name="pack",
    )(items, key_states, values)


HALVES = (slice(0, BLOCK), slice(BLOCK, 2 * BLOCK))
NEAR = 6 * BLOCK


def struct(shape, dtype=F32):
    return jax.ShapeDtypeStruct(shape, dtype)


def both(of):
    return jnp.concatenate([of(0), of(1)])


def owners_of(pick_ref, head):
    return [[pick_ref[b * PICKS + head * 3 + r] >> 1 for r in range(3)] for b in range(2)]


def near_blocks(side, at, edges, far_ref, owners):
    return [
        jnp.concatenate([edges[b][side, :, at]] + [far_ref[o, side] for o in owners[b]])
        for b in range(2)
    ]


def near_kernel(
    pick_ref,
    where_ref,
    query_ref,
    grad_ref,
    key_ref,
    value_ref,
    far_ref,
    prev_ref,
    next_ref,
    exp_ref,
    wgrad_ref,
    part_ref,
    top_ref,
    sum_ref,
):
    shard = where_ref[0]
    column = lax.broadcasted_iota(jnp.int32, (1, 4 * BLOCK), 1)
    bias = [
        jnp.where((shard == end) & (column < BLOCK), MASKED, 0.0) for end in (0, LAST)
    ]
    edges = (prev_ref, next_ref)

    def one(head, carry):
        at = lanes(head)
        query, grad = query_ref[:, at], grad_ref[:, at]
        key, value = key_ref[:, at], value_ref[:, at]
        owners = owners_of(pick_ref, head)
        keys = near_blocks(0, at, edges, far_ref, owners)
        values = near_blocks(1, at, edges, far_ref, owners)
        score_a = nt(query, key)
        score_b = both(lambda b: nt(query[HALVES[b]], keys[b]) + bias[b])
        score = jnp.concatenate([score_a, score_b], axis=1)
        top = jnp.max(score, axis=1, keepdims=True)
        exps = jnp.exp2((score - top) * EXP2_SCALE)
        top_ref[head] = top
        sum_ref[head] = jnp.sum(exps, axis=1, keepdims=True)
        exp_ref[head] = exps
        low = exps.astype(BF16)
        low_a, low_b = low[:, : 2 * BLOCK], low[:, 2 * BLOCK :]
        part_ref[head] = nn(low_a, value) + both(lambda b: nn(low_b[HALVES[b]], values[b]))
        wgrad_ref[head, :, : 2 * BLOCK] = nt(grad, value)
        for b in range(2):
            wgrad_ref[head, HALVES[b], 2 * BLOCK :] = nt(grad[HALVES[b]], values[b])
        return carry

    lax.fori_loop(0, HEADS, one, 0, unroll=4)


def near(picks, where, query, grad, key, value, far, prev, following):
    wide = struct((HEADS, 2 * BLOCK, NEAR))
    stat = struct((HEADS, 2 * BLOCK, 1))
    return pl.pallas_call(
        near_kernel,
        in_specs=[IN_SMEM, IN_SMEM] + [IN_VMEM] * 7,
        out_specs=[IN_VMEM] * 5,
        out_shape=[wide, wide, struct((HEADS, 2 * BLOCK, DH)), stat, stat],
        compiler_params=params(),
        cost_estimate=cost(6 * 10**8, 16 * 2**20, 10**6),
        name="near",
    )(picks, where, query, grad, key, value, far, prev, following)


def ends_kernel(
    where_ref,
    query_ref,
    grad_ref,
    part_ref,
    top_ref,
    sum_ref,
    ends0_ref,
    ends1_ref,
    ends2_ref,
    ends3_ref,
    attended_ref,
    query_part_ref,
    factor_ref,
    dot_ref,
    terms0_ref,
    terms1_ref,
    terms2_ref,
    terms3_ref,
):
    shard, my_x, my_y = where_ref[0], where_ref[1], where_ref[2]
    column = lax.broadcasted_iota(jnp.int32, (1, 2 * BLOCK), 1)
    no_end = ((shard == 0) & (column < BLOCK)) | ((shard == LAST) & (column >= BLOCK))
    bias = jnp.where(no_end, MASKED, 0.0)
    ends_refs = (ends0_ref, ends1_ref, ends2_ref, ends3_ref)
    terms_refs = (terms0_ref, terms1_ref, terms2_ref, terms3_ref)

    def one(ends_ref, terms_ref, head_x, y):
        head = head_x * 4 + ((my_y - y) & 3)
        to_y = (4 - y) & 3
        at = lanes(head)
        query, grad = query_ref[:, at], grad_ref[:, at]
        key = jnp.concatenate([ends_ref[y, 0, 0], ends_ref[y, 1, 0]])
        value = jnp.concatenate([ends_ref[y, 0, 1], ends_ref[y, 1, 1]])
        score = nt(query, key) + bias
        top = jnp.maximum(top_ref[head], jnp.max(score, axis=1, keepdims=True))
        exps = jnp.exp2((score - top) * EXP2_SCALE)
        shrink = jnp.exp2((top_ref[head] - top) * EXP2_SCALE)
        inverse = 1.0 / (sum_ref[head] * shrink + jnp.sum(exps, axis=1, keepdims=True))
        factor = shrink * inverse
        weight = exps * inverse
        low = weight.astype(BF16)
        attended = (part_ref[head] * factor + nn(low, value)).astype(BF16)
        attended_ref[:, at] = attended
        row_dot = jnp.sum(grad.astype(F32) * attended.astype(F32), axis=1, keepdims=True)
        sgrad = (weight * (nt(grad, value) - row_dot) * SCALE).astype(BF16)
        factor_ref[head] = factor
        dot_ref[head] = row_dot
        query_part_ref[head] = nn(sgrad, key)
        for side, left, right in ((0, sgrad, query), (1, low, grad)):
            terms = tn(left, right).astype(BF16)
            terms_ref[to_y, 0, side] = terms[:BLOCK]
            terms_ref[to_y, 1, side] = terms[BLOCK:]

    for x in range(NX):
        for y in range(NY):
            one(ends_refs[x], terms_refs[-x % NX], (my_x - x) & 3, y)


def ends(where, query, grad, part, top, total, lines):
    stat = struct((HEADS, 2 * BLOCK, 1))
    line = struct((NY, 2, 2, BLOCK, DH), BF16)
    return pl.pallas_call(
        ends_kernel,
        in_specs=[IN_SMEM] + [IN_VMEM] * 9,
        out_specs=[IN_VMEM] * 8,
        out_shape=[struct((2 * BLOCK, HEADS * DH), BF16), struct((HEADS, 2 * BLOCK, DH)), stat, stat]
        + [line] * NX,
        compiler_params=params(),
        cost_estimate=cost(4 * 10**8, 8 * 2**20, 3 * 10**5),
        name="ends",
    )(where, query, grad, part, top, total, *lines)


def rest_kernel(
    pick_ref,
    query_ref,
    grad_ref,
    key_ref,
    far_ref,
    prev_ref,
    next_ref,
    exp_ref,
    wgrad_ref,
    query_part_ref,
    factor_ref,
    dot_ref,
    query_grad_ref,
    terms_ref,
    own_ref,
    prev_terms_ref,
    next_terms_ref,
):
    edges = (prev_ref, next_ref)
    no_rows = jnp.zeros((BLOCK, DH), BF16)

    def split(block_rows):
        return jnp.concatenate(
            [
                jnp.concatenate([block_rows[HALVES[0]], no_rows], axis=1),
                jnp.concatenate([no_rows, block_rows[HALVES[1]]], axis=1),
            ]
        )

    def one(head, carry):
        at = lanes(head)
        query, grad = query_ref[:, at], grad_ref[:, at]
        owners = owners_of(pick_ref, head)
        keys = near_blocks(0, at, edges, far_ref, owners)
        weight = exp_ref[head] * factor_ref[head]
        low = weight.astype(BF16)
        sgrad = (weight * (wgrad_ref[head] - dot_ref[head]) * SCALE).astype(BF16)
        sgrad_b = sgrad[:, 2 * BLOCK :]
        query_grad = query_part_ref[head] + nn(sgrad[:, : 2 * BLOCK], key_ref[:, at])
        query_grad = query_grad + both(lambda b: nn(sgrad_b[HALVES[b]], keys[b]))
        query_grad_ref[:, at] = query_grad.astype(BF16)
        for side, left, right in ((0, sgrad, query), (1, low, grad)):
            own_ref[side, :, at] = tn(left[:, : 2 * BLOCK], right)
            parts = tn(left[:, 2 * BLOCK :], split(right)).astype(BF16)
            for b, edge_ref in enumerate((prev_terms_ref, next_terms_ref)):
                part = parts[:, b * DH : (b + 1) * DH]
                edge_ref[side, :, at] = part[:BLOCK]
                for r in range(3):
                    terms_ref[owners[b][r], side] = part[(r + 1) * BLOCK : (r + 2) * BLOCK]
        return carry

    lax.fori_loop(0, HEADS, one, 0, unroll=4)


def rest(picks, query, grad, key, far, prev, following, exps, wgrads, query_part, factor, dots):
    edge = struct((2, BLOCK, HEADS * DH), BF16)
    return pl.pallas_call(
        rest_kernel,
        in_specs=[IN_SMEM] + [IN_VMEM] * 11,
        out_specs=[IN_VMEM] * 5,
        out_shape=[
            struct((2 * BLOCK, HEADS * DH), BF16),
            struct((SHARDS, 2, BLOCK, DH), BF16),
            struct((2, 2 * BLOCK, HEADS * DH)),
            edge,
            edge,
        ],
        compiler_params=params(),
        cost_estimate=cost(8 * 10**8, 20 * 2**20),
        name="rest",
    )(picks, query, grad, key, far, prev, following, exps, wgrads, query_part, factor, dots)


def gather_kernel(
    order_ref, begin_ref, terms_ref, own_ref, low_ref, high_ref, key_ref, value_ref
):
    edges = (low_ref, high_ref)
    outs = (key_ref, value_ref)
    for block in range(2):
        for head in range(HEADS):
            item = block * HEADS + head
            at = slice(head * DH, (head + 1) * DH)

            def add(place, totals):
                slot = order_ref[place]
                return tuple(totals[side] + terms_ref[slot, side].astype(F32) for side in range(2))

            totals = tuple(
                own_ref[side, HALVES[block], at] + edges[block][side, :, at].astype(F32)
                for side in range(2)
            )
            totals = lax.fori_loop(begin_ref[item], begin_ref[item + 1], add, totals)
            for side in range(2):
                outs[side][HALVES[block], at] = totals[side].astype(BF16)


def gather(order, begins, terms, own, low, high):
    flat = struct((2 * BLOCK, HEADS * DH), BF16)
    return pl.pallas_call(
        gather_kernel,
        in_specs=[IN_SMEM, IN_SMEM] + [IN_VMEM] * 4,
        out_specs=[IN_VMEM] * 2,
        out_shape=[flat, flat],
        compiler_params=params(),
        cost_estimate=cost(10**6, 9 * 2**20),
        name="gather",
    )(order, begins, terms, own, low, high)


def shard_of(x, y, z):
    return (x % NX * NY + y % NY) * NZ + z


def send(value, route):
    return lax.ppermute(value, "seq", route)


def x_shift(by):
    cells = [(x, y, z) for x in range(NX) for y in range(NY) for z in range(NZ)]
    return [(shard_of(x, y, z), shard_of(x + by, y, z)) for x, y, z in cells]


def y_shift(by):
    cells = [(x, y, z) for x in range(NX) for y in range(NY) for z in range(NZ)]
    return [(shard_of(x, y, z), shard_of(x, y + by, z)) for x, y, z in cells]


def spread_ends(pair):
    line = jnp.stack([pair] + [send(pair, y_shift(by)) for by in range(1, NY)])
    return [line] + [send(line, x_shift(by)) for by in range(1, NX)]


def sum_ends(lines):
    line = lines[0].astype(F32)
    for by in range(1, NX):
        line = line + send(lines[by], x_shift(by)).astype(F32)
    low_line = line.astype(BF16)
    pair = line[0]
    for by in range(1, NY):
        pair = pair + send(low_line[by], y_shift(by)).astype(F32)
    return pair.astype(BF16)


def on_device(queries, key_states, values, out_grad, rand_blocks):
    shard = lax.axis_index("seq")
    where = jnp.stack([shard, shard // (NY * NZ), shard // NZ % NY]).astype(jnp.int32)
    wanted = rand_blocks // 2 == shard
    item = rand_blocks % 2 * HEADS + lax.broadcasted_iota(jnp.int32, rand_blocks.shape, 1)
    items = jnp.max(jnp.where(wanted, item, -1), axis=(1, 2))
    items = jnp.max(items.reshape(SHARDS, 2), axis=1)
    cell = jnp.arange(SHARDS, dtype=jnp.int32) // NZ
    items = jnp.where(shard == 0, cell, jnp.where(shard == LAST, HEADS + cell, items))
    picks = lax.dynamic_slice_in_dim(rand_blocks, 2 * shard, 2, 0).reshape(2 * PICKS)

    named = jnp.where(items < 0, 2 * HEADS, items)
    place = jnp.arange(SHARDS, dtype=jnp.int32)
    before = (named[None, :] < named[:, None]) | (
        (named[None, :] == named[:, None]) & (place[None, :] < place[:, None])
    )
    rank = jnp.sum(before.astype(jnp.int32), axis=1)
    order = jnp.sum(jnp.where(rank[None, :] == place[:, None], place[None, :], 0), axis=1)
    kinds = jnp.arange(2 * HEADS + 1, dtype=jnp.int32)
    begins = jnp.sum((named[None, :] < kinds[:, None]).astype(jnp.int32), axis=1)

    low = jnp.stack([key_states[:BLOCK], values[:BLOCK]])
    high = jnp.stack([key_states[BLOCK:], values[BLOCK:]])
    up, down = [(i, i + 1) for i in range(LAST)], [(i + 1, i) for i in range(LAST)]
    prev, following = send(high, up), send(low, down)
    slots = pack(jnp.maximum(items, 0), key_states, values)
    slots, prev, following = lax.optimization_barrier((slots, prev, following))
    far = lax.all_to_all(slots, "seq", split_axis=0, concat_axis=0, tiled=True)
    lines = spread_ends(jnp.stack([far[0], far[LAST]]))
    exps, wgrads, part, top, total = near(
        picks, where, queries, out_grad, key_states, values, far, prev, following
    )
    attended, query_part, factor, dots, *end_terms = ends(
        where, queries, out_grad, part, top, total, lines
    )
    end_pair = sum_ends(end_terms)
    query_grad, terms, own, prev_terms, next_terms = rest(
        picks, queries, out_grad, key_states, far, prev, following,
        exps, wgrads, query_part, factor, dots,
    )
    terms = terms.at[0].set(end_pair[0]).at[LAST].set(end_pair[1])
    back = lax.all_to_all(terms, "seq", split_axis=0, concat_axis=0, tiled=True)
    from_next, from_prev = send(prev_terms, down), send(next_terms, up)
    key_grad, value_grad = gather(order, begins, back, own, from_prev, from_next)
    return (attended, query_grad, key_grad, value_grad)


def solution(mesh):
    placed = P("seq", "head")
    return jax.shard_map(
        on_device,
        mesh=mesh,
        in_specs=(placed, placed, placed, placed, P(None, "head", None)),
        out_specs=(placed, placed, placed, placed),
        check_vma=False,
    )
```

```python
import math

import jax
import jax.numpy as jnp
from jax import lax
from jax.experimental import pallas as pl
from jax.experimental.pallas import tpu as pltpu
from jax.sharding import PartitionSpec as P

DH = 128
BLOCK = 64
HEADS = 16
SHARDS = 128
LAST = SHARDS - 1
PICKS = 3 * HEADS
NX, NY, NZ = 4, 4, 8
VMEM_BYTES = 60 * 2**20
MASKED = -1e30
SCALE = 1.0 / math.sqrt(DH)
EXP2_SCALE = SCALE * math.log2(math.e)
BF16 = jnp.bfloat16
F32 = jnp.float32

IN_VMEM = pl.BlockSpec(memory_space=pltpu.VMEM)
IN_SMEM = pl.BlockSpec(memory_space=pltpu.SMEM)
IN_HBM = pl.BlockSpec(memory_space=pltpu.HBM)


def params():
    return pltpu.CompilerParams(vmem_limit_bytes=VMEM_BYTES)


def cost(flops, moved, exps=0):
    return pl.CostEstimate(flops=flops, bytes_accessed=moved, transcendentals=exps)


def lanes(head):
    return pl.ds(pl.multiple_of(head * DH, DH), DH)


def rows(block):
    return pl.ds(pl.multiple_of(block * BLOCK, BLOCK), BLOCK)


def nt(a, b):
    return lax.dot_general(a, b, (((1,), (1,)), ((), ())), preferred_element_type=F32)


def nn(a, b):
    return lax.dot_general(a, b, (((1,), (0,)), ((), ())), preferred_element_type=F32)


def tn(a, b):
    return lax.dot_general(a, b, (((0,), (0,)), ((), ())), preferred_element_type=F32)


def pack_kernel(item_ref, key_ref, value_ref, slots_ref, sem):
    def moves(slot):
        item = item_ref[slot]
        block, head = item >> 4, item & 15
        return [
            pltpu.make_async_copy(
                ref.at[rows(block), lanes(head)], slots_ref.at[slot, side], sem.at[side]
            )
            for side, ref in enumerate((key_ref, value_ref))
        ]

    def start(slot, carry):
        for move in moves(slot):
            move.start()
        return carry

    lax.fori_loop(0, SHARDS, start, 0, unroll=8)
    for side in range(2):
        whole = slots_ref.at[:, side]
        pltpu.make_async_copy(whole, whole, sem.at[side]).wait()


def pack(items, key_states, values):
    return pl.pallas_call(
        pack_kernel,
        in_specs=[IN_SMEM, IN_VMEM, IN_VMEM],
        out_specs=pl.BlockSpec(memory_space=pl.ANY),
        out_shape=jax.ShapeDtypeStruct((SHARDS, 2, BLOCK, DH), BF16),
        scratch_shapes=[pltpu.SemaphoreType.DMA((2,))],
        compiler_params=params(),
        cost_estimate=cost(0, 6 * 2**20),
        name="pack",
    )(items, key_states, values)


HALVES = (slice(0, BLOCK), slice(BLOCK, 2 * BLOCK))
TOKENS_HERE = 2 * BLOCK
SOME = 4
STEPS = HEADS // SOME


def struct(shape, dtype=F32):
    return jax.ShapeDtypeStruct(shape, dtype)


def flat_spec(where_to):
    return pl.BlockSpec((TOKENS_HERE, SOME * DH), lambda *at: (0, where_to(*at)))


def edge_spec(where_to):
    return pl.BlockSpec((2, BLOCK, SOME * DH), lambda *at: (0, 0, where_to(*at)))


def head_spec(width, where_to):
    return pl.BlockSpec((SOME, TOKENS_HERE, width), lambda *at: (where_to(*at), 0, 0))


def grid_call(kernel, name, flops, moved, prefetch, in_specs, out_specs, out_shape, scratch=()):
    return pl.pallas_call(
        kernel,
        grid_spec=pltpu.PrefetchScalarGridSpec(
            num_scalar_prefetch=prefetch,
            grid=(STEPS,),
            in_specs=in_specs,
            out_specs=out_specs,
            scratch_shapes=scratch,
        ),
        out_shape=out_shape,
        compiler_params=params(),
        cost_estimate=cost(flops, moved, 10**6),
        name=name,
    )


def step_of(i, *scalars):
    return i


def columns_of(i):
    return slice(i * DH, (i + 1) * DH)


def both(of):
    return jnp.concatenate([of(0), of(1)])


def stacked(of):
    return jnp.concatenate([of(i) for i in range(SOME)])


def rows_of(i):
    return slice(i * TOKENS_HERE, (i + 1) * TOKENS_HERE)


def half_rows(i, b):
    return slice((2 * i + b) * BLOCK, (2 * i + b + 1) * BLOCK)


def owner_of(pick_ref, head, b, r):
    return pick_ref[b * PICKS + head * 3 + r] >> 1


def fetch(pick_ref, far_ref, held_ref, sem):
    def one(head, carry):
        for b in range(2):
            for r in range(3):
                source = far_ref.at[owner_of(pick_ref, head, b, r)]
                if len(held_ref.shape) == 4:
                    source = source.at[0]
                target = held_ref.at[head, b * 3 + r]
                pltpu.make_async_copy(source, target, sem.at[head]).start()
        return carry

    lax.fori_loop(0, HEADS, one, 0, unroll=4)


def fetched(held_ref, sem, head):
    pltpu.make_async_copy(held_ref.at[head], held_ref.at[head], sem.at[head]).wait()


def near_kernel(
    pick_ref,
    where_ref,
    query_ref,
    grad_ref,
    key_ref,
    value_ref,
    far_ref,
    prev_ref,
    next_ref,
    own_exp_ref,
    far_exp_ref,
    own_wgrad_ref,
    far_wgrad_ref,
    part_ref,
    stat_ref,
    held_ref,
    sem,
):
    step = pl.program_id(0)

    @pl.when(step == 0)
    def _():
        fetch(pick_ref, far_ref, held_ref, sem)

    shard = where_ref[0]
    column = lax.broadcasted_iota(jnp.int32, (1, 4 * BLOCK), 1)
    bias = [
        jnp.where((shard == end) & (column < BLOCK), MASKED, 0.0) for end in (0, LAST)
    ]
    edges = (prev_ref, next_ref)
    heads = [step * SOME + i for i in range(SOME)]
    queries = [query_ref[:, columns_of(i)] for i in range(SOME)]
    grads = [grad_ref[:, columns_of(i)] for i in range(SOME)]
    for head in heads:
        fetched(held_ref, sem, head)

    def picked(i, b, side):
        edge = edges[b][side, :, columns_of(i)]
        return jnp.concatenate([edge] + [held_ref[heads[i], b * 3 + r, side] for r in range(3)])

    keys, values = (
        [[picked(i, b, side) for b in range(2)] for i in range(SOME)] for side in range(2)
    )
    own_score = stacked(lambda i: nt(queries[i], key_ref[:, columns_of(i)]))
    far_score = stacked(lambda i: both(lambda b: nt(queries[i][HALVES[b]], keys[i][b]) + bias[b]))
    top = jnp.maximum(
        jnp.maximum(own_score, far_score[:, :TOKENS_HERE]), far_score[:, TOKENS_HERE:]
    )
    top = jnp.max(top, axis=1, keepdims=True)
    own_exp = jnp.exp2((own_score - top) * EXP2_SCALE)
    far_exp = jnp.exp2((far_score - top) * EXP2_SCALE)
    total = own_exp + far_exp[:, :TOKENS_HERE] + far_exp[:, TOKENS_HERE:]
    stat = jnp.concatenate([top, jnp.sum(total, axis=1, keepdims=True)], axis=1)
    own_low, far_low = own_exp.astype(BF16), far_exp.astype(BF16)
    for i in range(SOME):
        at = rows_of(i)
        own_exp_ref[i], far_exp_ref[i], stat_ref[i] = own_exp[at], far_exp[at], stat[at]
        own_wgrad_ref[i] = nt(grads[i], value_ref[:, columns_of(i)])
        far_part = both(lambda b: nn(far_low[half_rows(i, b)], values[i][b]))
        part_ref[i] = nn(own_low[at], value_ref[:, columns_of(i)]) + far_part
        for b in range(2):
            far_wgrad_ref[i, HALVES[b]] = nt(grads[i][HALVES[b]], values[i][b])


def near(picks, where, query, grad, key, value, far, prev, following):
    own, wide = (HEADS, TOKENS_HERE, TOKENS_HERE), (HEADS, TOKENS_HERE, 4 * BLOCK)
    return grid_call(
        near_kernel,
        "near",
        6 * 10**8,
        16 * 2**20,
        2,
        [flat_spec(step_of)] * 4 + [IN_HBM] + [edge_spec(step_of)] * 2,
        [head_spec(w, step_of) for w in (DH, 2 * DH, DH, 2 * DH, DH, 2)],
        [struct(own), struct(wide), struct(own), struct(wide), struct(own), struct(own[:2] + (2,))],
        [pltpu.VMEM((HEADS, 6, 2, BLOCK, DH), BF16), pltpu.SemaphoreType.DMA((HEADS,))],
    )(picks, where, query, grad, key, value, far, prev, following)


def ends_kernel(
    where_ref,
    query_ref,
    grad_ref,
    part_ref,
    stat_ref,
    ends0_ref,
    ends1_ref,
    ends2_ref,
    ends3_ref,
    attended_ref,
    query_part_ref,
    factor_ref,
    terms0_ref,
    terms1_ref,
    terms2_ref,
    terms3_ref,
):
    shard, my_y = where_ref[0], where_ref[2]
    column = lax.broadcasted_iota(jnp.int32, (1, TOKENS_HERE), 1)
    no_end = ((shard == 0) & (column < BLOCK)) | ((shard == LAST) & (column >= BLOCK))
    bias = jnp.where(no_end, MASKED, 0.0)
    ends_refs = (ends0_ref, ends1_ref, ends2_ref, ends3_ref)
    terms_refs = (terms0_ref, terms1_ref, terms2_ref, terms3_ref)

    def line(ends_ref, terms_ref):
        heads = [(my_y - y) & 3 for y in range(SOME)]
        queries = [query_ref[:, lanes(head)] for head in heads]
        grads = [grad_ref[:, lanes(head)] for head in heads]
        keys, values = (
            [jnp.concatenate([ends_ref[y, 0, side], ends_ref[y, 1, side]]) for y in range(SOME)]
            for side in range(2)
        )
        score = stacked(lambda i: nt(queries[i], keys[i])) + bias
        stat = stacked(lambda i: stat_ref[heads[i]])
        old_top = stat[:, 0:1]
        top = jnp.maximum(old_top, jnp.max(score, axis=1, keepdims=True))
        exps = jnp.exp2((score - top) * EXP2_SCALE)
        shrink = jnp.exp2((old_top - top) * EXP2_SCALE)
        total = stat[:, 1:2] * shrink
        inverse = 1.0 / (total + jnp.sum(exps, axis=1, keepdims=True))
        factor = shrink * inverse
        weight = exps * inverse
        low = weight.astype(BF16)
        wgrad = stacked(lambda i: nt(grads[i], values[i]))
        attended = stacked(lambda i: part_ref[heads[i]]) * factor
        attended = attended + stacked(lambda i: nn(low[rows_of(i)], values[i]))
        attended = attended.astype(BF16)
        grad = stacked(lambda i: grads[i].astype(F32))
        row_dot = jnp.sum(grad * attended.astype(F32), axis=1, keepdims=True)
        sgrad = (weight * (wgrad - row_dot) * SCALE).astype(BF16)
        stat = jnp.concatenate([factor, row_dot], axis=1)
        for i, head in enumerate(heads):
            at = rows_of(i)
            attended_ref[:, lanes(head)] = attended[at]
            factor_ref[head] = stat[at]
            query_part_ref[head] = nn(sgrad[at], keys[i])
            for side, left, right in ((0, sgrad, queries[i]), (1, low, grads[i])):
                terms = tn(left[at], right).astype(BF16)
                terms_ref[-i % NY, 0, side] = terms[:BLOCK]
                terms_ref[-i % NY, 1, side] = terms[BLOCK:]

    for x in range(NX):
        pl.when(pl.program_id(0) == x)(
            lambda x=x: line(ends_refs[x], terms_refs[-x % NX])
        )


def ends(where, query, grad, part, stat, lines):
    line = struct((NY, 2, 2, BLOCK, DH), BF16)
    line_spec = pl.BlockSpec(line.shape, lambda i, where: (0,) * 5)
    own = (HEADS, TOKENS_HERE, DH)

    def line_heads(i, where):
        return (where[1] - i) & 3

    return grid_call(
        ends_kernel,
        "ends",
        4 * 10**8,
        8 * 2**20,
        1,
        [flat_spec(line_heads)] * 2
        + [head_spec(DH, line_heads), head_spec(2, line_heads)]
        + [line_spec] * NX,
        [flat_spec(line_heads), head_spec(DH, line_heads), head_spec(2, line_heads)]
        + [line_spec] * NX,
        [struct((TOKENS_HERE, HEADS * DH), BF16), struct(own), struct(own[:2] + (2,))]
        + [line] * NX,
    )(where, query, grad, part, stat, *lines)


def far_terms_kernel(
    pick_ref,
    query_ref,
    grad_ref,
    exp_ref,
    wgrad_ref,
    factor_ref,
    terms_ref,
    prev_terms_ref,
    next_terms_ref,
    made_ref,
    sem,
):
    step = pl.program_id(0)
    no_rows = jnp.zeros((BLOCK, DH), BF16)

    def split(block_rows):
        return jnp.concatenate(
            [
                jnp.concatenate([block_rows[HALVES[0]], no_rows], axis=1),
                jnp.concatenate([no_rows, block_rows[HALVES[1]]], axis=1),
            ]
        )

    for i in range(SOME):
        head = step * SOME + i
        at = columns_of(i)
        weight = exp_ref[i] * factor_ref[i, :, 0:1]
        low = weight.astype(BF16)
        sgrad = (weight * (wgrad_ref[i] - factor_ref[i, :, 1:2]) * SCALE).astype(BF16)
        for side, left, right in ((0, sgrad, query_ref[:, at]), (1, low, grad_ref[:, at])):
            parts = tn(left, split(right)).astype(BF16)
            for b, edge_ref in enumerate((prev_terms_ref, next_terms_ref)):
                part = parts[:, columns_of(b)]
                edge_ref[side, :, at] = part[:BLOCK]
                for r in range(3):
                    made_ref[head, b * 3 + r, side] = part[(r + 1) * BLOCK : (r + 2) * BLOCK]
        for b in range(2):
            for r in range(3):
                pltpu.make_async_copy(
                    made_ref.at[head, b * 3 + r],
                    terms_ref.at[owner_of(pick_ref, head, b, r)],
                    sem.at[0],
                ).start()

    @pl.when(step == STEPS - 1)
    def _():
        pltpu.make_async_copy(made_ref, made_ref, sem.at[0]).wait()


def far_terms(picks, query, grad, exps, wgrads, factor):
    edge = struct((2, BLOCK, HEADS * DH), BF16)
    return grid_call(
        far_terms_kernel,
        "far_terms",
        4 * 10**8,
        14 * 2**20,
        1,
        [flat_spec(step_of)] * 2 + [head_spec(w, step_of) for w in (2 * DH, 2 * DH, 2)],
        [IN_HBM, edge_spec(step_of), edge_spec(step_of)],
        [struct((SHARDS, 2, BLOCK, DH), BF16), edge, edge],
        [pltpu.VMEM((HEADS, 6, 2, BLOCK, DH), BF16), pltpu.SemaphoreType.DMA((1,))],
    )(picks, query, grad, exps, wgrads, factor)


def own_terms_kernel(
    pick_ref,
    query_ref,
    grad_ref,
    key_ref,
    far_ref,
    prev_ref,
    next_ref,
    own_exp_ref,
    far_exp_ref,
    own_wgrad_ref,
    far_wgrad_ref,
    query_part_ref,
    factor_ref,
    query_grad_ref,
    own_ref,
    held_ref,
    sem,
):
    step = pl.program_id(0)

    @pl.when(step == 0)
    def _():
        fetch(pick_ref, far_ref, held_ref, sem)

    edges = (prev_ref, next_ref)
    for i in range(SOME):
        head = step * SOME + i
        at = columns_of(i)
        fetched(held_ref, sem, head)
        factor, row_dot = factor_ref[i, :, 0:1], factor_ref[i, :, 1:2]
        weight = own_exp_ref[i] * factor
        sgrad = (weight * (own_wgrad_ref[i] - row_dot) * SCALE).astype(BF16)
        far_sgrad = far_exp_ref[i] * factor * (far_wgrad_ref[i] - row_dot) * SCALE
        far_sgrad = far_sgrad.astype(BF16)

        def far_key(b):
            picked = [held_ref[head, b * 3 + r] for r in range(3)]
            return jnp.concatenate([edges[b][0, :, at]] + picked)

        query_grad = query_part_ref[i] + nn(sgrad, key_ref[:, at])
        query_grad = query_grad + both(lambda b: nn(far_sgrad[HALVES[b]], far_key(b)))
        query_grad_ref[:, at] = query_grad.astype(BF16)
        own_ref[0, :, at] = tn(sgrad, query_ref[:, at])
        own_ref[1, :, at] = tn(weight.astype(BF16), grad_ref[:, at])


def own_terms(picks, query, grad, key, far, prev, following, exps, wgrads, query_part, factor):
    return grid_call(
        own_terms_kernel,
        "own_terms",
        5 * 10**8,
        16 * 2**20,
        1,
        [flat_spec(step_of)] * 3
        + [IN_HBM]
        + [edge_spec(step_of)] * 2
        + [head_spec(w, step_of) for w in (DH, 2 * DH, DH, 2 * DH, DH, 2)],
        [
            flat_spec(step_of),
            pl.BlockSpec((2, TOKENS_HERE, SOME * DH), lambda i, picks: (0, 0, i)),
        ],
        [
            struct((TOKENS_HERE, HEADS * DH), BF16),
            struct((2, TOKENS_HERE, HEADS * DH)),
        ],
        [pltpu.VMEM((HEADS, 6, BLOCK, DH), BF16), pltpu.SemaphoreType.DMA((HEADS,))],
    )(picks, query, grad, key, far, prev, following, *exps, *wgrads, query_part, factor)


def gather_kernel(
    order_ref, begin_ref, terms_ref, own_ref, low_ref, high_ref, key_ref, value_ref
):
    edges = (low_ref, high_ref)
    outs = (key_ref, value_ref)
    for block in range(2):
        for head in range(HEADS):
            item = block * HEADS + head
            at = slice(head * DH, (head + 1) * DH)

            def add(place, totals):
                slot = order_ref[place]
                return tuple(totals[side] + terms_ref[slot, side].astype(F32) for side in range(2))

            totals = tuple(
                own_ref[side, HALVES[block], at] + edges[block][side, :, at].astype(F32)
                for side in range(2)
            )
            totals = lax.fori_loop(begin_ref[item], begin_ref[item + 1], add, totals)
            for side in range(2):
                outs[side][HALVES[block], at] = totals[side].astype(BF16)


def gather(order, begins, terms, own, low, high):
    flat = struct((2 * BLOCK, HEADS * DH), BF16)
    return pl.pallas_call(
        gather_kernel,
        in_specs=[IN_SMEM, IN_SMEM] + [IN_VMEM] * 4,
        out_specs=[IN_VMEM] * 2,
        out_shape=[flat, flat],
        compiler_params=params(),
        cost_estimate=cost(10**6, 9 * 2**20),
        name="gather",
    )(order, begins, terms, own, low, high)


def shard_of(x, y, z):
    return (x % NX * NY + y % NY) * NZ + z


def send(value, route):
    return lax.ppermute(value, "seq", route)


def x_shift(by):
    cells = [(x, y, z) for x in range(NX) for y in range(NY) for z in range(NZ)]
    return [(shard_of(x, y, z), shard_of(x + by, y, z)) for x, y, z in cells]


def y_shift(by):
    cells = [(x, y, z) for x in range(NX) for y in range(NY) for z in range(NZ)]
    return [(shard_of(x, y, z), shard_of(x, y + by, z)) for x, y, z in cells]


def spread_ends(pair):
    line = jnp.stack([pair] + [send(pair, y_shift(by)) for by in range(1, NY)])
    return [line] + [send(line, x_shift(by)) for by in range(1, NX)]


def sum_line(lines):
    line = lines[0].astype(F32)
    for by in range(1, NX):
        line = line + send(lines[by], x_shift(by)).astype(F32)
    return line.astype(BF16), line[0]


def sum_plane(low_line, pair):
    for by in range(1, NY):
        pair = pair + send(low_line[by], y_shift(by)).astype(F32)
    return pair.astype(BF16)


def on_device(queries, key_states, values, out_grad, rand_blocks):
    shard = lax.axis_index("seq")
    where = jnp.stack([shard, shard // (NY * NZ), shard // NZ % NY]).astype(jnp.int32)
    wanted = rand_blocks // 2 == shard
    item = rand_blocks % 2 * HEADS + lax.broadcasted_iota(jnp.int32, rand_blocks.shape, 1)
    items = jnp.max(jnp.where(wanted, item, -1), axis=(1, 2))
    items = jnp.max(items.reshape(SHARDS, 2), axis=1)
    cell = jnp.arange(SHARDS, dtype=jnp.int32) // NZ
    items = jnp.where(shard == 0, cell, jnp.where(shard == LAST, HEADS + cell, items))
    picks = lax.dynamic_slice_in_dim(rand_blocks, 2 * shard, 2, 0).reshape(2 * PICKS)

    named = jnp.where(items < 0, 2 * HEADS, items)
    place = jnp.arange(SHARDS, dtype=jnp.int32)
    before = (named[None, :] < named[:, None]) | (
        (named[None, :] == named[:, None]) & (place[None, :] < place[:, None])
    )
    rank = jnp.sum(before.astype(jnp.int32), axis=1)
    order = jnp.sum(jnp.where(rank[None, :] == place[:, None], place[None, :], 0), axis=1)
    kinds = jnp.arange(2 * HEADS + 1, dtype=jnp.int32)
    begins = jnp.sum((named[None, :] < kinds[:, None]).astype(jnp.int32), axis=1)

    low = jnp.stack([key_states[:BLOCK], values[:BLOCK]])
    high = jnp.stack([key_states[BLOCK:], values[BLOCK:]])
    up, down = [(i, i + 1) for i in range(LAST)], [(i + 1, i) for i in range(LAST)]
    slots = pack(jnp.maximum(items, 0), key_states, values)
    far = lax.all_to_all(slots, "seq", split_axis=0, concat_axis=0, tiled=True)
    far, low, high = lax.optimization_barrier((far, low, high))
    lines = spread_ends(jnp.stack([far[0], far[LAST]]))
    prev, following = send(high, up), send(low, down)
    own_exps, far_exps, own_wgrads, far_wgrads, part, stat = near(
        picks, where, queries, out_grad, key_states, values, far, prev, following
    )
    attended, query_part, factor, *end_terms = ends(where, queries, out_grad, part, stat, lines)
    low_line, pair = sum_line(end_terms)
    terms, prev_terms, next_terms = far_terms(
        picks, queries, out_grad, far_exps, far_wgrads, factor
    )
    low_line, pair, terms = lax.optimization_barrier((low_line, pair, terms))
    end_pair = sum_plane(low_line, pair)
    terms = terms.at[0].set(end_pair[0]).at[LAST].set(end_pair[1])
    back = lax.all_to_all(terms, "seq", split_axis=0, concat_axis=0, tiled=True)
    from_next, from_prev = send(prev_terms, down), send(next_terms, up)
    query_grad, own = own_terms(
        picks, queries, out_grad, key_states, far, prev, following,
        (own_exps, far_exps), (own_wgrads, far_wgrads), query_part, factor,
    )
    key_grad, value_grad = gather(order, begins, back, own, from_prev, from_next)
    return (attended, query_grad, key_grad, value_grad)


def solution(mesh):
    placed = P("seq", "head")
    return jax.shard_map(
        on_device,
        mesh=mesh,
        in_specs=(placed, placed, placed, placed, P(None, "head", None)),
        out_specs=(placed, placed, placed, placed),
        check_vma=False,
    )
```

```python
import math

import jax
import jax.numpy as jnp
from jax import lax
from jax.experimental import pallas as pl
from jax.experimental.pallas import tpu as pltpu
from jax.sharding import PartitionSpec as P

DH = 128
BLOCK = 64
HEADS = 16
SHARDS = 128
LAST = SHARDS - 1
PICKS = 3 * HEADS
NX, NY, NZ = 4, 4, 8
VMEM_BYTES = 60 * 2**20
MASKED = -1e30
SCALE = 1.0 / math.sqrt(DH)
EXP2_SCALE = SCALE * math.log2(math.e)
BF16 = jnp.bfloat16
F32 = jnp.float32

IN_VMEM = pl.BlockSpec(memory_space=pltpu.VMEM)
IN_SMEM = pl.BlockSpec(memory_space=pltpu.SMEM)
IN_HBM = pl.BlockSpec(memory_space=pltpu.HBM)


def params():
    return pltpu.CompilerParams(vmem_limit_bytes=VMEM_BYTES)


def cost(flops, moved, exps=0):
    return pl.CostEstimate(flops=flops, bytes_accessed=moved, transcendentals=exps)


def lanes(head):
    return pl.ds(pl.multiple_of(head * DH, DH), DH)


def rows(block):
    return pl.ds(pl.multiple_of(block * BLOCK, BLOCK), BLOCK)


def nt(a, b):
    return lax.dot_general(a, b, (((1,), (1,)), ((), ())), preferred_element_type=F32)


def nn(a, b):
    return lax.dot_general(a, b, (((1,), (0,)), ((), ())), preferred_element_type=F32)


def tn(a, b):
    return lax.dot_general(a, b, (((0,), (0,)), ((), ())), preferred_element_type=F32)


def pack_kernel(item_ref, key_ref, value_ref, slots_ref, sem):
    def moves(slot):
        item = item_ref[slot]
        block, head = item >> 4, item & 15
        return [
            pltpu.make_async_copy(
                ref.at[rows(block), lanes(head)], slots_ref.at[slot, side], sem.at[side]
            )
            for side, ref in enumerate((key_ref, value_ref))
        ]

    def start(slot, carry):
        for move in moves(slot):
            move.start()
        return carry

    lax.fori_loop(0, SHARDS, start, 0, unroll=8)
    for side in range(2):
        whole = slots_ref.at[:, side]
        pltpu.make_async_copy(whole, whole, sem.at[side]).wait()


def pack(items, key_states, values):
    return pl.pallas_call(
        pack_kernel,
        in_specs=[IN_SMEM, IN_VMEM, IN_VMEM],
        out_specs=pl.BlockSpec(memory_space=pl.ANY),
        out_shape=jax.ShapeDtypeStruct((SHARDS, 2, BLOCK, DH), BF16),
        scratch_shapes=[pltpu.SemaphoreType.DMA((2,))],
        compiler_params=params(),
        cost_estimate=cost(0, 6 * 2**20),
        name="pack",
    )(items, key_states, values)


PICKED = slice(0, 3 * BLOCK)
HALVES = (slice(0, BLOCK), slice(BLOCK, 2 * BLOCK))
TOKENS_HERE = 2 * BLOCK
SOME = 4
STEPS = HEADS // SOME


def struct(shape, dtype=F32):
    return jax.ShapeDtypeStruct(shape, dtype)


def flat_spec(where_to):
    return pl.BlockSpec((TOKENS_HERE, SOME * DH), lambda *at: (0, where_to(*at)))


def edge_spec(where_to):
    return pl.BlockSpec((2, BLOCK, SOME * DH), lambda *at: (0, 0, where_to(*at)))


def head_spec(width, where_to):
    return pl.BlockSpec((SOME, TOKENS_HERE, width), lambda *at: (where_to(*at), 0, 0))


def grid_call(kernel, name, flops, moved, prefetch, in_specs, out_specs, out_shape, scratch=()):
    return pl.pallas_call(
        kernel,
        grid_spec=pltpu.PrefetchScalarGridSpec(
            num_scalar_prefetch=prefetch,
            grid=(STEPS,),
            in_specs=in_specs,
            out_specs=out_specs,
            scratch_shapes=scratch,
        ),
        out_shape=out_shape,
        compiler_params=params(),
        cost_estimate=cost(flops, moved, 10**6),
        name=name,
    )


def step_of(i, *scalars):
    return i


def columns_of(i):
    return slice(i * DH, (i + 1) * DH)


def both(of):
    return jnp.concatenate([of(0), of(1)])


def stacked(of):
    return jnp.concatenate([of(i) for i in range(SOME)])


def rows_of(i):
    return slice(i * TOKENS_HERE, (i + 1) * TOKENS_HERE)


def half_rows(i, b):
    return slice((2 * i + b) * BLOCK, (2 * i + b + 1) * BLOCK)


def no_block():
    return jnp.zeros((BLOCK, DH), BF16)


def split(block_rows):
    return jnp.concatenate(
        [
            jnp.concatenate([block_rows[HALVES[0]], no_block()], axis=1),
            jnp.concatenate([no_block(), block_rows[HALVES[1]]], axis=1),
        ]
    )


def owner_of(pick_ref, head, b, r):
    return pick_ref[b * PICKS + head * 3 + r] >> 1


def fetch(pick_ref, far_ref, held_ref, sem):
    def one(head, carry):
        for b in range(2):
            for r in range(3):
                source = far_ref.at[owner_of(pick_ref, head, b, r)]
                if len(held_ref.shape) == 4:
                    source = source.at[0]
                target = held_ref.at[head, b * 3 + r]
                pltpu.make_async_copy(source, target, sem.at[head]).start()
        return carry

    lax.fori_loop(0, HEADS, one, 0, unroll=4)


def fetched(held_ref, sem, head):
    pltpu.make_async_copy(held_ref.at[head], held_ref.at[head], sem.at[head]).wait()


def near_kernel(
    pick_ref,
    query_ref,
    grad_ref,
    key_ref,
    value_ref,
    far_ref,
    own_exp_ref,
    far_exp_ref,
    own_wgrad_ref,
    far_wgrad_ref,
    part_ref,
    stat_ref,
    held_ref,
    sem,
):
    step = pl.program_id(0)

    @pl.when(step == 0)
    def _():
        fetch(pick_ref, far_ref, held_ref, sem)

    column = lax.broadcasted_iota(jnp.int32, (1, 4 * BLOCK), 1)
    bias = jnp.where(column >= 3 * BLOCK, MASKED, 0.0)
    heads = [step * SOME + i for i in range(SOME)]
    queries = [query_ref[:, columns_of(i)] for i in range(SOME)]
    grads = [grad_ref[:, columns_of(i)] for i in range(SOME)]
    for head in heads:
        fetched(held_ref, sem, head)

    def picked(i, b, side):
        blocks = [held_ref[heads[i], b * 3 + r, side] for r in range(3)]
        return jnp.concatenate(blocks + [no_block()])

    keys, values = (
        [[picked(i, b, side) for b in range(2)] for i in range(SOME)] for side in range(2)
    )
    own_score = stacked(lambda i: nt(queries[i], key_ref[:, columns_of(i)]))
    far_score = stacked(lambda i: both(lambda b: nt(queries[i][HALVES[b]], keys[i][b]) + bias))
    top = jnp.maximum(
        jnp.maximum(own_score, far_score[:, :TOKENS_HERE]), far_score[:, TOKENS_HERE:]
    )
    top = jnp.max(top, axis=1, keepdims=True)
    own_exp = jnp.exp2((own_score - top) * EXP2_SCALE)
    far_exp = jnp.exp2((far_score - top) * EXP2_SCALE)
    total = own_exp + far_exp[:, :TOKENS_HERE] + far_exp[:, TOKENS_HERE:]
    stat = jnp.concatenate([top, jnp.sum(total, axis=1, keepdims=True)], axis=1)
    own_low, far_low = own_exp.astype(BF16), far_exp.astype(BF16)
    for i in range(SOME):
        at = rows_of(i)
        own_exp_ref[i], far_exp_ref[i], stat_ref[i] = own_exp[at], far_exp[at], stat[at]
        own_wgrad_ref[i] = nt(grads[i], value_ref[:, columns_of(i)])
        far_part = both(lambda b: nn(far_low[half_rows(i, b)], values[i][b]))
        part_ref[i] = nn(own_low[at], value_ref[:, columns_of(i)]) + far_part
        for b in range(2):
            far_wgrad_ref[i, HALVES[b]] = nt(grads[i][HALVES[b]], values[i][b])


def near(picks, query, grad, key, value, far):
    own, wide = (HEADS, TOKENS_HERE, TOKENS_HERE), (HEADS, TOKENS_HERE, 4 * BLOCK)
    return grid_call(
        near_kernel,
        "near",
        6 * 10**8,
        16 * 2**20,
        1,
        [flat_spec(step_of)] * 4 + [IN_HBM],
        [head_spec(w, step_of) for w in (DH, 2 * DH, DH, 2 * DH, DH, 2)],
        [struct(own), struct(wide), struct(own), struct(wide), struct(own), struct(own[:2] + (2,))],
        [pltpu.VMEM((HEADS, 6, 2, BLOCK, DH), BF16), pltpu.SemaphoreType.DMA((HEADS,))],
    )(picks, query, grad, key, value, far)


def ends_kernel(
    where_ref,
    query_ref,
    grad_ref,
    part_ref,
    stat_ref,
    ends_ref,
    prev_ref,
    next_ref,
    attended_ref,
    query_part_ref,
    factor_ref,
    terms_ref,
    prev_terms_ref,
    next_terms_ref,
):
    shard = where_ref[0]
    column = lax.broadcasted_iota(jnp.int32, (1, TOKENS_HERE), 1)
    no_end = ((shard == 0) & (column < BLOCK)) | ((shard == LAST) & (column >= BLOCK))
    bias = jnp.where(no_end, MASKED, 0.0)
    edge_bias = [
        jnp.where((shard == end) | (column >= BLOCK), MASKED, 0.0) for end in (0, LAST)
    ]
    edges = (prev_ref, next_ref)
    queries = [query_ref[:, columns_of(i)] for i in range(SOME)]
    grads = [grad_ref[:, columns_of(i)] for i in range(SOME)]
    keys, values = (
        [jnp.concatenate([ends_ref[i, 0, side], ends_ref[i, 1, side]]) for i in range(SOME)]
        for side in range(2)
    )
    edge_keys, edge_values = (
        [
            [jnp.concatenate([edge[side, :, columns_of(i)], no_block()]) for edge in edges]
            for i in range(SOME)
        ]
        for side in range(2)
    )

    def by_edge(of):
        return stacked(lambda i: both(lambda b: of(i, b)))

    score = stacked(lambda i: nt(queries[i], keys[i])) + bias
    edge_score = by_edge(lambda i, b: nt(queries[i][HALVES[b]], edge_keys[i][b]) + edge_bias[b])
    stat = stacked(lambda i: stat_ref[i])
    old_top = stat[:, 0:1]
    top = jnp.max(jnp.maximum(score, edge_score), axis=1, keepdims=True)
    top = jnp.maximum(old_top, top)
    exps = jnp.exp2((score - top) * EXP2_SCALE)
    edge_exps = jnp.exp2((edge_score - top) * EXP2_SCALE)
    shrink = jnp.exp2((old_top - top) * EXP2_SCALE)
    total = stat[:, 1:2] * shrink
    inverse = 1.0 / (total + jnp.sum(exps + edge_exps, axis=1, keepdims=True))
    factor = shrink * inverse
    weight, edge_weight = exps * inverse, edge_exps * inverse
    low, edge_low = weight.astype(BF16), edge_weight.astype(BF16)
    wgrad = stacked(lambda i: nt(grads[i], values[i]))
    edge_wgrad = by_edge(lambda i, b: nt(grads[i][HALVES[b]], edge_values[i][b]))
    attended = stacked(lambda i: part_ref[i]) * factor
    attended = attended + stacked(lambda i: nn(low[rows_of(i)], values[i]))
    attended = attended + by_edge(lambda i, b: nn(edge_low[half_rows(i, b)], edge_values[i][b]))
    attended = attended.astype(BF16)
    grad = stacked(lambda i: grads[i].astype(F32))
    row_dot = jnp.sum(grad * attended.astype(F32), axis=1, keepdims=True)
    sgrad = (weight * (wgrad - row_dot) * SCALE).astype(BF16)
    edge_sgrad = (edge_weight * (edge_wgrad - row_dot) * SCALE).astype(BF16)
    stat = jnp.concatenate([factor, row_dot], axis=1)
    for i in range(SOME):
        at, here = rows_of(i), columns_of(i)
        attended_ref[:, here] = attended[at]
        factor_ref[i] = stat[at]
        edge_part = both(lambda b: nn(edge_sgrad[half_rows(i, b)], edge_keys[i][b]))
        query_part_ref[i] = nn(sgrad[at], keys[i]) + edge_part
        for side, left, edge_left, right in (
            (0, sgrad, edge_sgrad, queries[i]),
            (1, low, edge_low, grads[i]),
        ):
            terms = tn(left[at], right).astype(BF16)
            terms_ref[i, 0, side] = terms[:BLOCK]
            terms_ref[i, 1, side] = terms[BLOCK:]
            edge_terms = tn(edge_left[at], split(right))[:BLOCK].astype(BF16)
            prev_terms_ref[side, :, here] = edge_terms[:, :DH]
            next_terms_ref[side, :, here] = edge_terms[:, DH:]


def ends(where, query, grad, part, stat, blocks, prev, following):
    own = (HEADS, TOKENS_HERE, DH)
    edge = struct((2, BLOCK, HEADS * DH), BF16)
    pair_spec = pl.BlockSpec((SOME, 2, 2, BLOCK, DH), lambda i, where: (i, 0, 0, 0, 0))
    heads_specs = [head_spec(DH, step_of), head_spec(2, step_of)]
    return grid_call(
        ends_kernel,
        "ends",
        6 * 10**8,
        10 * 2**20,
        1,
        [flat_spec(step_of)] * 2 + heads_specs + [pair_spec] + [edge_spec(step_of)] * 2,
        [flat_spec(step_of)] + heads_specs + [pair_spec] + [edge_spec(step_of)] * 2,
        [
            struct((TOKENS_HERE, HEADS * DH), BF16),
            struct(own),
            struct(own[:2] + (2,)),
            struct((HEADS, 2, 2, BLOCK, DH), BF16),
            edge,
            edge,
        ],
    )(where, query, grad, part, stat, blocks, prev, following)


def far_terms_kernel(
    pick_ref,
    query_ref,
    grad_ref,
    exp_ref,
    wgrad_ref,
    factor_ref,
    terms_ref,
    made_ref,
    sem,
):
    step = pl.program_id(0)
    for i in range(SOME):
        head = step * SOME + i
        at = columns_of(i)
        weight = exp_ref[i] * factor_ref[i, :, 0:1]
        low = weight.astype(BF16)
        sgrad = (weight * (wgrad_ref[i] - factor_ref[i, :, 1:2]) * SCALE).astype(BF16)
        for side, left, right in ((0, sgrad, query_ref[:, at]), (1, low, grad_ref[:, at])):
            parts = tn(left[:, PICKED], split(right)).astype(BF16)
            for b in range(2):
                for r in range(3):
                    span = slice(r * BLOCK, (r + 1) * BLOCK)
                    made_ref[head, b * 3 + r, side] = parts[span, columns_of(b)]
        for b in range(2):
            for r in range(3):
                pltpu.make_async_copy(
                    made_ref.at[head, b * 3 + r],
                    terms_ref.at[owner_of(pick_ref, head, b, r)],
                    sem.at[0],
                ).start()

    @pl.when(step == STEPS - 1)
    def _():
        pltpu.make_async_copy(made_ref, made_ref, sem.at[0]).wait()


def far_terms(picks, query, grad, exps, wgrads, factor):
    return grid_call(
        far_terms_kernel,
        "far_terms",
        4 * 10**8,
        14 * 2**20,
        1,
        [flat_spec(step_of)] * 2 + [head_spec(w, step_of) for w in (2 * DH, 2 * DH, 2)],
        IN_HBM,
        struct((SHARDS, 2, BLOCK, DH), BF16),
        [pltpu.VMEM((HEADS, 6, 2, BLOCK, DH), BF16), pltpu.SemaphoreType.DMA((1,))],
    )(picks, query, grad, exps, wgrads, factor)


def own_terms_kernel(
    pick_ref,
    query_ref,
    grad_ref,
    key_ref,
    far_ref,
    own_exp_ref,
    far_exp_ref,
    own_wgrad_ref,
    far_wgrad_ref,
    query_part_ref,
    factor_ref,
    query_grad_ref,
    own_ref,
    held_ref,
    sem,
):
    step = pl.program_id(0)

    @pl.when(step == 0)
    def _():
        fetch(pick_ref, far_ref, held_ref, sem)

    for i in range(SOME):
        head = step * SOME + i
        at = columns_of(i)
        fetched(held_ref, sem, head)
        factor, row_dot = factor_ref[i, :, 0:1], factor_ref[i, :, 1:2]
        weight = own_exp_ref[i] * factor
        sgrad = (weight * (own_wgrad_ref[i] - row_dot) * SCALE).astype(BF16)
        far_sgrad = far_exp_ref[i] * factor * (far_wgrad_ref[i] - row_dot) * SCALE
        far_sgrad = far_sgrad.astype(BF16)

        def far_key(b):
            return jnp.concatenate([held_ref[head, b * 3 + r] for r in range(3)])

        query_grad = query_part_ref[i] + nn(sgrad, key_ref[:, at])
        query_grad = query_grad + both(lambda b: nn(far_sgrad[HALVES[b], PICKED], far_key(b)))
        query_grad_ref[:, at] = query_grad.astype(BF16)
        own_ref[0, :, at] = tn(sgrad, query_ref[:, at])
        own_ref[1, :, at] = tn(weight.astype(BF16), grad_ref[:, at])


def own_terms(picks, query, grad, key, far, exps, wgrads, query_part, factor):
    return grid_call(
        own_terms_kernel,
        "own_terms",
        5 * 10**8,
        16 * 2**20,
        1,
        [flat_spec(step_of)] * 3
        + [IN_HBM]
        + [head_spec(w, step_of) for w in (DH, 2 * DH, DH, 2 * DH, DH, 2)],
        [
            flat_spec(step_of),
            pl.BlockSpec((2, TOKENS_HERE, SOME * DH), lambda i, picks: (0, 0, i)),
        ],
        [
            struct((TOKENS_HERE, HEADS * DH), BF16),
            struct((2, TOKENS_HERE, HEADS * DH)),
        ],
        [pltpu.VMEM((HEADS, 6, BLOCK, DH), BF16), pltpu.SemaphoreType.DMA((HEADS,))],
    )(picks, query, grad, key, far, *exps, *wgrads, query_part, factor)


def gather_kernel(
    order_ref, begin_ref, terms_ref, own_ref, low_ref, high_ref, key_ref, value_ref
):
    edges = (low_ref, high_ref)

    def one_side(out_ref):
        for block in range(2):
            for head in range(HEADS):
                item = block * HEADS + head
                at = columns_of(head)

                def add(place, total):
                    return total + terms_ref[order_ref[place], 0].astype(F32)

                total = own_ref[0, HALVES[block], at] + edges[block][0, :, at].astype(F32)
                total = lax.fori_loop(begin_ref[item], begin_ref[item + 1], add, total)
                out_ref[HALVES[block], at] = total.astype(BF16)

    for side, out_ref in enumerate((key_ref, value_ref)):
        pl.when(pl.program_id(0) == side)(lambda out_ref=out_ref: one_side(out_ref))


def gather(order, begins, terms, own, low, high):
    flat = struct((TOKENS_HERE, HEADS * DH), BF16)
    flat_whole = pl.BlockSpec(flat.shape, lambda side, *scalars: (0, 0))

    def side_spec(rows_there):
        return pl.BlockSpec(
            (1, rows_there, HEADS * DH), lambda side, *scalars: (side, 0, 0)
        )

    return pl.pallas_call(
        gather_kernel,
        grid_spec=pltpu.PrefetchScalarGridSpec(
            num_scalar_prefetch=2,
            grid=(2,),
            in_specs=[
                pl.BlockSpec((SHARDS, 1, BLOCK, DH), lambda side, *scalars: (0, side, 0, 0)),
                side_spec(TOKENS_HERE),
                side_spec(BLOCK),
                side_spec(BLOCK),
            ],
            out_specs=[flat_whole, flat_whole],
        ),
        out_shape=[flat, flat],
        compiler_params=params(),
        cost_estimate=cost(10**6, 9 * 2**20),
        name="gather",
    )(order, begins, terms, own, low, high)


def send(value, route):
    return lax.ppermute(value, "seq", route)


def repeat_kernel(far_ref, out_ref, sem):
    for cell in range(HEADS):
        for end, source in enumerate((0, LAST)):
            pltpu.make_async_copy(far_ref.at[source], out_ref.at[cell, end], sem.at[0]).start()
    pltpu.make_async_copy(out_ref, out_ref, sem.at[0]).wait()


def repeat_ends(far):
    return pl.pallas_call(
        repeat_kernel,
        in_specs=[IN_HBM],
        out_specs=IN_HBM,
        out_shape=struct((HEADS, 2, 2, BLOCK, DH), BF16),
        scratch_shapes=[pltpu.SemaphoreType.DMA((1,))],
        compiler_params=params(),
        cost_estimate=cost(0, 2 * 2**20),
        name="repeat_ends",
    )(far)


def swap_in_plane(pieces):
    planes = [[cell * NZ + z for cell in range(NX * NY)] for z in range(NZ)]
    return lax.all_to_all(
        pieces, "seq", split_axis=0, concat_axis=0, tiled=True, axis_index_groups=planes
    )


def on_device(queries, key_states, values, out_grad, rand_blocks):
    shard = lax.axis_index("seq")
    where = shard.astype(jnp.int32).reshape(1)
    wanted = rand_blocks // 2 == shard
    item = rand_blocks % 2 * HEADS + lax.broadcasted_iota(jnp.int32, rand_blocks.shape, 1)
    items = jnp.max(jnp.where(wanted, item, -1), axis=(1, 2))
    items = jnp.max(items.reshape(SHARDS, 2), axis=1)
    cell = jnp.arange(SHARDS, dtype=jnp.int32) // NZ
    items = jnp.where(shard == 0, cell, jnp.where(shard == LAST, HEADS + cell, items))
    picks = lax.dynamic_slice_in_dim(rand_blocks, 2 * shard, 2, 0).reshape(2 * PICKS)

    named = jnp.where(items < 0, 2 * HEADS, items)
    place = jnp.arange(SHARDS, dtype=jnp.int32)
    before = (named[None, :] < named[:, None]) | (
        (named[None, :] == named[:, None]) & (place[None, :] < place[:, None])
    )
    rank = jnp.sum(before.astype(jnp.int32), axis=1)
    order = jnp.sum(jnp.where(rank[None, :] == place[:, None], place[None, :], 0), axis=1)
    kinds = jnp.arange(2 * HEADS + 1, dtype=jnp.int32)
    begins = jnp.sum((named[None, :] < kinds[:, None]).astype(jnp.int32), axis=1)

    low = jnp.stack([key_states[:BLOCK], values[:BLOCK]])
    high = jnp.stack([key_states[BLOCK:], values[BLOCK:]])
    up, down = [(i, i + 1) for i in range(LAST)], [(i + 1, i) for i in range(LAST)]
    slots = pack(jnp.maximum(items, 0), key_states, values)
    far = lax.all_to_all(slots, "seq", split_axis=0, concat_axis=0, tiled=True)
    far, low, high, picks, where = lax.optimization_barrier((far, low, high, picks, where))
    blocks = swap_in_plane(repeat_ends(far))
    prev, following = send(high, up), send(low, down)
    own_exps, far_exps, own_wgrads, far_wgrads, part, stat = near(
        picks, queries, out_grad, key_states, values, far
    )
    attended, query_part, factor, end_terms, prev_terms, next_terms = ends(
        where, queries, out_grad, part, stat, blocks, prev, following
    )
    end_terms = swap_in_plane(end_terms)
    from_next, from_prev = send(prev_terms, down), send(next_terms, up)
    terms = far_terms(picks, queries, out_grad, far_exps, far_wgrads, factor)
    terms, from_next, from_prev = lax.optimization_barrier((terms, from_next, from_prev))
    end_pair = jnp.sum(end_terms.astype(F32), axis=0).astype(BF16)
    terms = terms.at[0].set(end_pair[0]).at[LAST].set(end_pair[1])
    back = lax.all_to_all(terms, "seq", split_axis=0, concat_axis=0, tiled=True)
    query_grad, own = own_terms(
        picks, queries, out_grad, key_states, far,
        (own_exps, far_exps), (own_wgrads, far_wgrads), query_part, factor,
    )
    key_grad, value_grad = gather(order, begins, back, own, from_prev, from_next)
    return (attended, query_grad, key_grad, value_grad)


def solution(mesh):
    placed = P("seq", "head")
    return jax.shard_map(
        on_device,
        mesh=mesh,
        in_specs=(placed, placed, placed, placed, P(None, "head", None)),
        out_specs=(placed, placed, placed, placed),
        check_vma=False,
    )
```

```python
import math

import jax
import jax.numpy as jnp
from jax import lax
from jax.experimental import pallas as pl
from jax.experimental.pallas import tpu as pltpu
from jax.sharding import PartitionSpec as P

DH = 128
BLOCK = 64
HEADS = 16
SHARDS = 128
LAST = SHARDS - 1
PICKS = 3 * HEADS
NX, NY, NZ = 4, 4, 8
VMEM_BYTES = 60 * 2**20
MASKED = -1e30
SCALE = 1.0 / math.sqrt(DH)
EXP2_SCALE = SCALE * math.log2(math.e)
BF16 = jnp.bfloat16
F32 = jnp.float32

IN_VMEM = pl.BlockSpec(memory_space=pltpu.VMEM)
IN_SMEM = pl.BlockSpec(memory_space=pltpu.SMEM)
IN_HBM = pl.BlockSpec(memory_space=pltpu.HBM)


def params():
    return pltpu.CompilerParams(vmem_limit_bytes=VMEM_BYTES)


def cost(flops, moved, exps=0):
    return pl.CostEstimate(flops=flops, bytes_accessed=moved, transcendentals=exps)


def lanes(head):
    return pl.ds(pl.multiple_of(head * DH, DH), DH)


def rows(block):
    return pl.ds(pl.multiple_of(block * BLOCK, BLOCK), BLOCK)


def nt(a, b):
    return lax.dot_general(a, b, (((1,), (1,)), ((), ())), preferred_element_type=F32)


def nn(a, b):
    return lax.dot_general(a, b, (((1,), (0,)), ((), ())), preferred_element_type=F32)


def tn(a, b):
    return lax.dot_general(a, b, (((0,), (0,)), ((), ())), preferred_element_type=F32)


def pack_kernel(item_ref, key_ref, value_ref, slots_ref, sem):
    def moves(slot):
        item = item_ref[slot]
        block, head = item >> 4, item & 15
        return [
            pltpu.make_async_copy(
                ref.at[rows(block), lanes(head)], slots_ref.at[slot, side], sem.at[side]
            )
            for side, ref in enumerate((key_ref, value_ref))
        ]

    def start(slot, carry):
        for move in moves(slot):
            move.start()
        return carry

    lax.fori_loop(0, SHARDS, start, 0, unroll=8)
    for side in range(2):
        whole = slots_ref.at[:, side]
        pltpu.make_async_copy(whole, whole, sem.at[side]).wait()


def pack(items, key_states, values):
    return pl.pallas_call(
        pack_kernel,
        in_specs=[IN_SMEM, IN_VMEM, IN_VMEM],
        out_specs=pl.BlockSpec(memory_space=pl.ANY),
        out_shape=jax.ShapeDtypeStruct((SHARDS, 2, BLOCK, DH), BF16),
        scratch_shapes=[pltpu.SemaphoreType.DMA((2,))],
        compiler_params=params(),
        cost_estimate=cost(0, 6 * 2**20),
        name="pack",
    )(items, key_states, values)


HALVES = (slice(0, BLOCK), slice(BLOCK, 2 * BLOCK))
TOKENS_HERE = 2 * BLOCK
SOME = 4
STEPS = HEADS // SOME


def struct(shape, dtype=F32):
    return jax.ShapeDtypeStruct(shape, dtype)


def flat_spec(where_to):
    return pl.BlockSpec((TOKENS_HERE, SOME * DH), lambda *at: (0, where_to(*at)))


def edge_spec(where_to):
    return pl.BlockSpec((2, BLOCK, SOME * DH), lambda *at: (0, 0, where_to(*at)))


def head_spec(width, where_to):
    return pl.BlockSpec((SOME, TOKENS_HERE, width), lambda *at: (where_to(*at), 0, 0))


def grid_call(kernel, name, flops, moved, prefetch, in_specs, out_specs, out_shape, scratch=()):
    return pl.pallas_call(
        kernel,
        grid_spec=pltpu.PrefetchScalarGridSpec(
            num_scalar_prefetch=prefetch,
            grid=(STEPS,),
            in_specs=in_specs,
            out_specs=out_specs,
            scratch_shapes=scratch,
        ),
        out_shape=out_shape,
        compiler_params=params(),
        cost_estimate=cost(flops, moved, 10**6),
        name=name,
    )


def step_of(i, *scalars):
    return i


def columns_of(i):
    return slice(i * DH, (i + 1) * DH)


def both(of):
    return jnp.concatenate([of(0), of(1)])


def stacked(of):
    return jnp.concatenate([of(i) for i in range(SOME)])


def rows_of(i):
    return slice(i * TOKENS_HERE, (i + 1) * TOKENS_HERE)


def half_rows(i, b):
    return slice((2 * i + b) * BLOCK, (2 * i + b + 1) * BLOCK)


def owner_of(pick_ref, head, b, r):
    return pick_ref[b * PICKS + head * 3 + r] >> 1


def fetch(pick_ref, far_ref, held_ref, sem):
    def one(head, carry):
        for b in range(2):
            for r in range(3):
                source = far_ref.at[owner_of(pick_ref, head, b, r)]
                if len(held_ref.shape) == 4:
                    source = source.at[0]
                target = held_ref.at[head, b * 3 + r]
                pltpu.make_async_copy(source, target, sem.at[head]).start()
        return carry

    lax.fori_loop(0, HEADS, one, 0, unroll=4)


def fetched(held_ref, sem, head):
    pltpu.make_async_copy(held_ref.at[head], held_ref.at[head], sem.at[head]).wait()


def near_kernel(
    pick_ref,
    where_ref,
    query_ref,
    grad_ref,
    key_ref,
    value_ref,
    far_ref,
    prev_ref,
    next_ref,
    own_exp_ref,
    far_exp_ref,
    own_wgrad_ref,
    far_wgrad_ref,
    part_ref,
    stat_ref,
    held_ref,
    sem,
):
    step = pl.program_id(0)

    @pl.when(step == 0)
    def _():
        fetch(pick_ref, far_ref, held_ref, sem)

    shard = where_ref[0]
    column = lax.broadcasted_iota(jnp.int32, (1, 4 * BLOCK), 1)
    bias = [
        jnp.where((shard == end) & (column < BLOCK), MASKED, 0.0) for end in (0, LAST)
    ]
    edges = (prev_ref, next_ref)
    heads = [step * SOME + i for i in range(SOME)]
    queries = [query_ref[:, columns_of(i)] for i in range(SOME)]
    grads = [grad_ref[:, columns_of(i)] for i in range(SOME)]
    for head in heads:
        fetched(held_ref, sem, head)

    def picked(i, b, side):
        edge = edges[b][side, :, columns_of(i)]
        return jnp.concatenate([edge] + [held_ref[heads[i], b * 3 + r, side] for r in range(3)])

    keys, values = (
        [[picked(i, b, side) for b in range(2)] for i in range(SOME)] for side in range(2)
    )
    own_score = stacked(lambda i: nt(queries[i], key_ref[:, columns_of(i)]))
    far_score = stacked(lambda i: both(lambda b: nt(queries[i][HALVES[b]], keys[i][b]) + bias[b]))
    top = jnp.maximum(
        jnp.maximum(own_score, far_score[:, :TOKENS_HERE]), far_score[:, TOKENS_HERE:]
    )
    top = jnp.max(top, axis=1, keepdims=True)
    own_exp = jnp.exp2((own_score - top) * EXP2_SCALE)
    far_exp = jnp.exp2((far_score - top) * EXP2_SCALE)
    total = own_exp + far_exp[:, :TOKENS_HERE] + far_exp[:, TOKENS_HERE:]
    stat = jnp.concatenate([top, jnp.sum(total, axis=1, keepdims=True)], axis=1)
    own_low, far_low = own_exp.astype(BF16), far_exp.astype(BF16)
    for i in range(SOME):
        at = rows_of(i)
        own_exp_ref[i], far_exp_ref[i], stat_ref[i] = own_exp[at], far_exp[at], stat[at]
        own_wgrad_ref[i] = nt(grads[i], value_ref[:, columns_of(i)])
        far_part = both(lambda b: nn(far_low[half_rows(i, b)], values[i][b]))
        part_ref[i] = nn(own_low[at], value_ref[:, columns_of(i)]) + far_part
        for b in range(2):
            far_wgrad_ref[i, HALVES[b]] = nt(grads[i][HALVES[b]], values[i][b])


def near(picks, where, query, grad, key, value, far, prev, following):
    own, wide = (HEADS, TOKENS_HERE, TOKENS_HERE), (HEADS, TOKENS_HERE, 4 * BLOCK)
    return grid_call(
        near_kernel,
        "near",
        6 * 10**8,
        16 * 2**20,
        2,
        [flat_spec(step_of)] * 4 + [IN_HBM] + [edge_spec(step_of)] * 2,
        [head_spec(w, step_of) for w in (DH, 2 * DH, DH, 2 * DH, DH, 2)],
        [struct(own), struct(wide), struct(own), struct(wide), struct(own), struct(own[:2] + (2,))],
        [pltpu.VMEM((HEADS, 6, 2, BLOCK, DH), BF16), pltpu.SemaphoreType.DMA((HEADS,))],
    )(picks, where, query, grad, key, value, far, prev, following)


def ends_kernel(
    where_ref,
    query_ref,
    grad_ref,
    part_ref,
    stat_ref,
    ends_ref,
    attended_ref,
    query_part_ref,
    factor_ref,
    terms_ref,
):
    shard = where_ref[0]
    column = lax.broadcasted_iota(jnp.int32, (1, TOKENS_HERE), 1)
    no_end = ((shard == 0) & (column < BLOCK)) | ((shard == LAST) & (column >= BLOCK))
    bias = jnp.where(no_end, MASKED, 0.0)
    queries = [query_ref[:, columns_of(i)] for i in range(SOME)]
    grads = [grad_ref[:, columns_of(i)] for i in range(SOME)]
    keys, values = (
        [jnp.concatenate([ends_ref[i, 0, side], ends_ref[i, 1, side]]) for i in range(SOME)]
        for side in range(2)
    )
    score = stacked(lambda i: nt(queries[i], keys[i])) + bias
    stat = stacked(lambda i: stat_ref[i])
    old_top = stat[:, 0:1]
    top = jnp.maximum(old_top, jnp.max(score, axis=1, keepdims=True))
    exps = jnp.exp2((score - top) * EXP2_SCALE)
    shrink = jnp.exp2((old_top - top) * EXP2_SCALE)
    total = stat[:, 1:2] * shrink
    inverse = 1.0 / (total + jnp.sum(exps, axis=1, keepdims=True))
    factor = shrink * inverse
    weight = exps * inverse
    low = weight.astype(BF16)
    wgrad = stacked(lambda i: nt(grads[i], values[i]))
    attended = stacked(lambda i: part_ref[i]) * factor
    attended = attended + stacked(lambda i: nn(low[rows_of(i)], values[i]))
    attended = attended.astype(BF16)
    grad = stacked(lambda i: grads[i].astype(F32))
    row_dot = jnp.sum(grad * attended.astype(F32), axis=1, keepdims=True)
    sgrad = (weight * (wgrad - row_dot) * SCALE).astype(BF16)
    stat = jnp.concatenate([factor, row_dot], axis=1)
    for i in range(SOME):
        at = rows_of(i)
        attended_ref[:, columns_of(i)] = attended[at]
        factor_ref[i] = stat[at]
        query_part_ref[i] = nn(sgrad[at], keys[i])
        for side, left, right in ((0, sgrad, queries[i]), (1, low, grads[i])):
            terms = tn(left[at], right).astype(BF16)
            terms_ref[i, 0, side] = terms[:BLOCK]
            terms_ref[i, 1, side] = terms[BLOCK:]


def ends(where, query, grad, part, stat, blocks):
    own = (HEADS, TOKENS_HERE, DH)
    pair_spec = pl.BlockSpec((SOME, 2, 2, BLOCK, DH), lambda i, where: (i, 0, 0, 0, 0))
    heads_specs = [head_spec(DH, step_of), head_spec(2, step_of)]
    return grid_call(
        ends_kernel,
        "ends",
        4 * 10**8,
        8 * 2**20,
        1,
        [flat_spec(step_of)] * 2 + heads_specs + [pair_spec],
        [flat_spec(step_of)] + heads_specs + [pair_spec],
        [
            struct((TOKENS_HERE, HEADS * DH), BF16),
            struct(own),
            struct(own[:2] + (2,)),
            struct((HEADS, 2, 2, BLOCK, DH), BF16),
        ],
    )(where, query, grad, part, stat, blocks)


def far_terms_kernel(
    pick_ref,
    query_ref,
    grad_ref,
    exp_ref,
    wgrad_ref,
    factor_ref,
    terms_ref,
    prev_terms_ref,
    next_terms_ref,
    made_ref,
    sem,
):
    step = pl.program_id(0)
    no_rows = jnp.zeros((BLOCK, DH), BF16)

    def split(block_rows):
        return jnp.concatenate(
            [
                jnp.concatenate([block_rows[HALVES[0]], no_rows], axis=1),
                jnp.concatenate([no_rows, block_rows[HALVES[1]]], axis=1),
            ]
        )

    for i in range(SOME):
        head = step * SOME + i
        at = columns_of(i)
        weight = exp_ref[i] * factor_ref[i, :, 0:1]
        low = weight.astype(BF16)
        sgrad = (weight * (wgrad_ref[i] - factor_ref[i, :, 1:2]) * SCALE).astype(BF16)
        for side, left, right in ((0, sgrad, query_ref[:, at]), (1, low, grad_ref[:, at])):
            parts = tn(left, split(right)).astype(BF16)
            for b, edge_ref in enumerate((prev_terms_ref, next_terms_ref)):
                part = parts[:, columns_of(b)]
                edge_ref[side, :, at] = part[:BLOCK]
                for r in range(3):
                    made_ref[head, b * 3 + r, side] = part[(r + 1) * BLOCK : (r + 2) * BLOCK]
        for b in range(2):
            for r in range(3):
                pltpu.make_async_copy(
                    made_ref.at[head, b * 3 + r],
                    terms_ref.at[owner_of(pick_ref, head, b, r)],
                    sem.at[0],
                ).start()

    @pl.when(step == STEPS - 1)
    def _():
        pltpu.make_async_copy(made_ref, made_ref, sem.at[0]).wait()


def far_terms(picks, query, grad, exps, wgrads, factor):
    edge = struct((2, BLOCK, HEADS * DH), BF16)
    return grid_call(
        far_terms_kernel,
        "far_terms",
        4 * 10**8,
        14 * 2**20,
        1,
        [flat_spec(step_of)] * 2 + [head_spec(w, step_of) for w in (2 * DH, 2 * DH, 2)],
        [IN_HBM, edge_spec(step_of), edge_spec(step_of)],
        [struct((SHARDS, 2, BLOCK, DH), BF16), edge, edge],
        [pltpu.VMEM((HEADS, 6, 2, BLOCK, DH), BF16), pltpu.SemaphoreType.DMA((1,))],
    )(picks, query, grad, exps, wgrads, factor)


def own_terms_kernel(
    pick_ref,
    query_ref,
    grad_ref,
    key_ref,
    far_ref,
    prev_ref,
    next_ref,
    own_exp_ref,
    far_exp_ref,
    own_wgrad_ref,
    far_wgrad_ref,
    query_part_ref,
    factor_ref,
    query_grad_ref,
    own_ref,
    held_ref,
    sem,
):
    step = pl.program_id(0)

    @pl.when(step == 0)
    def _():
        fetch(pick_ref, far_ref, held_ref, sem)

    edges = (prev_ref, next_ref)
    for i in range(SOME):
        head = step * SOME + i
        at = columns_of(i)
        fetched(held_ref, sem, head)
        factor, row_dot = factor_ref[i, :, 0:1], factor_ref[i, :, 1:2]
        weight = own_exp_ref[i] * factor
        sgrad = (weight * (own_wgrad_ref[i] - row_dot) * SCALE).astype(BF16)
        far_sgrad = far_exp_ref[i] * factor * (far_wgrad_ref[i] - row_dot) * SCALE
        far_sgrad = far_sgrad.astype(BF16)

        def far_key(b):
            picked = [held_ref[head, b * 3 + r] for r in range(3)]
            return jnp.concatenate([edges[b][0, :, at]] + picked)

        query_grad = query_part_ref[i] + nn(sgrad, key_ref[:, at])
        query_grad = query_grad + both(lambda b: nn(far_sgrad[HALVES[b]], far_key(b)))
        query_grad_ref[:, at] = query_grad.astype(BF16)
        own_ref[0, :, at] = tn(sgrad, query_ref[:, at])
        own_ref[1, :, at] = tn(weight.astype(BF16), grad_ref[:, at])


def own_terms(picks, query, grad, key, far, prev, following, exps, wgrads, query_part, factor):
    return grid_call(
        own_terms_kernel,
        "own_terms",
        5 * 10**8,
        16 * 2**20,
        1,
        [flat_spec(step_of)] * 3
        + [IN_HBM]
        + [edge_spec(step_of)] * 2
        + [head_spec(w, step_of) for w in (DH, 2 * DH, DH, 2 * DH, DH, 2)],
        [
            flat_spec(step_of),
            pl.BlockSpec((2, TOKENS_HERE, SOME * DH), lambda i, picks: (0, 0, i)),
        ],
        [
            struct((TOKENS_HERE, HEADS * DH), BF16),
            struct((2, TOKENS_HERE, HEADS * DH)),
        ],
        [pltpu.VMEM((HEADS, 6, BLOCK, DH), BF16), pltpu.SemaphoreType.DMA((HEADS,))],
    )(picks, query, grad, key, far, prev, following, *exps, *wgrads, query_part, factor)


def gather_kernel(
    order_ref, begin_ref, terms_ref, own_ref, low_ref, high_ref, key_ref, value_ref
):
    edges = (low_ref, high_ref)
    outs = (key_ref, value_ref)
    for block in range(2):
        for head in range(HEADS):
            item = block * HEADS + head
            at = slice(head * DH, (head + 1) * DH)

            def add(place, totals):
                slot = order_ref[place]
                return tuple(totals[side] + terms_ref[slot, side].astype(F32) for side in range(2))

            totals = tuple(
                own_ref[side, HALVES[block], at] + edges[block][side, :, at].astype(F32)
                for side in range(2)
            )
            totals = lax.fori_loop(begin_ref[item], begin_ref[item + 1], add, totals)
            for side in range(2):
                outs[side][HALVES[block], at] = totals[side].astype(BF16)


def gather(order, begins, terms, own, low, high):
    flat = struct((2 * BLOCK, HEADS * DH), BF16)
    return pl.pallas_call(
        gather_kernel,
        in_specs=[IN_SMEM, IN_SMEM] + [IN_VMEM] * 4,
        out_specs=[IN_VMEM] * 2,
        out_shape=[flat, flat],
        compiler_params=params(),
        cost_estimate=cost(10**6, 9 * 2**20),
        name="gather",
    )(order, begins, terms, own, low, high)


def send(value, route):
    return lax.ppermute(value, "seq", route)


def swap_in_plane(pieces):
    planes = [[cell * NZ + z for cell in range(NX * NY)] for z in range(NZ)]
    return lax.all_to_all(
        pieces, "seq", split_axis=0, concat_axis=0, tiled=True, axis_index_groups=planes
    )


def on_device(queries, key_states, values, out_grad, rand_blocks):
    shard = lax.axis_index("seq")
    where = shard.astype(jnp.int32).reshape(1)
    wanted = rand_blocks // 2 == shard
    item = rand_blocks % 2 * HEADS + lax.broadcasted_iota(jnp.int32, rand_blocks.shape, 1)
    items = jnp.max(jnp.where(wanted, item, -1), axis=(1, 2))
    items = jnp.max(items.reshape(SHARDS, 2), axis=1)
    cell = jnp.arange(SHARDS, dtype=jnp.int32) // NZ
    items = jnp.where(shard == 0, cell, jnp.where(shard == LAST, HEADS + cell, items))
    picks = lax.dynamic_slice_in_dim(rand_blocks, 2 * shard, 2, 0).reshape(2 * PICKS)

    named = jnp.where(items < 0, 2 * HEADS, items)
    place = jnp.arange(SHARDS, dtype=jnp.int32)
    before = (named[None, :] < named[:, None]) | (
        (named[None, :] == named[:, None]) & (place[None, :] < place[:, None])
    )
    rank = jnp.sum(before.astype(jnp.int32), axis=1)
    order = jnp.sum(jnp.where(rank[None, :] == place[:, None], place[None, :], 0), axis=1)
    kinds = jnp.arange(2 * HEADS + 1, dtype=jnp.int32)
    begins = jnp.sum((named[None, :] < kinds[:, None]).astype(jnp.int32), axis=1)

    low = jnp.stack([key_states[:BLOCK], values[:BLOCK]])
    high = jnp.stack([key_states[BLOCK:], values[BLOCK:]])
    up, down = [(i, i + 1) for i in range(LAST)], [(i + 1, i) for i in range(LAST)]
    slots = pack(jnp.maximum(items, 0), key_states, values)
    far = lax.all_to_all(slots, "seq", split_axis=0, concat_axis=0, tiled=True)
    prev, following = send(high, up), send(low, down)
    far, prev, following, picks, where = lax.optimization_barrier(
        (far, prev, following, picks, where)
    )
    pair = jnp.stack([far[0], far[LAST]])
    blocks = swap_in_plane(jnp.broadcast_to(pair[None], (HEADS,) + pair.shape))
    own_exps, far_exps, own_wgrads, far_wgrads, part, stat = near(
        picks, where, queries, out_grad, key_states, values, far, prev, following
    )
    attended, query_part, factor, end_terms = ends(where, queries, out_grad, part, stat, blocks)
    end_terms = swap_in_plane(end_terms)
    terms, prev_terms, next_terms = far_terms(
        picks, queries, out_grad, far_exps, far_wgrads, factor
    )
    end_pair = jnp.sum(end_terms.astype(F32), axis=0).astype(BF16)
    terms = terms.at[0].set(end_pair[0]).at[LAST].set(end_pair[1])
    back = lax.all_to_all(terms, "seq", split_axis=0, concat_axis=0, tiled=True)
    from_next, from_prev = send(prev_terms, down), send(next_terms, up)
    query_grad, own = own_terms(
        picks, queries, out_grad, key_states, far, prev, following,
        (own_exps, far_exps), (own_wgrads, far_wgrads), query_part, factor,
    )
    key_grad, value_grad = gather(order, begins, back, own, from_prev, from_next)
    return (attended, query_grad, key_grad, value_grad)


def solution(mesh):
    placed = P("seq", "head")
    return jax.shard_map(
        on_device,
        mesh=mesh,
        in_specs=(placed, placed, placed, placed, P(None, "head", None)),
        out_specs=(placed, placed, placed, placed),
        check_vma=False,
    )
```

```python
import math

import jax
import jax.numpy as jnp
from jax import lax
from jax.experimental import pallas as pl
from jax.experimental.pallas import tpu as pltpu
from jax.sharding import PartitionSpec as P

DH = 128
BLOCK = 64
HEADS = 16
SHARDS = 128
LAST = SHARDS - 1
PICKS = 3 * HEADS
NX, NY, NZ = 4, 4, 8
VMEM_BYTES = 60 * 2**20
MASKED = -1e30
SCALE = 1.0 / math.sqrt(DH)
EXP2_SCALE = SCALE * math.log2(math.e)
BF16 = jnp.bfloat16
F32 = jnp.float32

IN_VMEM = pl.BlockSpec(memory_space=pltpu.VMEM)
IN_SMEM = pl.BlockSpec(memory_space=pltpu.SMEM)
IN_HBM = pl.BlockSpec(memory_space=pltpu.HBM)


def params():
    return pltpu.CompilerParams(vmem_limit_bytes=VMEM_BYTES)


def cost(flops, moved, exps=0):
    return pl.CostEstimate(flops=flops, bytes_accessed=moved, transcendentals=exps)


def lanes(head):
    return pl.ds(pl.multiple_of(head * DH, DH), DH)


def rows(block):
    return pl.ds(pl.multiple_of(block * BLOCK, BLOCK), BLOCK)


def nt(a, b):
    return lax.dot_general(a, b, (((1,), (1,)), ((), ())), preferred_element_type=F32)


def nn(a, b):
    return lax.dot_general(a, b, (((1,), (0,)), ((), ())), preferred_element_type=F32)


def tn(a, b):
    return lax.dot_general(a, b, (((0,), (0,)), ((), ())), preferred_element_type=F32)


def pack_kernel(item_ref, key_ref, value_ref, slots_ref, sem):
    def moves(slot):
        item = item_ref[slot]
        block, head = item >> 4, item & 15
        return [
            pltpu.make_async_copy(
                ref.at[rows(block), lanes(head)], slots_ref.at[slot, side], sem.at[side]
            )
            for side, ref in enumerate((key_ref, value_ref))
        ]

    def start(slot, carry):
        for move in moves(slot):
            move.start()
        return carry

    lax.fori_loop(0, SHARDS, start, 0, unroll=8)
    for side in range(2):
        whole = slots_ref.at[:, side]
        pltpu.make_async_copy(whole, whole, sem.at[side]).wait()


def pack(items, key_states, values):
    return pl.pallas_call(
        pack_kernel,
        in_specs=[IN_SMEM, IN_VMEM, IN_VMEM],
        out_specs=pl.BlockSpec(memory_space=pl.ANY),
        out_shape=jax.ShapeDtypeStruct((SHARDS, 2, BLOCK, DH), BF16),
        scratch_shapes=[pltpu.SemaphoreType.DMA((2,))],
        compiler_params=params(),
        cost_estimate=cost(0, 6 * 2**20),
        name="pack",
    )(items, key_states, values)


HALVES = (slice(0, BLOCK), slice(BLOCK, 2 * BLOCK))
TOKENS_HERE = 2 * BLOCK
SOME = 4
STEPS = HEADS // SOME


def struct(shape, dtype=F32):
    return jax.ShapeDtypeStruct(shape, dtype)


def flat_spec(where_to):
    return pl.BlockSpec((TOKENS_HERE, SOME * DH), lambda *at: (0, where_to(*at)))


def edge_spec(where_to):
    return pl.BlockSpec((2, BLOCK, SOME * DH), lambda *at: (0, 0, where_to(*at)))


def head_spec(width, where_to):
    return pl.BlockSpec((SOME, TOKENS_HERE, width), lambda *at: (where_to(*at), 0, 0))


def grid_call(kernel, name, flops, moved, prefetch, in_specs, out_specs, out_shape, scratch=()):
    return pl.pallas_call(
        kernel,
        grid_spec=pltpu.PrefetchScalarGridSpec(
            num_scalar_prefetch=prefetch,
            grid=(STEPS,),
            in_specs=in_specs,
            out_specs=out_specs,
            scratch_shapes=scratch,
        ),
        out_shape=out_shape,
        compiler_params=params(),
        cost_estimate=cost(flops, moved, 10**6),
        name=name,
    )


def step_of(i, *scalars):
    return i


def columns_of(i):
    return slice(i * DH, (i + 1) * DH)


def both(of):
    return jnp.concatenate([of(0), of(1)])


def stacked(of):
    return jnp.concatenate([of(i) for i in range(SOME)])


def rows_of(i):
    return slice(i * TOKENS_HERE, (i + 1) * TOKENS_HERE)


def half_rows(i, b):
    return slice((2 * i + b) * BLOCK, (2 * i + b + 1) * BLOCK)


def owner_of(pick_ref, head, b, r):
    return pick_ref[b * PICKS + head * 3 + r] >> 1


def fetch(pick_ref, far_ref, held_ref, sem):
    def one(head, carry):
        for b in range(2):
            for r in range(3):
                source = far_ref.at[owner_of(pick_ref, head, b, r)]
                if len(held_ref.shape) == 4:
                    source = source.at[0]
                target = held_ref.at[head, b * 3 + r]
                pltpu.make_async_copy(source, target, sem.at[head]).start()
        return carry

    lax.fori_loop(0, HEADS, one, 0, unroll=4)


def fetched(held_ref, sem, head):
    pltpu.make_async_copy(held_ref.at[head], held_ref.at[head], sem.at[head]).wait()


def near_kernel(
    pick_ref,
    where_ref,
    query_ref,
    grad_ref,
    key_ref,
    value_ref,
    far_ref,
    prev_ref,
    next_ref,
    own_exp_ref,
    far_exp_ref,
    own_wgrad_ref,
    far_wgrad_ref,
    part_ref,
    stat_ref,
    held_ref,
    sem,
):
    step = pl.program_id(0)

    @pl.when(step == 0)
    def _():
        fetch(pick_ref, far_ref, held_ref, sem)

    shard = where_ref[0]
    column = lax.broadcasted_iota(jnp.int32, (1, 4 * BLOCK), 1)
    bias = [
        jnp.where((shard == end) & (column < BLOCK), MASKED, 0.0) for end in (0, LAST)
    ]
    edges = (prev_ref, next_ref)
    heads = [step * SOME + i for i in range(SOME)]
    queries = [query_ref[:, columns_of(i)] for i in range(SOME)]
    grads = [grad_ref[:, columns_of(i)] for i in range(SOME)]
    for head in heads:
        fetched(held_ref, sem, head)

    def picked(i, b, side):
        edge = edges[b][side, :, columns_of(i)]
        return jnp.concatenate([edge] + [held_ref[heads[i], b * 3 + r, side] for r in range(3)])

    keys, values = (
        [[picked(i, b, side) for b in range(2)] for i in range(SOME)] for side in range(2)
    )
    own_score = stacked(lambda i: nt(queries[i], key_ref[:, columns_of(i)]))
    far_score = stacked(lambda i: both(lambda b: nt(queries[i][HALVES[b]], keys[i][b]) + bias[b]))
    top = jnp.maximum(
        jnp.maximum(own_score, far_score[:, :TOKENS_HERE]), far_score[:, TOKENS_HERE:]
    )
    top = jnp.max(top, axis=1, keepdims=True)
    own_exp = jnp.exp2((own_score - top) * EXP2_SCALE)
    far_exp = jnp.exp2((far_score - top) * EXP2_SCALE)
    total = own_exp + far_exp[:, :TOKENS_HERE] + far_exp[:, TOKENS_HERE:]
    stat = jnp.concatenate([top, jnp.sum(total, axis=1, keepdims=True)], axis=1)
    own_low, far_low = own_exp.astype(BF16), far_exp.astype(BF16)
    for i in range(SOME):
        at = rows_of(i)
        own_exp_ref[i], far_exp_ref[i], stat_ref[i] = own_exp[at], far_exp[at], stat[at]
        own_wgrad_ref[i] = nt(grads[i], value_ref[:, columns_of(i)])
        far_part = both(lambda b: nn(far_low[half_rows(i, b)], values[i][b]))
        part_ref[i] = nn(own_low[at], value_ref[:, columns_of(i)]) + far_part
        for b in range(2):
            far_wgrad_ref[i, HALVES[b]] = nt(grads[i][HALVES[b]], values[i][b])


def near(picks, where, query, grad, key, value, far, prev, following):
    own, wide = (HEADS, TOKENS_HERE, TOKENS_HERE), (HEADS, TOKENS_HERE, 4 * BLOCK)
    return grid_call(
        near_kernel,
        "near",
        6 * 10**8,
        16 * 2**20,
        2,
        [flat_spec(step_of)] * 4 + [IN_HBM] + [edge_spec(step_of)] * 2,
        [head_spec(w, step_of) for w in (DH, 2 * DH, DH, 2 * DH, DH, 2)],
        [struct(own), struct(wide), struct(own), struct(wide), struct(own), struct(own[:2] + (2,))],
        [pltpu.VMEM((HEADS, 6, 2, BLOCK, DH), BF16), pltpu.SemaphoreType.DMA((HEADS,))],
    )(picks, where, query, grad, key, value, far, prev, following)


def ends_kernel(
    where_ref,
    query_ref,
    grad_ref,
    part_ref,
    stat_ref,
    ends_ref,
    attended_ref,
    sgrad_ref,
    factor_ref,
    terms_ref,
):
    shard = where_ref[0]
    column = lax.broadcasted_iota(jnp.int32, (1, TOKENS_HERE), 1)
    no_end = ((shard == 0) & (column < BLOCK)) | ((shard == LAST) & (column >= BLOCK))
    bias = jnp.where(no_end, MASKED, 0.0)
    queries = [query_ref[:, columns_of(i)] for i in range(SOME)]
    grads = [grad_ref[:, columns_of(i)] for i in range(SOME)]
    keys, values = (
        [jnp.concatenate([ends_ref[i, 0, side], ends_ref[i, 1, side]]) for i in range(SOME)]
        for side in range(2)
    )
    score = stacked(lambda i: nt(queries[i], keys[i])) + bias
    stat = stacked(lambda i: stat_ref[i])
    old_top = stat[:, 0:1]
    top = jnp.maximum(old_top, jnp.max(score, axis=1, keepdims=True))
    exps = jnp.exp2((score - top) * EXP2_SCALE)
    shrink = jnp.exp2((old_top - top) * EXP2_SCALE)
    total = stat[:, 1:2] * shrink
    inverse = 1.0 / (total + jnp.sum(exps, axis=1, keepdims=True))
    factor = shrink * inverse
    weight = exps * inverse
    low = weight.astype(BF16)
    wgrad = stacked(lambda i: nt(grads[i], values[i]))
    attended = stacked(lambda i: part_ref[i]) * factor
    attended = attended + stacked(lambda i: nn(low[rows_of(i)], values[i]))
    attended = attended.astype(BF16)
    grad = stacked(lambda i: grads[i].astype(F32))
    row_dot = jnp.sum(grad * attended.astype(F32), axis=1, keepdims=True)
    sgrad = (weight * (wgrad - row_dot) * SCALE).astype(BF16)
    stat = jnp.concatenate([factor, row_dot], axis=1)
    for i in range(SOME):
        at = rows_of(i)
        attended_ref[:, columns_of(i)] = attended[at]
        factor_ref[i] = stat[at]
        sgrad_ref[i] = sgrad[at]
        for side, left, right in ((0, sgrad, queries[i]), (1, low, grads[i])):
            terms = tn(left[at], right).astype(BF16)
            terms_ref[i, 0, side] = terms[:BLOCK]
            terms_ref[i, 1, side] = terms[BLOCK:]


def ends(where, query, grad, part, stat, blocks):
    own = (HEADS, TOKENS_HERE, DH)
    pair_spec = pl.BlockSpec((SOME, 2, 2, BLOCK, DH), lambda i, where: (i, 0, 0, 0, 0))
    heads_specs = [head_spec(DH, step_of), head_spec(2, step_of)]
    return grid_call(
        ends_kernel,
        "ends",
        4 * 10**8,
        8 * 2**20,
        1,
        [flat_spec(step_of)] * 2 + heads_specs + [pair_spec],
        [flat_spec(step_of)] + heads_specs + [pair_spec],
        [
            struct((TOKENS_HERE, HEADS * DH), BF16),
            struct(own, BF16),
            struct(own[:2] + (2,)),
            struct((HEADS, 2, 2, BLOCK, DH), BF16),
        ],
    )(where, query, grad, part, stat, blocks)


def far_terms_kernel(
    pick_ref,
    query_ref,
    grad_ref,
    exp_ref,
    wgrad_ref,
    factor_ref,
    terms_ref,
    prev_terms_ref,
    next_terms_ref,
    made_ref,
    sem,
):
    step = pl.program_id(0)
    no_rows = jnp.zeros((BLOCK, DH), BF16)

    def split(block_rows):
        return jnp.concatenate(
            [
                jnp.concatenate([block_rows[HALVES[0]], no_rows], axis=1),
                jnp.concatenate([no_rows, block_rows[HALVES[1]]], axis=1),
            ]
        )

    for i in range(SOME):
        head = step * SOME + i
        at = columns_of(i)
        weight = exp_ref[i] * factor_ref[i, :, 0:1]
        low = weight.astype(BF16)
        sgrad = (weight * (wgrad_ref[i] - factor_ref[i, :, 1:2]) * SCALE).astype(BF16)
        for side, left, right in ((0, sgrad, query_ref[:, at]), (1, low, grad_ref[:, at])):
            parts = tn(left, split(right)).astype(BF16)
            for b, edge_ref in enumerate((prev_terms_ref, next_terms_ref)):
                part = parts[:, columns_of(b)]
                edge_ref[side, :, at] = part[:BLOCK]
                for r in range(3):
                    made_ref[head, b * 3 + r, side] = part[(r + 1) * BLOCK : (r + 2) * BLOCK]
        for b in range(2):
            for r in range(3):
                pltpu.make_async_copy(
                    made_ref.at[head, b * 3 + r],
                    terms_ref.at[owner_of(pick_ref, head, b, r)],
                    sem.at[0],
                ).start()

    @pl.when(step == STEPS - 1)
    def _():
        pltpu.make_async_copy(made_ref, made_ref, sem.at[0]).wait()


def far_terms(picks, query, grad, exps, wgrads, factor):
    edge = struct((2, BLOCK, HEADS * DH), BF16)
    return grid_call(
        far_terms_kernel,
        "far_terms",
        4 * 10**8,
        14 * 2**20,
        1,
        [flat_spec(step_of)] * 2 + [head_spec(w, step_of) for w in (2 * DH, 2 * DH, 2)],
        [IN_HBM, edge_spec(step_of), edge_spec(step_of)],
        [struct((SHARDS, 2, BLOCK, DH), BF16), edge, edge],
        [pltpu.VMEM((HEADS, 6, 2, BLOCK, DH), BF16), pltpu.SemaphoreType.DMA((1,))],
    )(picks, query, grad, exps, wgrads, factor)


def own_terms_kernel(
    pick_ref,
    query_ref,
    grad_ref,
    key_ref,
    far_ref,
    prev_ref,
    next_ref,
    own_exp_ref,
    far_exp_ref,
    own_wgrad_ref,
    far_wgrad_ref,
    end_sgrad_ref,
    ends_ref,
    factor_ref,
    query_grad_ref,
    own_ref,
    held_ref,
    sem,
):
    step = pl.program_id(0)

    @pl.when(step == 0)
    def _():
        fetch(pick_ref, far_ref, held_ref, sem)

    edges = (prev_ref, next_ref)
    for i in range(SOME):
        head = step * SOME + i
        at = columns_of(i)
        fetched(held_ref, sem, head)
        factor, row_dot = factor_ref[i, :, 0:1], factor_ref[i, :, 1:2]
        weight = own_exp_ref[i] * factor
        sgrad = (weight * (own_wgrad_ref[i] - row_dot) * SCALE).astype(BF16)
        far_sgrad = far_exp_ref[i] * factor * (far_wgrad_ref[i] - row_dot) * SCALE
        far_sgrad = far_sgrad.astype(BF16)

        def far_key(b):
            picked = [held_ref[head, b * 3 + r] for r in range(3)]
            return jnp.concatenate([edges[b][0, :, at]] + picked)

        end_key = jnp.concatenate([ends_ref[i, 0, 0], ends_ref[i, 1, 0]])
        query_grad = nn(end_sgrad_ref[i], end_key) + nn(sgrad, key_ref[:, at])
        query_grad = query_grad + both(lambda b: nn(far_sgrad[HALVES[b]], far_key(b)))
        query_grad_ref[:, at] = query_grad.astype(BF16)
        own_ref[0, :, at] = tn(sgrad, query_ref[:, at])
        own_ref[1, :, at] = tn(weight.astype(BF16), grad_ref[:, at])


def own_terms(picks, query, grad, key, far, prev, following, exps, wgrads, end_sgrad, blocks, factor):
    return grid_call(
        own_terms_kernel,
        "own_terms",
        5 * 10**8,
        16 * 2**20,
        1,
        [flat_spec(step_of)] * 3
        + [IN_HBM]
        + [edge_spec(step_of)] * 2
        + [head_spec(w, step_of) for w in (DH, 2 * DH, DH, 2 * DH, DH)]
        + [pl.BlockSpec((SOME, 2, 2, BLOCK, DH), lambda i, picks: (i, 0, 0, 0, 0))]
        + [head_spec(2, step_of)],
        [
            flat_spec(step_of),
            pl.BlockSpec((2, TOKENS_HERE, SOME * DH), lambda i, picks: (0, 0, i)),
        ],
        [
            struct((TOKENS_HERE, HEADS * DH), BF16),
            struct((2, TOKENS_HERE, HEADS * DH)),
        ],
        [pltpu.VMEM((HEADS, 6, BLOCK, DH), BF16), pltpu.SemaphoreType.DMA((HEADS,))],
    )(picks, query, grad, key, far, prev, following, *exps, *wgrads, end_sgrad, blocks, factor)


USUAL = 4


def gather_kernel(
    order_ref, begin_ref, terms_ref, own_ref, low_ref, high_ref, key_ref, value_ref
):
    edges = (low_ref, high_ref)

    def one_side(out_ref):
        for block in range(2):
            for head in range(HEADS):
                item = block * HEADS + head
                at = columns_of(head)
                begin, end = begin_ref[item], begin_ref[item + 1]

                def term(place):
                    return terms_ref[order_ref[place], 0].astype(F32)

                total = own_ref[0, HALVES[block], at] + edges[block][0, :, at].astype(F32)
                for i in range(USUAL):
                    found = term(jnp.minimum(begin + i, SHARDS - 1))
                    total = total + jnp.where(begin + i < end, found, 0.0)
                total = lax.fori_loop(
                    jnp.minimum(begin + USUAL, end), end, lambda p, sums: sums + term(p), total
                )
                out_ref[HALVES[block], at] = total.astype(BF16)

    for side, out_ref in enumerate((key_ref, value_ref)):
        pl.when(pl.program_id(0) == side)(lambda out_ref=out_ref: one_side(out_ref))


def gather(order, begins, terms, own, low, high):
    flat = struct((TOKENS_HERE, HEADS * DH), BF16)
    flat_whole = pl.BlockSpec(flat.shape, lambda side, *scalars: (0, 0))

    def side_spec(rows_there):
        return pl.BlockSpec(
            (1, rows_there, HEADS * DH), lambda side, *scalars: (side, 0, 0)
        )

    return pl.pallas_call(
        gather_kernel,
        grid_spec=pltpu.PrefetchScalarGridSpec(
            num_scalar_prefetch=2,
            grid=(2,),
            in_specs=[
                pl.BlockSpec((SHARDS, 1, BLOCK, DH), lambda side, *scalars: (0, side, 0, 0)),
                side_spec(TOKENS_HERE),
                side_spec(BLOCK),
                side_spec(BLOCK),
            ],
            out_specs=[flat_whole, flat_whole],
        ),
        out_shape=[flat, flat],
        compiler_params=params(),
        cost_estimate=cost(10**6, 9 * 2**20),
        name="gather",
    )(order, begins, terms, own, low, high)


def send(value, route):
    return lax.ppermute(value, "seq", route)


def swap_in_plane(pieces):
    planes = [[cell * NZ + z for cell in range(NX * NY)] for z in range(NZ)]
    return lax.all_to_all(
        pieces, "seq", split_axis=0, concat_axis=0, tiled=True, axis_index_groups=planes
    )


def on_device(queries, key_states, values, out_grad, rand_blocks):
    shard = lax.axis_index("seq")
    where = shard.astype(jnp.int32).reshape(1)
    wanted = rand_blocks // 2 == shard
    item = rand_blocks % 2 * HEADS + lax.broadcasted_iota(jnp.int32, rand_blocks.shape, 1)
    items = jnp.max(jnp.where(wanted, item, -1), axis=(1, 2))
    items = jnp.max(items.reshape(SHARDS, 2), axis=1)
    cell = jnp.arange(SHARDS, dtype=jnp.int32) // NZ
    items = jnp.where(shard == 0, cell, jnp.where(shard == LAST, HEADS + cell, items))
    picks = lax.dynamic_slice_in_dim(rand_blocks, 2 * shard, 2, 0).reshape(2 * PICKS)

    named = jnp.where(items < 0, 2 * HEADS, items)
    place = jnp.arange(SHARDS, dtype=jnp.int32)
    before = (named[None, :] < named[:, None]) | (
        (named[None, :] == named[:, None]) & (place[None, :] < place[:, None])
    )
    rank = jnp.sum(before.astype(jnp.int32), axis=1)
    order = jnp.sum(jnp.where(rank[None, :] == place[:, None], place[None, :], 0), axis=1)
    kinds = jnp.arange(2 * HEADS + 1, dtype=jnp.int32)
    begins = jnp.sum((named[None, :] < kinds[:, None]).astype(jnp.int32), axis=1)

    low = jnp.stack([key_states[:BLOCK], values[:BLOCK]])
    high = jnp.stack([key_states[BLOCK:], values[BLOCK:]])
    up, down = [(i, i + 1) for i in range(LAST)], [(i + 1, i) for i in range(LAST)]
    slots = pack(jnp.maximum(items, 0), key_states, values)
    far = lax.all_to_all(slots, "seq", split_axis=0, concat_axis=0, tiled=True)
    prev, following = send(high, up), send(low, down)
    far, prev, following, picks, where = lax.optimization_barrier(
        (far, prev, following, picks, where)
    )
    pair = jnp.stack([far[0], far[LAST]])
    blocks = swap_in_plane(jnp.broadcast_to(pair[None], (HEADS,) + pair.shape))
    own_exps, far_exps, own_wgrads, far_wgrads, part, stat = near(
        picks, where, queries, out_grad, key_states, values, far, prev, following
    )
    attended, end_sgrad, factor, end_terms = ends(where, queries, out_grad, part, stat, blocks)
    end_terms = swap_in_plane(end_terms)
    terms, prev_terms, next_terms = far_terms(
        picks, queries, out_grad, far_exps, far_wgrads, factor
    )
    end_pair = jnp.sum(end_terms.astype(F32), axis=0).astype(BF16)
    terms = terms.at[0].set(end_pair[0]).at[LAST].set(end_pair[1])
    back = lax.all_to_all(terms, "seq", split_axis=0, concat_axis=0, tiled=True)
    from_next, from_prev = send(prev_terms, down), send(next_terms, up)
    query_grad, own = own_terms(
        picks, queries, out_grad, key_states, far, prev, following,
        (own_exps, far_exps), (own_wgrads, far_wgrads), end_sgrad, blocks, factor,
    )
    key_grad, value_grad = gather(order, begins, back, own, from_prev, from_next)
    return (attended, query_grad, key_grad, value_grad)


def solution(mesh):
    placed = P("seq", "head")
    return jax.shard_map(
        on_device,
        mesh=mesh,
        in_specs=(placed, placed, placed, placed, P(None, "head", None)),
        out_specs=(placed, placed, placed, placed),
        check_vma=False,
    )
```

```python
import math

import jax
import jax.numpy as jnp
from jax import lax
from jax.experimental import pallas as pl
from jax.experimental.pallas import tpu as pltpu
from jax.sharding import PartitionSpec as P

DH = 128
BLOCK = 64
HEADS = 16
SHARDS = 128
LAST = SHARDS - 1
PICKS = 3 * HEADS
NX, NY, NZ = 4, 4, 8
VMEM_BYTES = 60 * 2**20
MASKED = -1e30
SCALE = 1.0 / math.sqrt(DH)
EXP2_SCALE = SCALE * math.log2(math.e)
BF16 = jnp.bfloat16
F32 = jnp.float32

IN_VMEM = pl.BlockSpec(memory_space=pltpu.VMEM)
IN_SMEM = pl.BlockSpec(memory_space=pltpu.SMEM)
IN_HBM = pl.BlockSpec(memory_space=pltpu.HBM)


def params(vmem_bytes=VMEM_BYTES):
    return pltpu.CompilerParams(vmem_limit_bytes=vmem_bytes)


def cost(flops, moved, exps=0):
    return pl.CostEstimate(flops=flops, bytes_accessed=moved, transcendentals=exps)


def lanes(head):
    return pl.ds(pl.multiple_of(head * DH, DH), DH)


def rows(block):
    return pl.ds(pl.multiple_of(block * BLOCK, BLOCK), BLOCK)


def nt(a, b):
    return lax.dot_general(a, b, (((1,), (1,)), ((), ())), preferred_element_type=F32)


def nn(a, b):
    return lax.dot_general(a, b, (((1,), (0,)), ((), ())), preferred_element_type=F32)


def tn(a, b):
    return lax.dot_general(a, b, (((0,), (0,)), ((), ())), preferred_element_type=F32)


def pack_kernel(item_ref, key_ref, value_ref, slots_ref, sem):
    def moves(slot):
        item = item_ref[slot]
        block, head = item >> 4, item & 15
        return [
            pltpu.make_async_copy(
                ref.at[rows(block), lanes(head)], slots_ref.at[slot, side], sem.at[side]
            )
            for side, ref in enumerate((key_ref, value_ref))
        ]

    def start(slot, carry):
        for move in moves(slot):
            move.start()
        return carry

    lax.fori_loop(0, SHARDS, start, 0, unroll=8)
    for side in range(2):
        whole = slots_ref.at[:, side]
        pltpu.make_async_copy(whole, whole, sem.at[side]).wait()


def pack(items, key_states, values):
    return pl.pallas_call(
        pack_kernel,
        in_specs=[IN_SMEM, IN_VMEM, IN_VMEM],
        out_specs=pl.BlockSpec(memory_space=pl.ANY),
        out_shape=jax.ShapeDtypeStruct((SHARDS, 2, BLOCK, DH), BF16),
        scratch_shapes=[pltpu.SemaphoreType.DMA((2,))],
        compiler_params=params(),
        cost_estimate=cost(0, 6 * 2**20),
        name="pack",
    )(items, key_states, values)


HALVES = (slice(0, BLOCK), slice(BLOCK, 2 * BLOCK))
TOKENS_HERE = 2 * BLOCK
SOME = 4
STEPS = HEADS // SOME


def struct(shape, dtype=F32):
    return jax.ShapeDtypeStruct(shape, dtype)


def flat_spec(where_to):
    return pl.BlockSpec((TOKENS_HERE, SOME * DH), lambda *at: (0, where_to(*at)))


def edge_spec(where_to):
    return pl.BlockSpec((2, BLOCK, SOME * DH), lambda *at: (0, 0, where_to(*at)))


def head_spec(width, where_to):
    return pl.BlockSpec((SOME, TOKENS_HERE, width), lambda *at: (where_to(*at), 0, 0))


def stat_spec(where_to):
    return pl.BlockSpec((1, TOKENS_HERE, 2 * SOME), lambda *at: (where_to(*at), 0, 0))


STATS = (STEPS, TOKENS_HERE, 2 * SOME)


def side_by_side(stat):
    return jnp.concatenate([stat[rows_of(i)] for i in range(SOME)], axis=1)


def stat_of(stat_ref, i, which):
    return stat_ref[0, :, 2 * i + which : 2 * i + which + 1]


def grid_call(kernel, name, flops, moved, prefetch, in_specs, out_specs, out_shape, scratch=()):
    return pl.pallas_call(
        kernel,
        grid_spec=pltpu.PrefetchScalarGridSpec(
            num_scalar_prefetch=prefetch,
            grid=(STEPS,),
            in_specs=in_specs,
            out_specs=out_specs,
            scratch_shapes=scratch,
        ),
        out_shape=out_shape,
        compiler_params=params(),
        cost_estimate=cost(flops, moved, 10**6),
        name=name,
    )


def step_of(i, *scalars):
    return i


def columns_of(i):
    return slice(i * DH, (i + 1) * DH)


def both(of):
    return jnp.concatenate([of(0), of(1)])


def stacked(of):
    return jnp.concatenate([of(i) for i in range(SOME)])


def rows_of(i):
    return slice(i * TOKENS_HERE, (i + 1) * TOKENS_HERE)


def half_rows(i, b):
    return slice((2 * i + b) * BLOCK, (2 * i + b + 1) * BLOCK)


def owner_of(pick_ref, head, b, r):
    return pick_ref[b * PICKS + head * 3 + r] >> 1


def fetch(pick_ref, far_ref, held_ref, sem):
    def one(head, carry):
        for b in range(2):
            for r in range(3):
                source = far_ref.at[owner_of(pick_ref, head, b, r)]
                if len(held_ref.shape) == 4:
                    source = source.at[0]
                target = held_ref.at[head, b * 3 + r]
                pltpu.make_async_copy(source, target, sem.at[head]).start()
        return carry

    lax.fori_loop(0, HEADS, one, 0, unroll=4)


def fetched(held_ref, sem, head):
    pltpu.make_async_copy(held_ref.at[head], held_ref.at[head], sem.at[head]).wait()


def near_kernel(
    pick_ref,
    where_ref,
    query_ref,
    grad_ref,
    key_ref,
    value_ref,
    far_ref,
    prev_ref,
    next_ref,
    own_exp_ref,
    far_exp_ref,
    own_wgrad_ref,
    far_wgrad_ref,
    part_ref,
    stat_ref,
    held_ref,
    sem,
):
    step = pl.program_id(0)

    @pl.when(step == 0)
    def _():
        fetch(pick_ref, far_ref, held_ref, sem)

    shard = where_ref[0]
    column = lax.broadcasted_iota(jnp.int32, (1, 4 * BLOCK), 1)
    bias = [
        jnp.where((shard == end) & (column < BLOCK), MASKED, 0.0) for end in (0, LAST)
    ]
    edges = (prev_ref, next_ref)
    heads = [step * SOME + i for i in range(SOME)]
    queries = [query_ref[:, columns_of(i)] for i in range(SOME)]
    grads = [grad_ref[:, columns_of(i)] for i in range(SOME)]
    for head in heads:
        fetched(held_ref, sem, head)

    def picked(i, b, side):
        edge = edges[b][side, :, columns_of(i)]
        return jnp.concatenate([edge] + [held_ref[heads[i], b * 3 + r, side] for r in range(3)])

    keys, values = (
        [[picked(i, b, side) for b in range(2)] for i in range(SOME)] for side in range(2)
    )
    own_score = stacked(lambda i: nt(queries[i], key_ref[:, columns_of(i)]))
    far_score = stacked(lambda i: both(lambda b: nt(queries[i][HALVES[b]], keys[i][b]) + bias[b]))
    top = jnp.maximum(
        jnp.maximum(own_score, far_score[:, :TOKENS_HERE]), far_score[:, TOKENS_HERE:]
    )
    top = jnp.max(top, axis=1, keepdims=True)
    own_exp = jnp.exp2((own_score - top) * EXP2_SCALE)
    far_exp = jnp.exp2((far_score - top) * EXP2_SCALE)
    total = own_exp + far_exp[:, :TOKENS_HERE] + far_exp[:, TOKENS_HERE:]
    stat = jnp.concatenate([top, jnp.sum(total, axis=1, keepdims=True)], axis=1)
    stat_ref[0] = side_by_side(stat)
    own_low, far_low = own_exp.astype(BF16), far_exp.astype(BF16)
    for i in range(SOME):
        at = rows_of(i)
        own_exp_ref[i], far_exp_ref[i] = own_exp[at], far_exp[at]
        own_wgrad_ref[i] = nt(grads[i], value_ref[:, columns_of(i)])
        far_part = both(lambda b: nn(far_low[half_rows(i, b)], values[i][b]))
        part_ref[i] = nn(own_low[at], value_ref[:, columns_of(i)]) + far_part
        for b in range(2):
            far_wgrad_ref[i, HALVES[b]] = nt(grads[i][HALVES[b]], values[i][b])


def near(picks, where, query, grad, key, value, far, prev, following):
    own, wide = (HEADS, TOKENS_HERE, TOKENS_HERE), (HEADS, TOKENS_HERE, 4 * BLOCK)
    return grid_call(
        near_kernel,
        "near",
        6 * 10**8,
        16 * 2**20,
        2,
        [flat_spec(step_of)] * 4 + [IN_HBM] + [edge_spec(step_of)] * 2,
        [head_spec(w, step_of) for w in (DH, 2 * DH, DH, 2 * DH, DH)] + [stat_spec(step_of)],
        [struct(own), struct(wide), struct(own), struct(wide), struct(own), struct(STATS)],
        [pltpu.VMEM((HEADS, 6, 2, BLOCK, DH), BF16), pltpu.SemaphoreType.DMA((HEADS,))],
    )(picks, where, query, grad, key, value, far, prev, following)


def ends_kernel(
    where_ref,
    query_ref,
    grad_ref,
    part_ref,
    stat_ref,
    ends_ref,
    attended_ref,
    sgrad_ref,
    factor_ref,
    terms_ref,
):
    shard = where_ref[0]
    column = lax.broadcasted_iota(jnp.int32, (1, TOKENS_HERE), 1)
    no_end = ((shard == 0) & (column < BLOCK)) | ((shard == LAST) & (column >= BLOCK))
    bias = jnp.where(no_end, MASKED, 0.0)
    queries = [query_ref[:, columns_of(i)] for i in range(SOME)]
    grads = [grad_ref[:, columns_of(i)] for i in range(SOME)]
    keys, values = (
        [jnp.concatenate([ends_ref[i, 0, side], ends_ref[i, 1, side]]) for i in range(SOME)]
        for side in range(2)
    )
    score = stacked(lambda i: nt(queries[i], keys[i])) + bias
    old_top = stacked(lambda i: stat_of(stat_ref, i, 0))
    top = jnp.maximum(old_top, jnp.max(score, axis=1, keepdims=True))
    exps = jnp.exp2((score - top) * EXP2_SCALE)
    shrink = jnp.exp2((old_top - top) * EXP2_SCALE)
    total = stacked(lambda i: stat_of(stat_ref, i, 1)) * shrink
    inverse = 1.0 / (total + jnp.sum(exps, axis=1, keepdims=True))
    factor = shrink * inverse
    weight = exps * inverse
    low = weight.astype(BF16)
    wgrad = stacked(lambda i: nt(grads[i], values[i]))
    attended = stacked(lambda i: part_ref[i]) * factor
    attended = attended + stacked(lambda i: nn(low[rows_of(i)], values[i]))
    attended = attended.astype(BF16)
    grad = stacked(lambda i: grads[i].astype(F32))
    row_dot = jnp.sum(grad * attended.astype(F32), axis=1, keepdims=True)
    sgrad = (weight * (wgrad - row_dot) * SCALE).astype(BF16)
    factor_ref[0] = side_by_side(jnp.concatenate([factor, row_dot], axis=1))
    for i in range(SOME):
        at = rows_of(i)
        attended_ref[:, columns_of(i)] = attended[at]
        sgrad_ref[i] = sgrad[at]
        for side, left, right in ((0, sgrad, queries[i]), (1, low, grads[i])):
            terms = tn(left[at], right).astype(BF16)
            terms_ref[i, 0, side] = terms[:BLOCK]
            terms_ref[i, 1, side] = terms[BLOCK:]


def ends(where, query, grad, part, stat, blocks):
    own = (HEADS, TOKENS_HERE, DH)
    pair_spec = pl.BlockSpec((SOME, 2, 2, BLOCK, DH), lambda i, where: (i, 0, 0, 0, 0))
    heads_specs = [head_spec(DH, step_of), stat_spec(step_of)]
    return grid_call(
        ends_kernel,
        "ends",
        4 * 10**8,
        8 * 2**20,
        1,
        [flat_spec(step_of)] * 2 + heads_specs + [pair_spec],
        [flat_spec(step_of)] + heads_specs + [pair_spec],
        [
            struct((TOKENS_HERE, HEADS * DH), BF16),
            struct(own, BF16),
            struct(STATS),
            struct((HEADS, 2, 2, BLOCK, DH), BF16),
        ],
    )(where, query, grad, part, stat, blocks)


def far_terms_kernel(
    pick_ref,
    query_ref,
    grad_ref,
    exp_ref,
    wgrad_ref,
    factor_ref,
    terms_ref,
    prev_terms_ref,
    next_terms_ref,
    made_ref,
    sem,
):
    step = pl.program_id(0)
    no_rows = jnp.zeros((BLOCK, DH), BF16)

    def split(block_rows):
        return jnp.concatenate(
            [
                jnp.concatenate([block_rows[HALVES[0]], no_rows], axis=1),
                jnp.concatenate([no_rows, block_rows[HALVES[1]]], axis=1),
            ]
        )

    for i in range(SOME):
        head = step * SOME + i
        at = columns_of(i)
        weight = exp_ref[i] * stat_of(factor_ref, i, 0)
        low = weight.astype(BF16)
        sgrad = (weight * (wgrad_ref[i] - stat_of(factor_ref, i, 1)) * SCALE).astype(BF16)
        for side, left, right in ((0, sgrad, query_ref[:, at]), (1, low, grad_ref[:, at])):
            parts = tn(left, split(right)).astype(BF16)
            for b, edge_ref in enumerate((prev_terms_ref, next_terms_ref)):
                part = parts[:, columns_of(b)]
                edge_ref[side, :, at] = part[:BLOCK]
                for r in range(3):
                    made_ref[head, b * 3 + r, side] = part[(r + 1) * BLOCK : (r + 2) * BLOCK]
        for b in range(2):
            for r in range(3):
                pltpu.make_async_copy(
                    made_ref.at[head, b * 3 + r],
                    terms_ref.at[owner_of(pick_ref, head, b, r)],
                    sem.at[0],
                ).start()

    @pl.when(step == STEPS - 1)
    def _():
        pltpu.make_async_copy(made_ref, made_ref, sem.at[0]).wait()


def far_terms(picks, query, grad, exps, wgrads, factor):
    edge = struct((2, BLOCK, HEADS * DH), BF16)
    return grid_call(
        far_terms_kernel,
        "far_terms",
        4 * 10**8,
        14 * 2**20,
        1,
        [flat_spec(step_of)] * 2 + [head_spec(2 * DH, step_of)] * 2 + [stat_spec(step_of)],
        [IN_HBM, edge_spec(step_of), edge_spec(step_of)],
        [struct((SHARDS, 2, BLOCK, DH), BF16), edge, edge],
        [pltpu.VMEM((HEADS, 6, 2, BLOCK, DH), BF16), pltpu.SemaphoreType.DMA((1,))],
    )(picks, query, grad, exps, wgrads, factor)


def own_terms_kernel(
    pick_ref,
    query_ref,
    grad_ref,
    key_ref,
    far_ref,
    prev_ref,
    next_ref,
    own_exp_ref,
    far_exp_ref,
    own_wgrad_ref,
    far_wgrad_ref,
    end_sgrad_ref,
    ends_ref,
    factor_ref,
    query_grad_ref,
    own_ref,
    held_ref,
    sem,
):
    step = pl.program_id(0)

    @pl.when(step == 0)
    def _():
        fetch(pick_ref, far_ref, held_ref, sem)

    edges = (prev_ref, next_ref)
    for i in range(SOME):
        head = step * SOME + i
        at = columns_of(i)
        fetched(held_ref, sem, head)
        factor, row_dot = stat_of(factor_ref, i, 0), stat_of(factor_ref, i, 1)
        weight = own_exp_ref[i] * factor
        sgrad = (weight * (own_wgrad_ref[i] - row_dot) * SCALE).astype(BF16)
        far_sgrad = far_exp_ref[i] * factor * (far_wgrad_ref[i] - row_dot) * SCALE
        far_sgrad = far_sgrad.astype(BF16)

        def far_key(b):
            picked = [held_ref[head, b * 3 + r] for r in range(3)]
            return jnp.concatenate([edges[b][0, :, at]] + picked)

        end_key = jnp.concatenate([ends_ref[i, 0, 0], ends_ref[i, 1, 0]])
        query_grad = nn(end_sgrad_ref[i], end_key) + nn(sgrad, key_ref[:, at])
        query_grad = query_grad + both(lambda b: nn(far_sgrad[HALVES[b]], far_key(b)))
        query_grad_ref[:, at] = query_grad.astype(BF16)
        own_ref[0, :, at] = tn(sgrad, query_ref[:, at])
        own_ref[1, :, at] = tn(weight.astype(BF16), grad_ref[:, at])


def own_terms(picks, query, grad, key, far, prev, following, exps, wgrads, end_sgrad, blocks, factor):
    return grid_call(
        own_terms_kernel,
        "own_terms",
        5 * 10**8,
        16 * 2**20,
        1,
        [flat_spec(step_of)] * 3
        + [IN_HBM]
        + [edge_spec(step_of)] * 2
        + [head_spec(w, step_of) for w in (DH, 2 * DH, DH, 2 * DH, DH)]
        + [pl.BlockSpec((SOME, 2, 2, BLOCK, DH), lambda i, picks: (i, 0, 0, 0, 0))]
        + [stat_spec(step_of)],
        [
            flat_spec(step_of),
            pl.BlockSpec((2, TOKENS_HERE, SOME * DH), lambda i, picks: (0, 0, i)),
        ],
        [
            struct((TOKENS_HERE, HEADS * DH), BF16),
            struct((2, TOKENS_HERE, HEADS * DH)),
        ],
        [pltpu.VMEM((HEADS, 6, BLOCK, DH), BF16), pltpu.SemaphoreType.DMA((HEADS,))],
    )(picks, query, grad, key, far, prev, following, *exps, *wgrads, end_sgrad, blocks, factor)


USUAL = 4


def gather_kernel(
    order_ref, begin_ref, terms_ref, own_ref, low_ref, high_ref, key_ref, value_ref
):
    edges = (low_ref, high_ref)

    def one_side(out_ref):
        for block in range(2):
            for head in range(HEADS):
                item = block * HEADS + head
                at = columns_of(head)
                begin, end = begin_ref[item], begin_ref[item + 1]

                def term(place):
                    return terms_ref[order_ref[place], 0].astype(F32)

                total = own_ref[0, HALVES[block], at] + edges[block][0, :, at].astype(F32)
                for i in range(USUAL):
                    found = term(jnp.minimum(begin + i, SHARDS - 1))
                    total = total + jnp.where(begin + i < end, found, 0.0)
                total = lax.fori_loop(
                    jnp.minimum(begin + USUAL, end), end, lambda p, sums: sums + term(p), total
                )
                out_ref[HALVES[block], at] = total.astype(BF16)

    for side, out_ref in enumerate((key_ref, value_ref)):
        pl.when(pl.program_id(0) == side)(lambda out_ref=out_ref: one_side(out_ref))


def gather(order, begins, terms, own, low, high):
    flat = struct((TOKENS_HERE, HEADS * DH), BF16)
    flat_whole = pl.BlockSpec(flat.shape, lambda side, *scalars: (0, 0))

    def side_spec(rows_there):
        return pl.BlockSpec(
            (1, rows_there, HEADS * DH), lambda side, *scalars: (side, 0, 0)
        )

    return pl.pallas_call(
        gather_kernel,
        grid_spec=pltpu.PrefetchScalarGridSpec(
            num_scalar_prefetch=2,
            grid=(2,),
            in_specs=[
                pl.BlockSpec((SHARDS, 1, BLOCK, DH), lambda side, *scalars: (0, side, 0, 0)),
                side_spec(TOKENS_HERE),
                side_spec(BLOCK),
                side_spec(BLOCK),
            ],
            out_specs=[flat_whole, flat_whole],
        ),
        out_shape=[flat, flat],
        compiler_params=params(16 * 2**20),
        cost_estimate=cost(10**6, 9 * 2**20),
        name="gather",
    )(order, begins, terms, own, low, high)


def send(value, route):
    return lax.ppermute(value, "seq", route)


def repeat_kernel(first_ref, last_ref, out_ref):
    for cell in range(HEADS):
        out_ref[cell, 0] = first_ref[0]
        out_ref[cell, 1] = last_ref[0]


def repeat_ends(far):
    def slot_spec(slot):
        return pl.BlockSpec((1, 2, BLOCK, DH), lambda i: (slot, 0, 0, 0))

    out = struct((HEADS, 2, 2, BLOCK, DH), BF16)
    return pl.pallas_call(
        repeat_kernel,
        grid=(1,),
        in_specs=[slot_spec(0), slot_spec(LAST)],
        out_specs=pl.BlockSpec(out.shape, lambda i: (0,) * 5),
        out_shape=out,
        compiler_params=params(),
        cost_estimate=cost(0, 2**20),
        name="repeat_ends",
    )(far, far)


def swap_in_plane(pieces):
    planes = [[cell * NZ + z for cell in range(NX * NY)] for z in range(NZ)]
    return lax.all_to_all(
        pieces, "seq", split_axis=0, concat_axis=0, tiled=True, axis_index_groups=planes
    )


def on_device(queries, key_states, values, out_grad, rand_blocks):
    shard = lax.axis_index("seq")
    where = shard.astype(jnp.int32).reshape(1)
    wanted = rand_blocks // 2 == shard
    item = rand_blocks % 2 * HEADS + lax.broadcasted_iota(jnp.int32, rand_blocks.shape, 1)
    items = jnp.max(jnp.where(wanted, item, -1), axis=(1, 2))
    items = jnp.max(items.reshape(SHARDS, 2), axis=1)
    cell = jnp.arange(SHARDS, dtype=jnp.int32) // NZ
    items = jnp.where(shard == 0, cell, jnp.where(shard == LAST, HEADS + cell, items))
    picks = lax.dynamic_slice_in_dim(rand_blocks, 2 * shard, 2, 0).reshape(2 * PICKS)

    named = jnp.where(items < 0, 2 * HEADS, items)
    place = jnp.arange(SHARDS, dtype=jnp.int32)
    before = (named[None, :] < named[:, None]) | (
        (named[None, :] == named[:, None]) & (place[None, :] < place[:, None])
    )
    rank = jnp.sum(before.astype(jnp.int32), axis=1)
    order = jnp.sum(jnp.where(rank[None, :] == place[:, None], place[None, :], 0), axis=1)
    kinds = jnp.arange(2 * HEADS + 1, dtype=jnp.int32)
    begins = jnp.sum((named[None, :] < kinds[:, None]).astype(jnp.int32), axis=1)

    low = jnp.stack([key_states[:BLOCK], values[:BLOCK]])
    high = jnp.stack([key_states[BLOCK:], values[BLOCK:]])
    up, down = [(i, i + 1) for i in range(LAST)], [(i + 1, i) for i in range(LAST)]
    slots = pack(jnp.maximum(items, 0), key_states, values)
    far = lax.all_to_all(slots, "seq", split_axis=0, concat_axis=0, tiled=True)
    prev, following = send(high, up), send(low, down)
    far, prev, following, picks, where = lax.optimization_barrier(
        (far, prev, following, picks, where)
    )
    blocks = swap_in_plane(repeat_ends(far))
    own_exps, far_exps, own_wgrads, far_wgrads, part, stat = near(
        picks, where, queries, out_grad, key_states, values, far, prev, following
    )
    attended, end_sgrad, factor, end_terms = ends(where, queries, out_grad, part, stat, blocks)
    end_terms = swap_in_plane(end_terms)
    terms, prev_terms, next_terms = far_terms(
        picks, queries, out_grad, far_exps, far_wgrads, factor
    )
    end_pair = jnp.sum(end_terms.astype(F32), axis=0).astype(BF16)
    terms = terms.at[0].set(end_pair[0]).at[LAST].set(end_pair[1])
    back = lax.all_to_all(terms, "seq", split_axis=0, concat_axis=0, tiled=True)
    from_next, from_prev = send(prev_terms, down), send(next_terms, up)
    query_grad, own = own_terms(
        picks, queries, out_grad, key_states, far, prev, following,
        (own_exps, far_exps), (own_wgrads, far_wgrads), end_sgrad, blocks, factor,
    )
    key_grad, value_grad = gather(order, begins, back, own, from_prev, from_next)
    return (attended, query_grad, key_grad, value_grad)


def solution(mesh):
    placed = P("seq", "head")
    return jax.shard_map(
        on_device,
        mesh=mesh,
        in_specs=(placed, placed, placed, placed, P(None, "head", None)),
        out_specs=(placed, placed, placed, placed),
        check_vma=False,
    )
```

```python
import math

import jax
import jax.numpy as jnp
from jax import lax
from jax.experimental import pallas as pl
from jax.experimental.pallas import tpu as pltpu
from jax.sharding import PartitionSpec as P

DH = 128
BLOCK = 64
HEADS = 16
SHARDS = 128
LAST = SHARDS - 1
PICKS = 3 * HEADS
NX, NY, NZ = 4, 4, 8
VMEM_BYTES = 60 * 2**20
MASKED = -1e30
SCALE = 1.0 / math.sqrt(DH)
EXP2_SCALE = SCALE * math.log2(math.e)
BF16 = jnp.bfloat16
F32 = jnp.float32

IN_VMEM = pl.BlockSpec(memory_space=pltpu.VMEM)
IN_SMEM = pl.BlockSpec(memory_space=pltpu.SMEM)
IN_HBM = pl.BlockSpec(memory_space=pltpu.HBM)


def params(vmem_bytes=VMEM_BYTES):
    return pltpu.CompilerParams(vmem_limit_bytes=vmem_bytes)


def cost(flops, moved, exps=0):
    return pl.CostEstimate(flops=flops, bytes_accessed=moved, transcendentals=exps)


def lanes(head):
    return pl.ds(pl.multiple_of(head * DH, DH), DH)


def rows(block):
    return pl.ds(pl.multiple_of(block * BLOCK, BLOCK), BLOCK)


def nt(a, b):
    return lax.dot_general(a, b, (((1,), (1,)), ((), ())), preferred_element_type=F32)


def nn(a, b):
    return lax.dot_general(a, b, (((1,), (0,)), ((), ())), preferred_element_type=F32)


def tn(a, b):
    return lax.dot_general(a, b, (((0,), (0,)), ((), ())), preferred_element_type=F32)


def pack_kernel(item_ref, key_ref, value_ref, slots_ref, sem):
    def moves(slot):
        item = item_ref[slot]
        block, head = item >> 4, item & 15
        return [
            pltpu.make_async_copy(
                ref.at[rows(block), lanes(head)], slots_ref.at[slot, side], sem.at[side]
            )
            for side, ref in enumerate((key_ref, value_ref))
        ]

    def start(slot, carry):
        for move in moves(slot):
            move.start()
        return carry

    lax.fori_loop(0, SHARDS, start, 0, unroll=8)
    for side in range(2):
        whole = slots_ref.at[:, side]
        pltpu.make_async_copy(whole, whole, sem.at[side]).wait()


def pack(items, key_states, values):
    return pl.pallas_call(
        pack_kernel,
        in_specs=[IN_SMEM, IN_VMEM, IN_VMEM],
        out_specs=pl.BlockSpec(memory_space=pl.ANY),
        out_shape=jax.ShapeDtypeStruct((SHARDS, 2, BLOCK, DH), BF16),
        scratch_shapes=[pltpu.SemaphoreType.DMA((2,))],
        compiler_params=params(),
        cost_estimate=cost(0, 6 * 2**20),
        name="pack",
    )(items, key_states, values)


HALVES = (slice(0, BLOCK), slice(BLOCK, 2 * BLOCK))
TOKENS_HERE = 2 * BLOCK
SOME = 4
STEPS = HEADS // SOME


def struct(shape, dtype=F32):
    return jax.ShapeDtypeStruct(shape, dtype)


def flat_spec(where_to):
    return pl.BlockSpec((TOKENS_HERE, SOME * DH), lambda *at: (0, where_to(*at)))


def edge_spec(where_to):
    return pl.BlockSpec((2, BLOCK, SOME * DH), lambda *at: (0, 0, where_to(*at)))


def head_spec(width, where_to):
    return pl.BlockSpec((SOME, TOKENS_HERE, width), lambda *at: (where_to(*at), 0, 0))


def stat_spec(where_to):
    return pl.BlockSpec((1, TOKENS_HERE, 2 * SOME), lambda *at: (where_to(*at), 0, 0))


STATS = (STEPS, TOKENS_HERE, 2 * SOME)


def side_by_side(stat):
    return jnp.concatenate([stat[rows_of(i)] for i in range(SOME)], axis=1)


def stat_of(stat_ref, i, which):
    return stat_ref[0, :, 2 * i + which : 2 * i + which + 1]


def grid_call(kernel, name, flops, moved, prefetch, in_specs, out_specs, out_shape, scratch=()):
    return pl.pallas_call(
        kernel,
        grid_spec=pltpu.PrefetchScalarGridSpec(
            num_scalar_prefetch=prefetch,
            grid=(STEPS,),
            in_specs=in_specs,
            out_specs=out_specs,
            scratch_shapes=scratch,
        ),
        out_shape=out_shape,
        compiler_params=params(),
        cost_estimate=cost(flops, moved, 10**6),
        name=name,
    )


def step_of(i, *scalars):
    return i


def columns_of(i):
    return slice(i * DH, (i + 1) * DH)


def both(of):
    return jnp.concatenate([of(0), of(1)])


def stacked(of):
    return jnp.concatenate([of(i) for i in range(SOME)])


def rows_of(i):
    return slice(i * TOKENS_HERE, (i + 1) * TOKENS_HERE)


def half_rows(i, b):
    return slice((2 * i + b) * BLOCK, (2 * i + b + 1) * BLOCK)


def owner_of(pick_ref, head, b, r):
    return pick_ref[b * PICKS + head * 3 + r] >> 1


def fetch(pick_ref, far_ref, held_ref, sem):
    def one(head, carry):
        for b in range(2):
            for r in range(3):
                source = far_ref.at[owner_of(pick_ref, head, b, r)]
                if len(held_ref.shape) == 4:
                    source = source.at[0]
                target = held_ref.at[head, b * 3 + r]
                pltpu.make_async_copy(source, target, sem.at[head]).start()
        return carry

    lax.fori_loop(0, HEADS, one, 0, unroll=4)


def fetched(held_ref, sem, head):
    pltpu.make_async_copy(held_ref.at[head], held_ref.at[head], sem.at[head]).wait()


def near_kernel(
    pick_ref,
    where_ref,
    query_ref,
    grad_ref,
    key_ref,
    value_ref,
    far_ref,
    prev_ref,
    next_ref,
    own_exp_ref,
    far_exp_ref,
    own_wgrad_ref,
    far_wgrad_ref,
    part_ref,
    stat_ref,
    held_ref,
    sem,
):
    step = pl.program_id(0)

    @pl.when(step == 0)
    def _():
        fetch(pick_ref, far_ref, held_ref, sem)

    shard = where_ref[0]
    column = lax.broadcasted_iota(jnp.int32, (1, 4 * BLOCK), 1)
    bias = [
        jnp.where((shard == end) & (column < BLOCK), MASKED, 0.0) for end in (0, LAST)
    ]
    edges = (prev_ref, next_ref)
    heads = [step * SOME + i for i in range(SOME)]
    queries = [query_ref[:, columns_of(i)] for i in range(SOME)]
    grads = [grad_ref[:, columns_of(i)] for i in range(SOME)]
    for head in heads:
        fetched(held_ref, sem, head)

    def picked(i, b, side):
        edge = edges[b][side, :, columns_of(i)]
        return jnp.concatenate([edge] + [held_ref[heads[i], b * 3 + r, side] for r in range(3)])

    keys, values = (
        [[picked(i, b, side) for b in range(2)] for i in range(SOME)] for side in range(2)
    )
    own_score = stacked(lambda i: nt(queries[i], key_ref[:, columns_of(i)]))
    far_score = stacked(lambda i: both(lambda b: nt(queries[i][HALVES[b]], keys[i][b]) + bias[b]))
    top = jnp.maximum(
        jnp.maximum(own_score, far_score[:, :TOKENS_HERE]), far_score[:, TOKENS_HERE:]
    )
    top = jnp.max(top, axis=1, keepdims=True)
    own_exp = jnp.exp2((own_score - top) * EXP2_SCALE)
    far_exp = jnp.exp2((far_score - top) * EXP2_SCALE)
    total = own_exp + far_exp[:, :TOKENS_HERE] + far_exp[:, TOKENS_HERE:]
    stat = jnp.concatenate([top, jnp.sum(total, axis=1, keepdims=True)], axis=1)
    stat_ref[0] = side_by_side(stat)
    own_low, far_low = own_exp.astype(BF16), far_exp.astype(BF16)
    for i in range(SOME):
        at = rows_of(i)
        own_exp_ref[i], far_exp_ref[i] = own_exp[at], far_exp[at]
        own_wgrad_ref[i] = nt(grads[i], value_ref[:, columns_of(i)])
        far_part = both(lambda b: nn(far_low[half_rows(i, b)], values[i][b]))
        part_ref[i] = nn(own_low[at], value_ref[:, columns_of(i)]) + far_part
        for b in range(2):
            far_wgrad_ref[i, HALVES[b]] = nt(grads[i][HALVES[b]], values[i][b])


def near(picks, where, query, grad, key, value, far, prev, following):
    own, wide = (HEADS, TOKENS_HERE, TOKENS_HERE), (HEADS, TOKENS_HERE, 4 * BLOCK)
    return grid_call(
        near_kernel,
        "near",
        6 * 10**8,
        16 * 2**20,
        2,
        [flat_spec(step_of)] * 4 + [IN_HBM] + [edge_spec(step_of)] * 2,
        [head_spec(w, step_of) for w in (DH, 2 * DH, DH, 2 * DH, DH)] + [stat_spec(step_of)],
        [struct(own), struct(wide), struct(own), struct(wide), struct(own), struct(STATS)],
        [pltpu.VMEM((HEADS, 6, 2, BLOCK, DH), BF16), pltpu.SemaphoreType.DMA((HEADS,))],
    )(picks, where, query, grad, key, value, far, prev, following)


def ends_kernel(
    where_ref,
    query_ref,
    grad_ref,
    part_ref,
    stat_ref,
    ends_ref,
    attended_ref,
    sgrad_ref,
    factor_ref,
    terms_ref,
):
    shard = where_ref[0]
    column = lax.broadcasted_iota(jnp.int32, (1, TOKENS_HERE), 1)
    no_end = ((shard == 0) & (column < BLOCK)) | ((shard == LAST) & (column >= BLOCK))
    bias = jnp.where(no_end, MASKED, 0.0)
    queries = [query_ref[:, columns_of(i)] for i in range(SOME)]
    grads = [grad_ref[:, columns_of(i)] for i in range(SOME)]
    keys, values = (
        [jnp.concatenate([ends_ref[i, 0, side], ends_ref[i, 1, side]]) for i in range(SOME)]
        for side in range(2)
    )
    score = stacked(lambda i: nt(queries[i], keys[i])) + bias
    old_top = stacked(lambda i: stat_of(stat_ref, i, 0))
    top = jnp.maximum(old_top, jnp.max(score, axis=1, keepdims=True))
    exps = jnp.exp2((score - top) * EXP2_SCALE)
    shrink = jnp.exp2((old_top - top) * EXP2_SCALE)
    total = stacked(lambda i: stat_of(stat_ref, i, 1)) * shrink
    inverse = 1.0 / (total + jnp.sum(exps, axis=1, keepdims=True))
    factor = shrink * inverse
    weight = exps * inverse
    low = weight.astype(BF16)
    wgrad = stacked(lambda i: nt(grads[i], values[i]))
    attended = stacked(lambda i: part_ref[i]) * factor
    attended = attended + stacked(lambda i: nn(low[rows_of(i)], values[i]))
    attended = attended.astype(BF16)
    grad = stacked(lambda i: grads[i].astype(F32))
    row_dot = jnp.sum(grad * attended.astype(F32), axis=1, keepdims=True)
    sgrad = (weight * (wgrad - row_dot) * SCALE).astype(BF16)
    factor_ref[0] = side_by_side(jnp.concatenate([factor, row_dot], axis=1))
    for i in range(SOME):
        at = rows_of(i)
        attended_ref[:, columns_of(i)] = attended[at]
        sgrad_ref[i] = sgrad[at]
        for side, left, right in ((0, sgrad, queries[i]), (1, low, grads[i])):
            terms = tn(left[at], right).astype(BF16)
            terms_ref[i, 0, side] = terms[:BLOCK]
            terms_ref[i, 1, side] = terms[BLOCK:]


def ends(where, query, grad, part, stat, blocks):
    own = (HEADS, TOKENS_HERE, DH)
    pair_spec = pl.BlockSpec((SOME, 2, 2, BLOCK, DH), lambda i, where: (i, 0, 0, 0, 0))
    heads_specs = [head_spec(DH, step_of), stat_spec(step_of)]
    return grid_call(
        ends_kernel,
        "ends",
        4 * 10**8,
        8 * 2**20,
        1,
        [flat_spec(step_of)] * 2 + heads_specs + [pair_spec],
        [flat_spec(step_of)] + heads_specs + [pair_spec],
        [
            struct((TOKENS_HERE, HEADS * DH), BF16),
            struct(own, BF16),
            struct(STATS),
            struct((HEADS, 2, 2, BLOCK, DH), BF16),
        ],
    )(where, query, grad, part, stat, blocks)


def far_terms_kernel(
    pick_ref,
    query_ref,
    grad_ref,
    exp_ref,
    wgrad_ref,
    factor_ref,
    terms_ref,
    prev_terms_ref,
    next_terms_ref,
    made_ref,
    sem,
):
    step = pl.program_id(0)
    no_rows = jnp.zeros((BLOCK, DH), BF16)

    def split(block_rows):
        return jnp.concatenate(
            [
                jnp.concatenate([block_rows[HALVES[0]], no_rows], axis=1),
                jnp.concatenate([no_rows, block_rows[HALVES[1]]], axis=1),
            ]
        )

    for i in range(SOME):
        head = step * SOME + i
        at = columns_of(i)
        weight = exp_ref[i] * stat_of(factor_ref, i, 0)
        low = weight.astype(BF16)
        sgrad = (weight * (wgrad_ref[i] - stat_of(factor_ref, i, 1)) * SCALE).astype(BF16)
        for side, left, right in ((0, sgrad, query_ref[:, at]), (1, low, grad_ref[:, at])):
            parts = tn(left, split(right)).astype(BF16)
            for b, edge_ref in enumerate((prev_terms_ref, next_terms_ref)):
                part = parts[:, columns_of(b)]
                edge_ref[side, :, at] = part[:BLOCK]
                for r in range(3):
                    made_ref[head, b * 3 + r, side] = part[(r + 1) * BLOCK : (r + 2) * BLOCK]
        for b in range(2):
            for r in range(3):
                pltpu.make_async_copy(
                    made_ref.at[head, b * 3 + r],
                    terms_ref.at[owner_of(pick_ref, head, b, r)],
                    sem.at[0],
                ).start()

    @pl.when(step == STEPS - 1)
    def _():
        pltpu.make_async_copy(made_ref, made_ref, sem.at[0]).wait()


def far_terms(picks, query, grad, exps, wgrads, factor):
    edge = struct((2, BLOCK, HEADS * DH), BF16)
    return grid_call(
        far_terms_kernel,
        "far_terms",
        4 * 10**8,
        14 * 2**20,
        1,
        [flat_spec(step_of)] * 2 + [head_spec(2 * DH, step_of)] * 2 + [stat_spec(step_of)],
        [IN_HBM, edge_spec(step_of), edge_spec(step_of)],
        [struct((SHARDS, 2, BLOCK, DH), BF16), edge, edge],
        [pltpu.VMEM((HEADS, 6, 2, BLOCK, DH), BF16), pltpu.SemaphoreType.DMA((1,))],
    )(picks, query, grad, exps, wgrads, factor)


def own_terms_kernel(
    pick_ref,
    query_ref,
    grad_ref,
    key_ref,
    far_ref,
    prev_ref,
    next_ref,
    own_exp_ref,
    far_exp_ref,
    own_wgrad_ref,
    far_wgrad_ref,
    end_sgrad_ref,
    ends_ref,
    factor_ref,
    query_grad_ref,
    own_ref,
    held_ref,
    sem,
):
    step = pl.program_id(0)

    @pl.when(step == 0)
    def _():
        fetch(pick_ref, far_ref, held_ref, sem)

    edges = (prev_ref, next_ref)
    for i in range(SOME):
        head = step * SOME + i
        at = columns_of(i)
        fetched(held_ref, sem, head)
        factor, row_dot = stat_of(factor_ref, i, 0), stat_of(factor_ref, i, 1)
        weight = own_exp_ref[i] * factor
        sgrad = (weight * (own_wgrad_ref[i] - row_dot) * SCALE).astype(BF16)
        far_sgrad = far_exp_ref[i] * factor * (far_wgrad_ref[i] - row_dot) * SCALE
        far_sgrad = far_sgrad.astype(BF16)

        def far_key(b):
            picked = [held_ref[head, b * 3 + r] for r in range(3)]
            return jnp.concatenate([edges[b][0, :, at]] + picked)

        end_key = jnp.concatenate([ends_ref[i, 0, 0], ends_ref[i, 1, 0]])
        query_grad = nn(end_sgrad_ref[i], end_key) + nn(sgrad, key_ref[:, at])
        query_grad = query_grad + both(lambda b: nn(far_sgrad[HALVES[b]], far_key(b)))
        query_grad_ref[:, at] = query_grad.astype(BF16)
        own_ref[0, :, at] = tn(sgrad, query_ref[:, at])
        own_ref[1, :, at] = tn(weight.astype(BF16), grad_ref[:, at])


def own_terms(picks, query, grad, key, far, prev, following, exps, wgrads, end_sgrad, blocks, factor):
    return grid_call(
        own_terms_kernel,
        "own_terms",
        5 * 10**8,
        16 * 2**20,
        1,
        [flat_spec(step_of)] * 3
        + [IN_HBM]
        + [edge_spec(step_of)] * 2
        + [head_spec(w, step_of) for w in (DH, 2 * DH, DH, 2 * DH, DH)]
        + [pl.BlockSpec((SOME, 2, 2, BLOCK, DH), lambda i, picks: (i, 0, 0, 0, 0))]
        + [stat_spec(step_of)],
        [
            flat_spec(step_of),
            pl.BlockSpec((2, TOKENS_HERE, SOME * DH), lambda i, picks: (0, 0, i)),
        ],
        [
            struct((TOKENS_HERE, HEADS * DH), BF16),
            struct((2, TOKENS_HERE, HEADS * DH)),
        ],
        [pltpu.VMEM((HEADS, 6, BLOCK, DH), BF16), pltpu.SemaphoreType.DMA((HEADS,))],
    )(picks, query, grad, key, far, prev, following, *exps, *wgrads, end_sgrad, blocks, factor)


USUAL = 4


def gather_kernel(
    order_ref, begin_ref, terms_ref, own_ref, low_ref, high_ref, key_ref, value_ref, total_ref
):
    edges = (low_ref, high_ref)
    places = [(block, head) for block in range(2) for head in range(HEADS)]

    def term(place):
        return terms_ref[order_ref[place], 0].astype(F32)

    def one_side(out_ref):
        for item, (block, head) in enumerate(places):
            at = columns_of(head)
            begin, end = begin_ref[item], begin_ref[item + 1]
            total = own_ref[0, HALVES[block], at] + edges[block][0, :, at].astype(F32)
            for i in range(USUAL):
                found = term(jnp.minimum(begin + i, SHARDS - 1))
                total = total + jnp.where(begin + i < end, found, 0.0)
            total_ref[item] = total

        def more(item, carry):
            def add(place, carry):
                total_ref[item] += term(place)
                return carry

            return lax.fori_loop(begin_ref[item] + USUAL, begin_ref[item + 1], add, carry)

        lax.fori_loop(0, 2 * HEADS, more, 0)
        for item, (block, head) in enumerate(places):
            out_ref[HALVES[block], columns_of(head)] = total_ref[item].astype(BF16)

    for side, out_ref in enumerate((key_ref, value_ref)):
        pl.when(pl.program_id(0) == side)(lambda out_ref=out_ref: one_side(out_ref))


def gather(order, begins, terms, own, low, high):
    flat = struct((TOKENS_HERE, HEADS * DH), BF16)
    flat_whole = pl.BlockSpec(flat.shape, lambda side, *scalars: (0, 0))

    def side_spec(rows_there):
        return pl.BlockSpec(
            (1, rows_there, HEADS * DH), lambda side, *scalars: (side, 0, 0)
        )

    return pl.pallas_call(
        gather_kernel,
        grid_spec=pltpu.PrefetchScalarGridSpec(
            num_scalar_prefetch=2,
            grid=(2,),
            in_specs=[
                pl.BlockSpec((SHARDS, 1, BLOCK, DH), lambda side, *scalars: (0, side, 0, 0)),
                side_spec(TOKENS_HERE),
                side_spec(BLOCK),
                side_spec(BLOCK),
            ],
            out_specs=[flat_whole, flat_whole],
            scratch_shapes=[pltpu.VMEM((2 * HEADS, BLOCK, DH), F32)],
        ),
        out_shape=[flat, flat],
        compiler_params=params(16 * 2**20),
        cost_estimate=cost(10**6, 9 * 2**20),
        name="gather",
    )(order, begins, terms, own, low, high)


def send(value, route):
    return lax.ppermute(value, "seq", route)


def repeat_kernel(first_ref, last_ref, out_ref):
    for cell in range(HEADS):
        out_ref[cell, 0] = first_ref[0]
        out_ref[cell, 1] = last_ref[0]


def repeat_ends(far):
    def slot_spec(slot):
        return pl.BlockSpec((1, 2, BLOCK, DH), lambda i: (slot, 0, 0, 0))

    out = struct((HEADS, 2, 2, BLOCK, DH), BF16)
    return pl.pallas_call(
        repeat_kernel,
        grid=(1,),
        in_specs=[slot_spec(0), slot_spec(LAST)],
        out_specs=pl.BlockSpec(out.shape, lambda i: (0,) * 5),
        out_shape=out,
        compiler_params=params(),
        cost_estimate=cost(0, 2**20),
        name="repeat_ends",
    )(far, far)


def swap_in_plane(pieces):
    planes = [[cell * NZ + z for cell in range(NX * NY)] for z in range(NZ)]
    return lax.all_to_all(
        pieces, "seq", split_axis=0, concat_axis=0, tiled=True, axis_index_groups=planes
    )


def on_device(queries, key_states, values, out_grad, rand_blocks):
    shard = lax.axis_index("seq")
    where = shard.astype(jnp.int32).reshape(1)
    wanted = rand_blocks // 2 == shard
    item = rand_blocks % 2 * HEADS + lax.broadcasted_iota(jnp.int32, rand_blocks.shape, 1)
    items = jnp.max(jnp.where(wanted, item, -1), axis=(1, 2))
    items = jnp.max(items.reshape(SHARDS, 2), axis=1)
    cell = jnp.arange(SHARDS, dtype=jnp.int32) // NZ
    items = jnp.where(shard == 0, cell, jnp.where(shard == LAST, HEADS + cell, items))
    picks = lax.dynamic_slice_in_dim(rand_blocks, 2 * shard, 2, 0).reshape(2 * PICKS)

    named = jnp.where(items < 0, 2 * HEADS, items)
    place = jnp.arange(SHARDS, dtype=jnp.int32)
    before = (named[None, :] < named[:, None]) | (
        (named[None, :] == named[:, None]) & (place[None, :] < place[:, None])
    )
    rank = jnp.sum(before.astype(jnp.int32), axis=1)
    order = jnp.sum(jnp.where(rank[None, :] == place[:, None], place[None, :], 0), axis=1)
    kinds = jnp.arange(2 * HEADS + 1, dtype=jnp.int32)
    begins = jnp.sum((named[None, :] < kinds[:, None]).astype(jnp.int32), axis=1)

    low = jnp.stack([key_states[:BLOCK], values[:BLOCK]])
    high = jnp.stack([key_states[BLOCK:], values[BLOCK:]])
    up, down = [(i, i + 1) for i in range(LAST)], [(i + 1, i) for i in range(LAST)]
    slots = pack(jnp.maximum(items, 0), key_states, values)
    far = lax.all_to_all(slots, "seq", split_axis=0, concat_axis=0, tiled=True)
    prev, following = send(high, up), send(low, down)
    far, prev, following, picks, where = lax.optimization_barrier(
        (far, prev, following, picks, where)
    )
    blocks = swap_in_plane(repeat_ends(far))
    own_exps, far_exps, own_wgrads, far_wgrads, part, stat = near(
        picks, where, queries, out_grad, key_states, values, far, prev, following
    )
    attended, end_sgrad, factor, end_terms = ends(where, queries, out_grad, part, stat, blocks)
    end_terms = swap_in_plane(end_terms)
    terms, prev_terms, next_terms = far_terms(
        picks, queries, out_grad, far_exps, far_wgrads, factor
    )
    end_pair = jnp.sum(end_terms.astype(F32), axis=0).astype(BF16)
    terms = terms.at[0].set(end_pair[0]).at[LAST].set(end_pair[1])
    back = lax.all_to_all(terms, "seq", split_axis=0, concat_axis=0, tiled=True)
    from_next, from_prev = send(prev_terms, down), send(next_terms, up)
    query_grad, own = own_terms(
        picks, queries, out_grad, key_states, far, prev, following,
        (own_exps, far_exps), (own_wgrads, far_wgrads), end_sgrad, blocks, factor,
    )
    key_grad, value_grad = gather(order, begins, back, own, from_prev, from_next)
    return (attended, query_grad, key_grad, value_grad)


def solution(mesh):
    placed = P("seq", "head")
    return jax.shard_map(
        on_device,
        mesh=mesh,
        in_specs=(placed, placed, placed, placed, P(None, "head", None)),
        out_specs=(placed, placed, placed, placed),
        check_vma=False,
    )
```
